256 devices in a mesh: tst: 64 (over y, z, core), req: 4 (over x).
Axes of the slice: x: 4, y: 4, z: 8, core: 2. Of those that a mesh axis runs over, the one named last changes fastest.
Arguments:
- coverage_tiles: bfloat16 [32768, 128, 128], P(('tst', 'req')), may hold values from 0 to 0.0006904602
- tile_rows: int32 [32768], P(('tst', 'req')), may hold values from 0 to 127
- tile_cols: int32 [32768], P(('tst', 'req')), may hold values from 0 to 63
- tile_counts: int32 [256], P(('tst', 'req')), may hold values from 32 to 128, as said below
- test_costs: float32 [524288], P('tst'), may hold values from 0.05 to 1.5, as said below
- runtimes: float32 [524288], P('tst'), may hold values from 0.05 to 4.5, as said below
- time_limit: float32 [1], replicated, may hold values from 0 to 0.2
- demand: float32 [65536], P('req'), may hold values from 0.1 to 0.6
- primal_start: float32 [524288], P('tst'), may hold values from 0 to 1
- dual_start: float32 [65536], P('req'), may hold values from 0 to 0.5
- limit_dual_start: float32 [1], replicated, may hold values from 0.5 to 1.5
- restarts: int32 [3], replicated, may hold values from 0 to 1
Outputs:
- primal_out: float32 [524288], P('tst')
- dual_out: float32 [65536], P('req')
- limit_dual: float32 [1], replicated
- move_norms: float32 [3, 2], replicated
The draws below stay inside these ranges and needn't reach their ends.
Inputs may be any that keep to these rules, and one draw needn't show every extreme that they name: `tile_counts`: live slots of a device; some device has all 128 live in every draw. `test_costs`: positive costs. `runtimes`: positive running times.
All inputs are finite; a program needn't handle non-finite values.
Results may differ from the reference program's by a relative error of at most 0.0003.
Values may be sent and summed in bfloat16 or wider, within the bound.
No kernel may reach another device: no remote copies, remote signals or barrier semaphores. Data moves between devices by JAX's collectives and lax.ppermute only.
A program may use at most 64 MiB of HBM per device.

```python
import jax
import jax.numpy as jnp
from jax import lax

CB = 64
RB = 128
K_CAP = 128
ITERS = 3
TESTS = 524288
REQS = 65536
TILES = 32768
N_TST = 64
N_REQ = 4


def draw_tile_counts(key, part):
    key = jax.random.fold_in(key, 5)
    first_key, second_key = jax.random.split(key)
    device_count = N_TST * N_REQ
    lowest = max(1, K_CAP // 4)
    counts_drawn = jax.random.randint(first_key, (device_count,), lowest, K_CAP + 1)
    full_device = jax.random.randint(second_key, (), 0, device_count)
    device_ids = jnp.arange(device_count, dtype=jnp.int32)
    return jnp.where(device_ids == full_device, K_CAP, counts_drawn).astype(jnp.int32)


def draw_test_costs(key, part):
    key = jax.random.fold_in(key, 11)
    position = jnp.arange(TESTS, dtype=jnp.float32) / TESTS
    rising = jnp.exp(jnp.log(3.0) * position)
    base_cost = jnp.exp(jax.random.uniform(key, (TESTS,), jnp.float32, jnp.log(0.05), jnp.log(0.5)))
    return (base_cost * rising).astype(jnp.float32)


def draw_runtimes(key, part):
    key = jax.random.fold_in(key, 17)
    position = jnp.arange(TESTS, dtype=jnp.float32) / TESTS
    rising = jnp.exp(jnp.log(3.0) * position)
    base_time = jnp.exp(jax.random.uniform(key, (TESTS,), jnp.float32, jnp.log(0.05), jnp.log(0.5)))
    return (base_time * rising).astype(jnp.float32)


def touch_ends(drawn, rng, smallest, largest):
    shape = drawn.shape
    spot = [jax.random.randint(jax.random.fold_in(rng, axis), (), 0, shape[axis]) for axis in range(len(shape))]
    drawn = drawn.at[tuple(spot)].set(smallest)
    longest = shape.index(max(shape))
    spot[longest] = (spot[longest] + 1) % shape[longest]
    return drawn.at[tuple(spot)].set(largest)


def block_scale(own_key, extent, shards, low, high):
    def one(axis_at, blocks):
        heights = jax.random.uniform(jax.random.fold_in(jax.random.fold_in(own_key, 6), axis_at), (blocks,), jnp.float32, low / len(shards), high / len(shards))
        return jnp.repeat(jnp.exp(heights), extent[axis_at] // blocks).reshape((-1,) + (1,) * (len(extent) - axis_at - 1))

    level = one(*shards[0])
    for cut in shards[1:]:
        level = level * one(*cut)
    return level


def setup_inputs(seed: int = 0) -> dict:
    seeds = jax.random.split(jax.random.key(seed), 13)
    return {
        "coverage_tiles": jnp.clip(0.0006904602 * jax.random.uniform(seeds[0], (TILES, 128, 128), jnp.float32) ** block_scale(seeds[0], (TILES, 128, 128), ((0, 256),), -0.2, 0.2), 0.0, 0.0006904602).astype(jnp.bfloat16),
        "tile_rows": touch_ends(jax.random.randint(seeds[1], (TILES,), 0, RB), jax.random.fold_in(seeds[1], 1), 0, RB - 1).astype(jnp.int32),
        "tile_cols": touch_ends(jax.random.randint(seeds[2], (TILES,), 0, CB), jax.random.fold_in(seeds[2], 1), 0, CB - 1).astype(jnp.int32),
        "tile_counts": draw_tile_counts(jax.random.fold_in(seeds[12], 71), 0),
        "test_costs": draw_test_costs(jax.random.fold_in(seeds[12], 71), 0),
        "runtimes": draw_runtimes(jax.random.fold_in(seeds[12], 71), 0),
        "time_limit": jnp.clip(jax.random.uniform(seeds[6], (1,), jnp.float32, 0.0, 0.2), 0.0, 0.2),
        "demand": jnp.clip(0.1 + 0.5 * jax.random.uniform(seeds[7], (REQS,), jnp.float32) ** block_scale(seeds[7], (REQS,), ((0, 4),), -0.2, 0.2), 0.1, 0.6),
        "primal_start": jnp.clip(1.0 * jax.random.uniform(seeds[8], (TESTS,), jnp.float32) ** block_scale(seeds[8], (TESTS,), ((0, 64),), -0.2, 0.2), 0.0, 1.0),
        "dual_start": jnp.clip(0.5 * jax.random.uniform(seeds[9], (REQS,), jnp.float32) ** block_scale(seeds[9], (REQS,), ((0, 4),), -0.2, 0.2), 0.0, 0.5),
        "limit_dual_start": jnp.clip(jax.random.uniform(seeds[10], (1,), jnp.float32, 0.5, 1.5), 0.5, 1.5),
        "restarts": jax.random.randint(seeds[11], (ITERS,), 0, 2).astype(jnp.int32),
    }


step_primal = 0.6
step_dual = 0.6


def tile_setup(coverage_tiles, tile_rows, tile_cols):
    device_count = N_TST * N_REQ
    tiles_dev = coverage_tiles.reshape(device_count, K_CAP, 128, 128)
    rows_dev = tile_rows.reshape(device_count, K_CAP)
    cols_dev = tile_cols.reshape(device_count, K_CAP)
    return tiles_dev, rows_dev, cols_dev


def transpose_apply(dual_half, tiles_dev, rows_dev, cols_dev, tile_counts):
    dual_blocks = dual_half.reshape(N_REQ, RB, 128)
    slot_ids = jnp.arange(K_CAP, dtype=jnp.int32)
    device_ids = jnp.arange(N_TST * N_REQ, dtype=jnp.int32)

    def visit(running, record):
        tile_block, row_ids, col_ids, live_count, device_index = record
        test_part = (device_index // N_REQ).astype(jnp.int32)
        req_part = (device_index % N_REQ).astype(jnp.int32)
        own_part = lax.dynamic_index_in_dim(dual_blocks, req_part, 0, keepdims=False)
        picked = jnp.take(own_part, row_ids, axis=0).astype(jnp.float32)
        contrib = jnp.einsum('kij,ki->kj', tile_block.astype(jnp.float32), picked, precision=lax.Precision.HIGHEST)
        contrib = contrib * (slot_ids < live_count).astype(jnp.float32)[:, None]
        local_sum = jax.ops.segment_sum(contrib, col_ids, num_segments=CB)
        current = lax.dynamic_index_in_dim(running, test_part, 0, keepdims=False)
        running = lax.dynamic_update_index_in_dim(running, current + local_sum, test_part, 0)
        return running, None

    zeros_init = jnp.zeros((N_TST, CB, 128), jnp.float32)
    running, _ = lax.scan(visit, zeros_init, (tiles_dev, rows_dev, cols_dev, tile_counts, device_ids))
    return running.reshape(-1)


def forward_apply(extrap, tiles_dev, rows_dev, cols_dev, tile_counts):
    test_blocks = extrap.reshape(N_TST, CB, 128)
    slot_ids = jnp.arange(K_CAP, dtype=jnp.int32)
    device_ids = jnp.arange(N_TST * N_REQ, dtype=jnp.int32)

    def visit(running, record):
        tile_block, row_ids, col_ids, live_count, device_index = record
        test_part = (device_index // N_REQ).astype(jnp.int32)
        req_part = (device_index % N_REQ).astype(jnp.int32)
        own_part = lax.dynamic_index_in_dim(test_blocks, test_part, 0, keepdims=False)
        picked = jnp.take(own_part, col_ids, axis=0).astype(jnp.float32)
        contrib = jnp.einsum('kij,kj->ki', tile_block.astype(jnp.float32), picked, precision=lax.Precision.HIGHEST)
        contrib = contrib * (slot_ids < live_count).astype(jnp.float32)[:, None]
        local_sum = jax.ops.segment_sum(contrib, row_ids, num_segments=RB)
        current = lax.dynamic_index_in_dim(running, req_part, 0, keepdims=False)
        running = lax.dynamic_update_index_in_dim(running, current + local_sum, req_part, 0)
        return running, None

    zeros_init = jnp.zeros((N_REQ, RB, 128), jnp.float32)
    running, _ = lax.scan(visit, zeros_init, (tiles_dev, rows_dev, cols_dev, tile_counts, device_ids))
    return running.reshape(-1)


def reference(coverage_tiles, tile_rows, tile_cols, tile_counts, test_costs, runtimes, time_limit, demand, primal_start, dual_start, limit_dual_start, restarts):
    tiles_dev, rows_dev, cols_dev = tile_setup(coverage_tiles, tile_rows, tile_cols)
    inverse_tests = 1.0 / TESTS
    primal = primal_start
    dual_now = dual_start
    bdual = limit_dual_start
    sum_primal = jnp.zeros_like(primal)
    sum_dual = jnp.zeros_like(dual_now)
    sum_bdual = jnp.zeros_like(bdual)
    seen = jnp.zeros((), jnp.float32)
    norms_list = []
    for iteration in range(ITERS):
        dual_half = dual_now.astype(jnp.bfloat16)
        pull = transpose_apply(dual_half, tiles_dev, rows_dev, cols_dev, tile_counts)
        primal_new = jnp.clip(primal - step_primal * (test_costs - pull + bdual * runtimes), 0.0, 1.0)
        extrap = (2.0 * primal_new - primal).astype(jnp.bfloat16)
        row_load = forward_apply(extrap, tiles_dev, rows_dev, cols_dev, tile_counts)
        spent_use = jnp.sum(runtimes * extrap.astype(jnp.float32)) * inverse_tests
        dual_new = jnp.maximum(dual_now + step_dual * (demand - row_load), 0.0)
        bdual_new = jnp.maximum(bdual + step_dual * (spent_use - time_limit), 0.0)
        move_primal = jnp.sum((primal_new - primal) ** 2)
        move_dual = jnp.sum((dual_new - dual_now) ** 2) + jnp.sum((bdual_new - bdual) ** 2)
        norms_list.append(jnp.stack([move_primal, move_dual]))
        sum_primal = sum_primal + primal_new
        sum_dual = sum_dual + dual_new
        sum_bdual = sum_bdual + bdual_new
        seen = seen + 1.0
        restart_now = restarts[iteration] == 1
        primal = jnp.where(restart_now, sum_primal / seen, primal_new)
        dual_now = jnp.where(restart_now, sum_dual / seen, dual_new)
        bdual = jnp.where(restart_now, sum_bdual / seen, bdual_new)
        sum_primal = jnp.where(restart_now, 0.0, sum_primal)
        sum_dual = jnp.where(restart_now, 0.0, sum_dual)
        sum_bdual = jnp.where(restart_now, 0.0, sum_bdual)
        seen = jnp.where(restart_now, 0.0, seen)
    return primal, dual_now, bdual, jnp.stack(norms_list)
```

```python
import functools

import jax
import jax.numpy as jnp
from jax import lax
from jax.experimental import pallas as pl
from jax.experimental.pallas import tpu as pltpu
from jax.sharding import PartitionSpec as P

ITERS = 3
LANES = 128
STAT_ROWS = 8
GROUP = 8

step_primal = 0.6
step_dual = 0.6

VMEM = pl.BlockSpec(memory_space=pltpu.VMEM)
SMEM = pl.BlockSpec(memory_space=pltpu.SMEM)
F32 = jnp.float32


def struct(*shape):
    return jax.ShapeDtypeStruct(shape, F32)


def sum_four(parts, rows):
    a, b, c, d = [part[rows, :] for part in parts]
    return (a + b) + (c + d)


def slot_count(restarts, iteration):
    seen = jnp.float32(1.0)
    for earlier in range(iteration):
        seen = jnp.where(restarts[earlier] == 1, 1.0, seen + 1.0)
    return seen


def pull_tiles(picked_rows, tiles, rows, cols, live, test_blocks):
    slots = tiles.shape[0]
    block_ids = lax.broadcasted_iota(jnp.int32, (test_blocks, LANES), 0)

    def step(group, acc):
        parts = []
        for offset in range(GROUP):
            k = group * GROUP + offset
            target = jnp.where(k < live, cols[k], -1)
            row = picked_rows[pl.ds(rows[k], 1), :]
            parts.append(jnp.where(block_ids == target, row, 0.0).astype(jnp.bfloat16))
        lhs = jnp.concatenate(parts, axis=1)
        rhs = tiles[pl.ds(group * GROUP, GROUP)].reshape(GROUP * LANES, LANES)
        return acc + jnp.dot(lhs, rhs, preferred_element_type=F32)

    return lax.fori_loop(0, slots // GROUP, step, jnp.zeros((test_blocks, LANES), F32))


def load_tiles(picked_rows, tiles, rows, cols, live, req_blocks):
    slots = tiles.shape[0]
    block_ids = lax.broadcasted_iota(jnp.int32, (req_blocks, LANES), 0)

    def step(group, acc):
        left, right = [], []
        for offset in range(GROUP):
            k = group * GROUP + offset
            target = jnp.where(k < live, rows[k], -1)
            row = picked_rows[pl.ds(cols[k], 1), :]
            left.append(jnp.where(block_ids == target, row, 0.0).astype(jnp.bfloat16))
            right.append(tiles[k])
        return acc + lax.dot_general(
            jnp.concatenate(left, axis=1),
            jnp.concatenate(right, axis=1),
            (((1,), (1,)), ((), ())),
            preferred_element_type=F32,
        )

    return lax.fori_loop(0, slots // GROUP, step, jnp.zeros((req_blocks, LANES), F32))


def first_pull_kernel(rows, cols, live, dual, tiles, pull_out, picked):
    picked[...] = dual[...].astype(jnp.bfloat16).astype(F32)
    test_blocks = pull_out.shape[0] - STAT_ROWS
    pull_out[:test_blocks, :] = pull_tiles(picked, tiles, rows, cols, live[0], test_blocks)
    pull_out[test_blocks:, :] = jnp.zeros((STAT_ROWS, LANES), F32)


def update_dual(iteration, core, restarts, time_limit, own, other, dual, sum_dual, scal, demand, load, inverse_tests):
    half = own.shape[0] - STAT_ROWS
    load[pl.ds(pl.multiple_of(core[0] * half, half), half), :] = own[:half, :]
    load[pl.ds(pl.multiple_of((1 - core[0]) * half, half), half), :] = other[:half, :]
    stats = own[half:, :]
    spent = jnp.sum(stats[0:1, :], axis=1, keepdims=True) * inverse_tests
    bdual = scal[0:1, :]
    bdual_new = jnp.maximum(bdual + step_dual * (spent - time_limit[0]), 0.0)
    bdual_total = scal[1:2, :] + bdual_new
    old = dual[...]
    new = jnp.maximum(old + step_dual * (demand[...] - load[...]), 0.0)
    dual_sq = jnp.sum((new - old) ** 2, axis=0, keepdims=True)
    total = sum_dual[...] + new
    seen = slot_count(restarts, iteration)
    restart_now = restarts[iteration] == 1
    dual_next = jnp.where(restart_now, total / seen, new)
    total_next = jnp.where(restart_now, 0.0, total)
    bdual_next = jnp.where(restart_now, bdual_total / seen, bdual_new)
    bdual_total = jnp.where(restart_now, 0.0, bdual_total)
    scal_next = jnp.concatenate(
        [bdual_next, bdual_total, (bdual_new - bdual) ** 2, stats[1:2, :], jnp.zeros((STAT_ROWS - 4, LANES), F32)],
        axis=0,
    )
    return dual_next, total_next, scal_next, dual_sq


def stat_rows(*given):
    return jnp.concatenate([*given, jnp.zeros((STAT_ROWS - len(given), LANES), F32)], axis=0)


def dual_pull_kernel(
    iteration, inverse_tests,
    rows, cols, live, core, restarts, time_limit, own, other, dual, sum_dual, scal, demand, tiles,
    pull_out, dual_out, sum_out, scal_out, picked,
):
    dual_next, total_next, scal_next, dual_sq = update_dual(
        iteration, core, restarts, time_limit, own, other, dual, sum_dual, scal, demand, picked, inverse_tests
    )
    dual_out[...] = dual_next
    sum_out[...] = total_next
    scal_out[...] = scal_next
    picked[...] = dual_next.astype(jnp.bfloat16).astype(F32)
    test_blocks = pull_out.shape[0] - STAT_ROWS
    pull_out[:test_blocks, :] = pull_tiles(picked, tiles, rows, cols, live[0], test_blocks)
    pull_out[test_blocks:, :] = stat_rows(dual_sq)


def dual_last_kernel(
    iteration, inverse_tests,
    core, restarts, time_limit, own, other, dual, sum_dual, scal, demand,
    dual_out, scal_out, sq_out, load,
):
    dual_next, _, scal_next, dual_sq = update_dual(
        iteration, core, restarts, time_limit, own, other, dual, sum_dual, scal, demand, load, inverse_tests
    )
    dual_out[...] = dual_next
    scal_out[...] = scal_next
    sq_out[...] = stat_rows(dual_sq)


def primal_load_kernel(
    iteration,
    rows, cols, live, core, restarts, pull_own, pull_1, pull_2, pull_3, primal, sum_primal, scal, costs, runtimes, tiles,
    mine_out, other_out, primal_out, sum_out, sq_out, picked, load,
):
    test_blocks = primal.shape[0]
    parts = (pull_own, pull_1, pull_2, pull_3)
    pull = sum_four(parts, slice(0, test_blocks))
    sq_out[...] = sum_four(parts, slice(test_blocks, test_blocks + STAT_ROWS))
    old = primal[...]
    new = jnp.clip(old - step_primal * (costs[...] - pull + scal[0:1, :] * runtimes[...]), 0.0, 1.0)
    extrap = (2.0 * new - old).astype(jnp.bfloat16).astype(F32)
    picked[...] = extrap
    stats = stat_rows(
        jnp.sum(runtimes[...] * extrap, axis=0, keepdims=True),
        jnp.sum((new - old) ** 2, axis=0, keepdims=True),
    )
    total = sum_primal[...] + new
    restart_now = restarts[iteration] == 1
    primal_out[...] = jnp.where(restart_now, total / slot_count(restarts, iteration), new)
    sum_out[...] = jnp.where(restart_now, 0.0, total)
    load[...] = load_tiles(picked, tiles, rows, cols, live[0], load.shape[0])
    half = load.shape[0] // 2
    mine_out[:half, :] = load[pl.ds(pl.multiple_of(core[0] * half, half), half), :]
    mine_out[half:, :] = stats
    other_out[:half, :] = load[pl.ds(pl.multiple_of((1 - core[0]) * half, half), half), :]
    other_out[half:, :] = stats


def norms_kernel(sq_0, sq_1, last_0, last_1, last_2, last_3, scal_0, scal_1, scal_2, norms_out):
    row_ids = lax.broadcasted_iota(jnp.int32, norms_out.shape, 0)
    col_ids = lax.broadcasted_iota(jnp.int32, norms_out.shape, 1)
    last = sum_four((last_0, last_1, last_2, last_3), slice(0, 1))
    out = jnp.zeros(norms_out.shape, F32)
    for k, (sq, scal) in enumerate(((sq_0[0:1, :], scal_0), (sq_1[0:1, :], scal_1), (last, scal_2))):
        move_dual = jnp.sum(sq, axis=1, keepdims=True) + scal[2:3, 0:1]
        move_primal = jnp.sum(scal[3:4, :], axis=1, keepdims=True)
        out = jnp.where(row_ids == k, jnp.where(col_ids == 0, move_primal, move_dual), out)
    norms_out[...] = out


def call(body, outs, n_smem, n_vmem, scratch=()):
    return pl.pallas_call(
        body,
        out_shape=outs,
        in_specs=[SMEM] * n_smem + [VMEM] * n_vmem,
        out_specs=jax.tree.map(lambda _: VMEM, outs),
        scratch_shapes=list(scratch),
        compiler_params=pltpu.CompilerParams(vmem_limit_bytes=24 * 1024 * 1024),
    )


def per_device(
    n_y, n_z,
    coverage_tiles, tile_rows, tile_cols, tile_counts, test_costs, runtimes, time_limit, demand,
    primal_start, dual_start, limit_dual_start, restarts,
):
    test_blocks = test_costs.shape[0] // LANES
    req_blocks = demand.shape[0] // LANES
    half = req_blocks // 2
    inverse_tests = 1.0 / (test_costs.shape[0] * lax.axis_size("tst"))
    core = (lax.axis_index("tst") % 2).astype(jnp.int32).reshape(1)
    costs = test_costs.reshape(test_blocks, LANES)
    runs = runtimes.reshape(test_blocks, LANES)
    want = demand.reshape(req_blocks, LANES)
    primal = primal_start.reshape(test_blocks, LANES)
    dual = dual_start.reshape(req_blocks, LANES)
    sum_primal = jnp.zeros_like(primal)
    sum_dual = jnp.zeros_like(dual)
    scal = jnp.concatenate(
        [jnp.broadcast_to(limit_dual_start.reshape(1, 1), (1, LANES)), jnp.zeros((STAT_ROWS - 1, LANES), F32)], axis=0
    )

    def on_tst(x, move):
        pairs = []
        for y in range(n_y):
            for z in range(n_z):
                for c in range(2):
                    to_y, to_z, to_c = move(y, z, c)
                    pairs.append(((y * n_z + z) * 2 + c, (to_y * n_z + to_z) * 2 + to_c))
        return lax.ppermute(x, "tst", pairs)

    def on_req(x):
        n_req = lax.axis_size("req")
        return [lax.ppermute(x, "req", [(i, i ^ bit) for i in range(n_req)]) for bit in (1, 2, 3)]

    def swap_core(x):
        return on_tst(x, lambda y, z, c: (y, z, 1 - c))

    def total_tst(mine, other):
        with jax.named_scope("sum_core"):
            x = mine + swap_core(other)
        with jax.named_scope("sum_y"):
            a, b, c = [on_tst(x, lambda y, z, c, bit=bit: (y ^ bit, z, c)) for bit in (1, 2, 3)]
            x = (x + a) + (b + c)
        with jax.named_scope("sum_z_inner"):
            a, b, c = [on_tst(x, lambda y, z, c, bit=bit: (y, z ^ bit, c)) for bit in (1, 2, 3)]
            x = (x + a) + (b + c)
        with jax.named_scope("sum_z_outer"):
            x = x + on_tst(x, lambda y, z, c: (y, n_z - 1 - z, c))
        with jax.named_scope("both_halves"):
            return x, swap_core(x)

    big_t = struct(test_blocks, LANES)
    big_r = struct(req_blocks, LANES)
    small = struct(STAT_ROWS, LANES)
    pull_shape = struct(test_blocks + STAT_ROWS, LANES)
    half_shape = struct(half + STAT_ROWS, LANES)
    rows_scratch = pltpu.VMEM((req_blocks, LANES), F32)
    cols_scratch = pltpu.VMEM((test_blocks, LANES), F32)
    slots = (tile_rows, tile_cols, tile_counts)
    sq_list, scal_list = [], []
    for iteration in range(ITERS):
        if iteration == 0:
            pull = call(first_pull_kernel, pull_shape, 3, 2, [rows_scratch])(*slots, dual, coverage_tiles)
        else:
            pull, dual, sum_dual, scal = call(
                functools.partial(dual_pull_kernel, iteration - 1, inverse_tests),
                (pull_shape, big_r, big_r, small), 6, 7, [rows_scratch],
            )(*slots, core, restarts, time_limit, own, other, dual, sum_dual, scal, want, coverage_tiles)
            scal_list.append(scal)
        with jax.named_scope("sum_req"):
            parts = [pull, *on_req(pull)]
        mine, other, primal, sum_primal, sq = call(
            functools.partial(primal_load_kernel, iteration),
            (half_shape, half_shape, big_t, big_t, small), 5, 10, [cols_scratch, rows_scratch],
        )(*slots, core, restarts, *parts, primal, sum_primal, scal, costs, runs, coverage_tiles)
        if iteration > 0:
            sq_list.append(sq)
        own, other = total_tst(mine, other)
    dual, scal, sq = call(
        functools.partial(dual_last_kernel, ITERS - 1, inverse_tests), (big_r, small, small), 3, 6, [rows_scratch]
    )(core, restarts, time_limit, own, other, dual, sum_dual, scal, want)
    scal_list.append(scal)
    with jax.named_scope("sum_req"):
        last = [sq, *on_req(sq)]
    norms = call(norms_kernel, struct(ITERS, 2), 0, 9)(*sq_list, *last, *scal_list)
    return primal.reshape(-1), dual.reshape(-1), scal[0, :1], norms


def solution(mesh):
    n_tst = mesh.shape["tst"]
    n_z = n_tst // 8
    return jax.shard_map(
        functools.partial(per_device, 4, n_z),
        mesh=mesh,
        in_specs=(
            P(("tst", "req"), None, None),
            P(("tst", "req")),
            P(("tst", "req")),
            P(("tst", "req")),
            P("tst"),
            P("tst"),
            P(),
            P("req"),
            P("tst"),
            P("req"),
            P(),
            P(),
        ),
        out_specs=(P("tst"), P("req"), P(), P()),
        check_vma=False,
    )
```

```python
import functools

import jax
import jax.numpy as jnp
from jax import lax
from jax.experimental import pallas as pl
from jax.experimental.pallas import tpu as pltpu
from jax.sharding import PartitionSpec as P

ITERS = 3
LANES = 128
STAT_ROWS = 8
GROUP = 16
CHUNKS = 4

step_primal = 0.6
step_dual = 0.6

VMEM = pl.BlockSpec(memory_space=pltpu.VMEM)
HBM = pl.BlockSpec(memory_space=pltpu.HBM)
F32 = jnp.float32
BF16 = jnp.bfloat16


def struct(*shape, dtype=F32):
    return jax.ShapeDtypeStruct(shape, dtype)


def stat_rows(*given):
    return jnp.concatenate([*given, jnp.zeros((STAT_ROWS - len(given), LANES), F32)], axis=0)


def sum_four(parts, rows):
    a, b, c, d = [part[rows, :] for part in parts]
    return (a + b) + (c + d)


def slot_count(params, iteration):
    seen = jnp.ones((1, LANES), F32)
    for earlier in range(iteration):
        seen = jnp.where(params[1 + earlier : 2 + earlier, :] == 1.0, 1.0, seen + 1.0)
    return seen


def average(params, iteration, total, new):
    restart_now = params[1 + iteration : 2 + iteration, :] == 1.0
    return (
        jnp.where(restart_now, total / slot_count(params, iteration), new),
        jnp.where(restart_now, 0.0, total),
    )


def spread(picked, group):
    rows = picked[group * GROUP : (group + 1) * GROUP, :]
    row_ids = lax.broadcasted_iota(jnp.int32, rows.shape, 0)
    return jnp.concatenate(
        [jnp.where(row_ids == offset, rows, 0.0) for offset in range(GROUP)], axis=1
    ).astype(BF16)


def gather_rows(pick, source):
    return jnp.dot(pick, source.astype(BF16), preferred_element_type=F32)


def scatter_sum(place, contrib):
    return jnp.dot(place, contrib, preferred_element_type=F32, precision=lax.Precision.HIGHEST)


def pull_group(picked, tiles, group):
    block = tiles[group * GROUP : (group + 1) * GROUP].reshape(GROUP * LANES, LANES)
    return jnp.dot(spread(picked, group), block, preferred_element_type=F32)


def load_group(picked, tiles, group):
    block = jnp.concatenate([tiles[group * GROUP + offset] for offset in range(GROUP)], axis=1)
    return lax.dot_general(
        spread(picked, group), block, (((1,), (1,)), ((), ())), preferred_element_type=F32
    )


def first_pull_kernel(
    tiles_in, dual_in, rows_in, cols_in, live_in, limit_in, bdual_in, restarts_in,
    pull_out, tiles, pick_rows, place_rows, pick_cols, place_cols, params_out, scal_out,
    dual, rows, cols, live, limit, bdual, restarts, sems, tile_sems,
):
    slots = tiles.shape[0]
    small = []
    for n, (source, target) in enumerate((
        (rows_in, rows), (cols_in, cols), (live_in, live), (dual_in, dual),
        (limit_in, limit), (bdual_in, bdual), (restarts_in, restarts),
    )):
        small.append(pltpu.make_async_copy(source, target, sems.at[n]))
        small[-1].start()
    per_chunk = slots // CHUNKS
    chunks = []
    for n in range(CHUNKS):
        part = pl.ds(n * per_chunk, per_chunk)
        chunks.append(pltpu.make_async_copy(tiles_in.at[part], tiles.at[part], tile_sems.at[n]))
        chunks[-1].start()
    for copy in small:
        copy.wait()
    req_blocks = dual.shape[0]
    test_blocks = pull_out.shape[0] - STAT_ROWS
    alive = lax.broadcasted_iota(jnp.int32, (1, slots), 1) < live[...]
    at_row = lax.broadcasted_iota(jnp.int32, (req_blocks, slots), 0) == rows[...]
    at_col = lax.broadcasted_iota(jnp.int32, (test_blocks, slots), 0) == cols[...]
    one_row = jnp.where(at_row, 1.0, 0.0)
    one_col = jnp.where(at_col, 1.0, 0.0)
    place_rows[...] = jnp.where(alive, one_row, 0.0)
    place_cols[...] = jnp.where(alive, one_col, 0.0)
    pick = one_row.T.astype(BF16)
    pick_rows[...] = pick
    pick_cols[...] = jnp.concatenate([one_col, jnp.zeros((slots - test_blocks, slots), F32)], axis=0).T.astype(BF16)
    wide = lambda x: jnp.broadcast_to(x, (1, LANES))
    flags = restarts[...].astype(F32)
    params_out[...] = stat_rows(wide(limit[...]), *[wide(flags[:, k : k + 1]) for k in range(ITERS)])
    scal_out[...] = stat_rows(wide(bdual[...]))
    picked = gather_rows(pick, dual[...])
    groups = slots // GROUP
    contrib = []
    for group in range(groups):
        if group % (groups // CHUNKS) == 0:
            chunks[group // (groups // CHUNKS)].wait()
        contrib.append(pull_group(picked, tiles, group))
    pull_out[:test_blocks, :] = scatter_sum(place_cols[...], jnp.concatenate(contrib, axis=0))
    pull_out[test_blocks:, :] = jnp.zeros((STAT_ROWS, LANES), F32)


def update_dual(iteration, inverse_tests, own, other, params, dual, sum_dual, scal, demand):
    req_blocks = dual.shape[0]
    load = own[:req_blocks, :] + other[:req_blocks, :]
    stats = own[req_blocks:, :] + other[req_blocks:, :]
    spent = jnp.sum(stats[0:1, :], axis=1, keepdims=True) * inverse_tests
    bdual = scal[0:1, :]
    bdual_new = jnp.maximum(bdual + step_dual * (spent - params[0:1, :]), 0.0)
    old = dual[...]
    new = jnp.maximum(old + step_dual * (demand[...] - load), 0.0)
    dual_sq = jnp.sum((new - old) ** 2, axis=0, keepdims=True)
    total = new if sum_dual is None else sum_dual[...] + new
    dual_next, total_next = average(params, iteration, total, new)
    bdual_next, bdual_total = average(params, iteration, scal[1:2, :] + bdual_new, bdual_new)
    scal_next = stat_rows(bdual_next, bdual_total, (bdual_new - bdual) ** 2, stats[1:2, :])
    return dual_next, total_next, scal_next, dual_sq


def dual_pull_kernel(iteration, inverse_tests, *refs):
    own, other, params, tiles, pick_rows, place_cols, dual, scal, demand, *refs = refs
    sum_dual = refs.pop(0) if iteration > 0 else None
    pull_out, dual_out, sum_out, scal_out = refs
    dual_next, total_next, scal_next, dual_sq = update_dual(
        iteration, inverse_tests, own, other, params, dual, sum_dual, scal, demand
    )
    dual_out[...] = dual_next
    sum_out[...] = total_next
    scal_out[...] = scal_next
    picked = gather_rows(pick_rows[...], dual_next)
    contrib = [pull_group(picked, tiles, group) for group in range(tiles.shape[0] // GROUP)]
    test_blocks = pull_out.shape[0] - STAT_ROWS
    pull_out[:test_blocks, :] = scatter_sum(place_cols[...], jnp.concatenate(contrib, axis=0))
    pull_out[test_blocks:, :] = stat_rows(dual_sq)


def dual_last_kernel(
    iteration, inverse_tests, own, other, params, dual, scal, demand, sum_dual, dual_out, scal_out, sq_out
):
    dual_next, _, scal_next, dual_sq = update_dual(
        iteration, inverse_tests, own, other, params, dual, sum_dual, scal, demand
    )
    dual_out[...] = dual_next
    scal_out[...] = scal_next
    sq_out[...] = stat_rows(dual_sq)


def primal_load_kernel(iteration, *refs):
    pull_own, pull_1, pull_2, pull_3, params, tiles, pick_cols, place_rows, primal, scal, costs, runtimes, *refs = refs
    sum_primal = refs.pop(0) if iteration > 0 else None
    load_out, primal_out, sum_out, sq_out = refs
    test_blocks = primal.shape[0]
    slots = tiles.shape[0]
    parts = (pull_own, pull_1, pull_2, pull_3)
    pull = sum_four(parts, slice(0, test_blocks))
    sq_out[...] = sum_four(parts, slice(test_blocks, test_blocks + STAT_ROWS))
    old = primal[...]
    new = jnp.clip(old - step_primal * (costs[...] - pull + scal[0:1, :] * runtimes[...]), 0.0, 1.0)
    extrap = (2.0 * new - old).astype(BF16).astype(F32)
    total = new if sum_primal is None else sum_primal[...] + new
    primal_next, total_next = average(params, iteration, total, new)
    primal_out[...] = primal_next
    sum_out[...] = total_next
    padded = jnp.concatenate([extrap, jnp.zeros((slots - test_blocks, LANES), F32)], axis=0)
    picked = gather_rows(pick_cols[...], padded)
    contrib = [load_group(picked, tiles, group) for group in range(slots // GROUP)]
    req_blocks = load_out.shape[0] - STAT_ROWS
    load_out[:req_blocks, :] = scatter_sum(place_rows[...], jnp.concatenate(contrib, axis=0))
    load_out[req_blocks:, :] = stat_rows(
        jnp.sum(runtimes[...] * extrap, axis=0, keepdims=True),
        jnp.sum((new - old) ** 2, axis=0, keepdims=True),
    )


def norms_kernel(sq_0, sq_1, last_0, last_1, last_2, last_3, scal_0, scal_1, scal_2, norms_out):
    row_ids = lax.broadcasted_iota(jnp.int32, norms_out.shape, 0)
    col_ids = lax.broadcasted_iota(jnp.int32, norms_out.shape, 1)
    last = sum_four((last_0, last_1, last_2, last_3), slice(0, 1))
    out = jnp.zeros(norms_out.shape, F32)
    for k, (sq, scal) in enumerate(((sq_0[0:1, :], scal_0), (sq_1[0:1, :], scal_1), (last, scal_2))):
        move_dual = jnp.sum(sq, axis=1, keepdims=True) + scal[2:3, 0:1]
        move_primal = jnp.sum(scal[3:4, :], axis=1, keepdims=True)
        out = jnp.where(row_ids == k, jnp.where(col_ids == 0, move_primal, move_dual), out)
    norms_out[...] = out


def call(body, outs, n_in, scratch=(), space=VMEM):
    return pl.pallas_call(
        body,
        out_shape=outs,
        in_specs=[space] * n_in,
        out_specs=jax.tree.map(lambda _: VMEM, outs),
        scratch_shapes=list(scratch),
        compiler_params=pltpu.CompilerParams(vmem_limit_bytes=16 * 1024 * 1024),
    )


def per_device(
    n_y, n_z,
    coverage_tiles, tile_rows, tile_cols, tile_counts, test_costs, runtimes, time_limit, demand,
    primal_start, dual_start, limit_dual_start, restarts,
):
    slots = coverage_tiles.shape[0]
    test_blocks = test_costs.shape[0] // LANES
    req_blocks = demand.shape[0] // LANES
    inverse_tests = 1.0 / (test_costs.shape[0] * lax.axis_size("tst"))
    costs = test_costs.reshape(test_blocks, LANES)
    runs = runtimes.reshape(test_blocks, LANES)
    want = demand.reshape(req_blocks, LANES)
    primal = primal_start.reshape(test_blocks, LANES)
    dual = dual_start.reshape(req_blocks, LANES)

    def on_tst(x, move):
        pairs = []
        for y in range(n_y):
            for z in range(n_z):
                for c in range(2):
                    to = move(y, z, c)
                    if to is not None:
                        pairs.append(((y * n_z + z) * 2 + c, (to[0] * n_z + to[1]) * 2 + to[2]))
        return lax.ppermute(x, "tst", pairs)

    def on_req(x):
        n_req = lax.axis_size("req")
        return [lax.ppermute(x, "req", [(i, i ^ bit) for i in range(n_req)]) for bit in (1, 2, 3)]

    def swap_core(x):
        return on_tst(x, lambda y, z, c: (y, z, 1 - c))

    def by_core(x, axis, bits):
        def move(y, z, c):
            if bits[c] is None:
                return None
            return (y ^ bits[c], z, c) if axis == "y" else (y, z ^ bits[c], c)

        return on_tst(x, move)

    def total_tst(x):
        first = lax.axis_index("tst") % 2 == 0
        with jax.named_scope("sum_core"):
            x = x + swap_core(x)
        with jax.named_scope("sum_z"):
            a, b, c = [by_core(x, "z", bits) for bits in ((1, 5), (2, 6), (3, 7))]
            d = by_core(x, "z", (None, 4))
            x = (jnp.where(first, x, d) + a) + (b + c)
        with jax.named_scope("sum_z_core"):
            x = x + swap_core(x)
        with jax.named_scope("sum_y"):
            a = by_core(x, "y", (1, 2))
            b = by_core(x, "y", (None, 3))
            x = jnp.where(first, x, b) + a
        with jax.named_scope("sum_y_core"):
            return x, swap_core(x)

    big_t = struct(test_blocks, LANES)
    big_r = struct(req_blocks, LANES)
    small = struct(STAT_ROWS, LANES)
    pull_shape = struct(test_blocks + STAT_ROWS, LANES)
    load_shape = struct(req_blocks + STAT_ROWS, LANES)
    sq_list, scal_list = [], []
    sum_primal = sum_dual = ()
    for iteration in range(ITERS):
        if iteration == 0:
            given = (
                coverage_tiles, dual, tile_rows.reshape(1, slots), tile_cols.reshape(1, slots), tile_counts.reshape(1, 1),
                time_limit.reshape(1, 1), limit_dual_start.reshape(1, 1), restarts.reshape(1, ITERS),
            )
            pull, tiles, pick_rows, place_rows, pick_cols, place_cols, params, scal = call(
                first_pull_kernel,
                (
                    pull_shape, struct(*coverage_tiles.shape, dtype=BF16), struct(slots, req_blocks, dtype=BF16),
                    struct(req_blocks, slots), struct(slots, slots, dtype=BF16), struct(test_blocks, slots), small, small,
                ),
                len(given),
                [pltpu.VMEM(x.shape, x.dtype) for x in given[1:]]
                + [pltpu.SemaphoreType.DMA((len(given) - 1,)), pltpu.SemaphoreType.DMA((CHUNKS,))],
                HBM,
            )(*given)
        else:
            given = (own, other, params, tiles, pick_rows, place_cols, dual, scal, want, *sum_dual)
            pull, dual, total, scal = call(
                functools.partial(dual_pull_kernel, iteration - 1, inverse_tests),
                (pull_shape, big_r, big_r, small), len(given),
            )(*given)
            sum_dual = (total,)
            scal_list.append(scal)
        with jax.named_scope("sum_req"):
            parts = [pull, *on_req(pull)]
        given = (*parts, params, tiles, pick_cols, place_rows, primal, scal, costs, runs, *sum_primal)
        load, primal, total, sq = call(
            functools.partial(primal_load_kernel, iteration), (load_shape, big_t, big_t, small), len(given)
        )(*given)
        sum_primal = (total,)
        if iteration > 0:
            sq_list.append(sq)
        own, other = total_tst(load)
    dual, scal, sq = call(
        functools.partial(dual_last_kernel, ITERS - 1, inverse_tests), (big_r, small, small), 7
    )(own, other, params, dual, scal, want, *sum_dual)
    scal_list.append(scal)
    with jax.named_scope("sum_req"):
        last = [sq, *on_req(sq)]
    norms = call(norms_kernel, struct(ITERS, 2), 9)(*sq_list, *last, *scal_list)
    return primal.reshape(-1), dual.reshape(-1), scal[0, :1], norms


def solution(mesh):
    n_y = 4
    n_z = mesh.shape["tst"] // (2 * n_y)
    return jax.shard_map(
        functools.partial(per_device, n_y, n_z),
        mesh=mesh,
        in_specs=(
            P(("tst", "req"), None, None),
            P(("tst", "req")),
            P(("tst", "req")),
            P(("tst", "req")),
            P("tst"),
            P("tst"),
            P(),
            P("req"),
            P("tst"),
            P("req"),
            P(),
            P(),
        ),
        out_specs=(P("tst"), P("req"), P(), P()),
        check_vma=False,
    )
```

```python
import functools

import jax
import jax.numpy as jnp
from jax import lax
from jax.experimental import pallas as pl
from jax.experimental.pallas import tpu as pltpu
from jax.sharding import PartitionSpec as P

ITERS = 3
LANES = 128
STAT_ROWS = 8
GROUP = 16

step_primal = 0.6
step_dual = 0.6

VMEM = pl.BlockSpec(memory_space=pltpu.VMEM)
HBM = pl.BlockSpec(memory_space=pltpu.HBM)
F32 = jnp.float32
BF16 = jnp.bfloat16


def struct(*shape, dtype=F32):
    return jax.ShapeDtypeStruct(shape, dtype)


def stat_rows(*given):
    return jnp.concatenate([*given, jnp.zeros((STAT_ROWS - len(given), LANES), F32)], axis=0)


def sum_four(parts, rows):
    a, b, c, d = [part[rows, :] for part in parts]
    return (a + b) + (c + d)


def slot_count(params, iteration):
    seen = jnp.ones((1, LANES), F32)
    for earlier in range(iteration):
        seen = jnp.where(params[1 + earlier : 2 + earlier, :] == 1.0, 1.0, seen + 1.0)
    return seen


def average(params, iteration, total, new):
    restart_now = params[1 + iteration : 2 + iteration, :] == 1.0
    return (
        jnp.where(restart_now, total / slot_count(params, iteration), new),
        jnp.where(restart_now, 0.0, total),
    )


def spread(picked, group):
    rows = picked[group * GROUP : (group + 1) * GROUP, :]
    row_ids = lax.broadcasted_iota(jnp.int32, rows.shape, 0)
    return jnp.concatenate(
        [jnp.where(row_ids == offset, rows, 0.0) for offset in range(GROUP)], axis=1
    ).astype(BF16)


def gather_rows(pick, source):
    return jnp.dot(pick, source.astype(BF16), preferred_element_type=F32)


def scatter_sum(place, contrib):
    return jnp.dot(place, contrib, preferred_element_type=F32, precision=lax.Precision.HIGHEST)


def pull_group(picked, tiles, group):
    block = tiles[group][...].reshape(GROUP * LANES, LANES)
    return jnp.dot(spread(picked, group), block, preferred_element_type=F32)


def load_group(picked, tiles, group):
    block = jnp.concatenate([tiles[group][offset] for offset in range(GROUP)], axis=1)
    return lax.dot_general(
        spread(picked, group), block, (((1,), (1,)), ((), ())), preferred_element_type=F32
    )


def first_pull_kernel(
    tiles_in, dual_in, rows_in, cols_in, live_in, pull_out, pick_rows, place_rows, pick_cols, place_cols, *refs
):
    slots = tiles_in.shape[0]
    groups = slots // GROUP
    tiles, (dual, rows, cols, live, sems, tile_sems) = refs[:groups], refs[groups:]
    small = []
    for n, (source, target) in enumerate(((rows_in, rows), (cols_in, cols), (live_in, live), (dual_in, dual))):
        small.append(pltpu.make_async_copy(source, target, sems.at[n]))
        small[-1].start()
    chunks = []
    for n in range(groups):
        chunks.append(pltpu.make_async_copy(tiles_in.at[pl.ds(n * GROUP, GROUP)], tiles[n], tile_sems.at[n]))
        chunks[-1].start()
    for copy in small:
        copy.wait()
    req_blocks = dual.shape[0]
    test_blocks = pull_out.shape[0] - STAT_ROWS
    alive = lax.broadcasted_iota(jnp.int32, (1, slots), 1) < live[...]
    at_row = lax.broadcasted_iota(jnp.int32, (req_blocks, slots), 0) == rows[...]
    at_col = lax.broadcasted_iota(jnp.int32, (test_blocks, slots), 0) == cols[...]
    one_row = jnp.where(at_row, 1.0, 0.0)
    one_col = jnp.where(at_col, 1.0, 0.0)
    place_rows[...] = jnp.where(alive, one_row, 0.0)
    place_cols[...] = jnp.where(alive, one_col, 0.0)
    pick = one_row.T.astype(BF16)
    pick_rows[...] = pick
    pick_cols[...] = jnp.concatenate([one_col, jnp.zeros((slots - test_blocks, slots), F32)], axis=0).T.astype(BF16)
    picked = gather_rows(pick, dual[...])
    contrib = []
    for group in range(groups):
        chunks[group].wait()
        contrib.append(pull_group(picked, tiles, group))
    pull_out[:test_blocks, :] = scatter_sum(place_cols[...], jnp.concatenate(contrib, axis=0))
    pull_out[test_blocks:, :] = jnp.zeros((STAT_ROWS, LANES), F32)


def update_dual(iteration, inverse_tests, summed, params, dual, sum_dual, scal, demand):
    req_blocks = dual.shape[0]
    load = summed[:req_blocks, :]
    stats = summed[req_blocks:, :]
    spent = jnp.sum(stats[0:1, :], axis=1, keepdims=True) * inverse_tests
    bdual = scal[0:1, :]
    bdual_new = jnp.maximum(bdual + step_dual * (spent - params[0:1, :]), 0.0)
    old = dual[...]
    new = jnp.maximum(old + step_dual * (demand[...] - load), 0.0)
    dual_sq = jnp.sum((new - old) ** 2, axis=0, keepdims=True)
    total = new if sum_dual is None else sum_dual[...] + new
    dual_next, total_next = average(params, iteration, total, new)
    bdual_next, bdual_total = average(params, iteration, scal[1:2, :] + bdual_new, bdual_new)
    scal_next = stat_rows(bdual_next, bdual_total, (bdual_new - bdual) ** 2, stats[1:2, :])
    return dual_next, total_next, scal_next, dual_sq


def dual_pull_kernel(iteration, inverse_tests, *refs):
    summed, params, pick_rows, place_cols, dual, scal, demand, *refs = refs
    groups = pick_rows.shape[0] // GROUP
    tiles, refs = refs[:groups], refs[groups:]
    sum_dual = refs.pop(0) if iteration > 0 else None
    pull_out, dual_out, sum_out, scal_out = refs
    dual_next, total_next, scal_next, dual_sq = update_dual(
        iteration, inverse_tests, summed, params, dual, sum_dual, scal, demand
    )
    dual_out[...] = dual_next
    sum_out[...] = total_next
    scal_out[...] = scal_next
    picked = gather_rows(pick_rows[...], dual_next)
    contrib = [pull_group(picked, tiles, group) for group in range(groups)]
    test_blocks = pull_out.shape[0] - STAT_ROWS
    pull_out[:test_blocks, :] = scatter_sum(place_cols[...], jnp.concatenate(contrib, axis=0))
    pull_out[test_blocks:, :] = stat_rows(dual_sq)


def dual_last_kernel(
    iteration, inverse_tests, summed, params, dual, scal, demand, sum_dual, dual_out, scal_out, sq_out
):
    dual_next, _, scal_next, dual_sq = update_dual(
        iteration, inverse_tests, summed, params, dual, sum_dual, scal, demand
    )
    dual_out[...] = dual_next
    scal_out[...] = scal_next
    sq_out[...] = stat_rows(dual_sq)


def primal_load_kernel(iteration, *refs):
    pull_own, pull_1, pull_2, pull_3, params, pick_cols, place_rows, primal, scal, costs, runtimes, *refs = refs
    slots = pick_cols.shape[0]
    groups = slots // GROUP
    tiles, refs = refs[:groups], refs[groups:]
    sum_primal = refs.pop(0) if iteration > 0 else None
    load_out, primal_out, sum_out, sq_out = refs
    test_blocks = primal.shape[0]
    parts = (pull_own, pull_1, pull_2, pull_3)
    pull = sum_four(parts, slice(0, test_blocks))
    sq_out[...] = sum_four(parts, slice(test_blocks, test_blocks + STAT_ROWS))
    old = primal[...]
    new = jnp.clip(old - step_primal * (costs[...] - pull + scal[0:1, :] * runtimes[...]), 0.0, 1.0)
    extrap = (2.0 * new - old).astype(BF16).astype(F32)
    total = new if sum_primal is None else sum_primal[...] + new
    primal_next, total_next = average(params, iteration, total, new)
    primal_out[...] = primal_next
    sum_out[...] = total_next
    padded = jnp.concatenate([extrap, jnp.zeros((slots - test_blocks, LANES), F32)], axis=0)
    picked = gather_rows(pick_cols[...], padded)
    contrib = [load_group(picked, tiles, group) for group in range(groups)]
    req_blocks = load_out.shape[0] - STAT_ROWS
    load_out[:req_blocks, :] = scatter_sum(place_rows[...], jnp.concatenate(contrib, axis=0))
    load_out[req_blocks:, :] = stat_rows(
        jnp.sum(runtimes[...] * extrap, axis=0, keepdims=True),
        jnp.sum((new - old) ** 2, axis=0, keepdims=True),
    )


def norms_kernel(sq_0, sq_1, last_0, last_1, last_2, last_3, scal_0, scal_1, scal_2, norms_out):
    row_ids = lax.broadcasted_iota(jnp.int32, norms_out.shape, 0)
    col_ids = lax.broadcasted_iota(jnp.int32, norms_out.shape, 1)
    last = sum_four((last_0, last_1, last_2, last_3), slice(0, 1))
    out = jnp.zeros(norms_out.shape, F32)
    for k, (sq, scal) in enumerate(((sq_0[0:1, :], scal_0), (sq_1[0:1, :], scal_1), (last, scal_2))):
        move_dual = jnp.sum(sq, axis=1, keepdims=True) + scal[2:3, 0:1]
        move_primal = jnp.sum(scal[3:4, :], axis=1, keepdims=True)
        out = jnp.where(row_ids == k, jnp.where(col_ids == 0, move_primal, move_dual), out)
    norms_out[...] = out


def call(body, outs, n_in, scratch=(), space=VMEM, limit=16):
    return pl.pallas_call(
        body,
        out_shape=outs,
        in_specs=[space] * n_in,
        out_specs=jax.tree.map(lambda _: VMEM, outs),
        scratch_shapes=list(scratch),
        compiler_params=pltpu.CompilerParams(vmem_limit_bytes=limit * 1024 * 1024),
    )


def per_device(
    n_y, n_z,
    coverage_tiles, tile_rows, tile_cols, tile_counts, test_costs, runtimes, time_limit, demand,
    primal_start, dual_start, limit_dual_start, restarts,
):
    slots = coverage_tiles.shape[0]
    test_blocks = test_costs.shape[0] // LANES
    req_blocks = demand.shape[0] // LANES
    inverse_tests = 1.0 / (test_costs.shape[0] * lax.axis_size("tst"))
    costs = test_costs.reshape(test_blocks, LANES)
    runs = runtimes.reshape(test_blocks, LANES)
    want = demand.reshape(req_blocks, LANES)
    primal = primal_start.reshape(test_blocks, LANES)
    dual = dual_start.reshape(req_blocks, LANES)

    far_core = lax.axis_index("tst") % 2 == 1

    def on_tst(x, move):
        pairs = []
        for y in range(n_y):
            for z in range(n_z):
                for c in range(2):
                    to_y, to_z, to_c = move(y, z, c)
                    pairs.append(((y * n_z + z) * 2 + c, (to_y * n_z + to_z) * 2 + to_c))
        return lax.ppermute(x, "tst", pairs)

    def swap_core(x):
        return on_tst(x, lambda y, z, c: (y, z, 1 - c))

    def chips(x, y_bits, z_bits):
        return on_tst(x, lambda y, z, c: (y ^ y_bits, z ^ z_bits, c) if c == 1 else (y, z, c))

    def on_req(x):
        n_req = lax.axis_size("req")
        return [lax.ppermute(x, "req", [(i, i ^ bit) for i in range(n_req)]) for bit in (1, 2, 3)]

    def total_tst(x):
        with jax.named_scope("sum_core"):
            x = x + swap_core(x)
        with jax.named_scope("sum_y"):
            a, b, c = [chips(x, bits, 0) for bits in (1, 2, 3)]
            x = (x + a) + (b + c)
        with jax.named_scope("sum_z_inner"):
            a, b, c = [chips(x, 0, bits) for bits in (1, 2, 3)]
            x = (x + a) + (b + c)
        with jax.named_scope("sum_z_outer"):
            x = x + chips(x, 0, n_z - 1)
        with jax.named_scope("back_core"):
            return jnp.where(far_core, x, swap_core(x))

    wide = lambda x: jnp.broadcast_to(x.astype(F32).reshape(-1, 1), (x.shape[0], LANES))
    params = jnp.concatenate([wide(time_limit), wide(restarts), jnp.zeros((STAT_ROWS - 1 - ITERS, LANES), F32)], axis=0)
    scal = jnp.concatenate([wide(limit_dual_start), jnp.zeros((STAT_ROWS - 1, LANES), F32)], axis=0)
    big_t = struct(test_blocks, LANES)
    big_r = struct(req_blocks, LANES)
    small = struct(STAT_ROWS, LANES)
    pull_shape = struct(test_blocks + STAT_ROWS, LANES)
    load_shape = struct(req_blocks + STAT_ROWS, LANES)
    sq_list, scal_list = [], []
    sum_primal = sum_dual = ()
    for iteration in range(ITERS):
        if iteration == 0:
            given = (
                coverage_tiles, dual, tile_rows.reshape(1, slots), tile_cols.reshape(1, slots), tile_counts.reshape(1, 1)
            )
            pull, pick_rows, place_rows, pick_cols, place_cols, *tiles = call(
                first_pull_kernel,
                (
                    pull_shape, struct(slots, req_blocks, dtype=BF16), struct(req_blocks, slots),
                    struct(slots, slots, dtype=BF16), struct(test_blocks, slots),
                    *[struct(GROUP, LANES, LANES, dtype=BF16)] * (slots // GROUP),
                ),
                len(given),
                [pltpu.VMEM(x.shape, x.dtype) for x in given[1:]]
                + [pltpu.SemaphoreType.DMA((len(given) - 1,)), pltpu.SemaphoreType.DMA((slots // GROUP,))],
                HBM,
                50,
            )(*given)
        else:
            given = (summed, params, pick_rows, place_cols, dual, scal, want, *tiles, *sum_dual)
            pull, dual, total, scal = call(
                functools.partial(dual_pull_kernel, iteration - 1, inverse_tests),
                (pull_shape, big_r, big_r, small), len(given),
            )(*given)
            sum_dual = (total,)
            scal_list.append(scal)
        with jax.named_scope("sum_req"):
            parts = [pull, *on_req(pull)]
        given = (*parts, params, pick_cols, place_rows, primal, scal, costs, runs, *tiles, *sum_primal)
        load, primal, total, sq = call(
            functools.partial(primal_load_kernel, iteration), (load_shape, big_t, big_t, small), len(given)
        )(*given)
        sum_primal = (total,)
        if iteration > 0:
            sq_list.append(sq)
        summed = total_tst(load)
    dual, scal, sq = call(
        functools.partial(dual_last_kernel, ITERS - 1, inverse_tests), (big_r, small, small), 6
    )(summed, params, dual, scal, want, *sum_dual)
    scal_list.append(scal)
    with jax.named_scope("sum_req"):
        last = [sq, *on_req(sq)]
    norms = call(norms_kernel, struct(ITERS, 2), 9)(*sq_list, *last, *scal_list)
    return primal.reshape(-1), dual.reshape(-1), scal[0, :1], norms


def solution(mesh):
    n_y = 4
    n_z = mesh.shape["tst"] // (2 * n_y)
    return jax.shard_map(
        functools.partial(per_device, n_y, n_z),
        mesh=mesh,
        in_specs=(
            P(("tst", "req"), None, None),
            P(("tst", "req")),
            P(("tst", "req")),
            P(("tst", "req")),
            P("tst"),
            P("tst"),
            P(),
            P("req"),
            P("tst"),
            P("req"),
            P(),
            P(),
        ),
        out_specs=(P("tst"), P("req"), P(), P()),
        check_vma=False,
    )
```

```python
import functools

import jax
import jax.numpy as jnp
from jax import lax
from jax.experimental import pallas as pl
from jax.experimental.pallas import tpu as pltpu
from jax.sharding import PartitionSpec as P

ITERS = 3
LANES = 128
STAT_ROWS = 8
GROUP = 16

step_primal = 0.6
step_dual = 0.6

VMEM = pl.BlockSpec(memory_space=pltpu.VMEM)
HBM = pl.BlockSpec(memory_space=pltpu.HBM)
F32 = jnp.float32
BF16 = jnp.bfloat16


def struct(*shape, dtype=F32):
    return jax.ShapeDtypeStruct(shape, dtype)


def stat_rows(*given):
    return jnp.concatenate([*given, jnp.zeros((STAT_ROWS - len(given), LANES), F32)], axis=0)


def sum_four(parts, rows):
    a, b, c, d = [part[rows, :] for part in parts]
    return (a + b) + (c + d)


def slot_count(params, iteration):
    seen = jnp.ones((1, LANES), F32)
    for earlier in range(iteration):
        seen = jnp.where(params[1 + earlier : 2 + earlier, :] == 1.0, 1.0, seen + 1.0)
    return seen


def average(params, iteration, total, new):
    restart_now = params[1 + iteration : 2 + iteration, :] == 1.0
    return (
        jnp.where(restart_now, total / slot_count(params, iteration), new),
        jnp.where(restart_now, 0.0, total),
    )


def spread(picked, group):
    rows = picked[group * GROUP : (group + 1) * GROUP, :]
    row_ids = lax.broadcasted_iota(jnp.int32, rows.shape, 0)
    return jnp.concatenate(
        [jnp.where(row_ids == offset, rows, 0.0) for offset in range(GROUP)], axis=1
    ).astype(BF16)


def gather_rows(pick, source):
    return jnp.dot(pick, source.astype(BF16), preferred_element_type=F32)


def scatter_sum(place, contrib):
    return jnp.dot(place, contrib, preferred_element_type=F32, precision=lax.Precision.HIGHEST)


def pull_group(picked, tiles, group):
    block = tiles[group][...].reshape(GROUP * LANES, LANES)
    return jnp.dot(spread(picked, group), block, preferred_element_type=F32)


def load_group(picked, tiles, group):
    block = jnp.concatenate([tiles[group][offset] for offset in range(GROUP)], axis=1)
    return lax.dot_general(
        spread(picked, group), block, (((1,), (1,)), ((), ())), preferred_element_type=F32
    )


def first_pull_kernel(
    tiles_in, dual_in, rows_in, cols_in, live_in, pull_out, pick_rows, place_rows, pick_cols, place_cols, *refs
):
    slots = tiles_in.shape[0]
    groups = slots // GROUP
    tiles, (dual, rows, cols, live, sems, tile_sems) = refs[:groups], refs[groups:]
    small = []
    for n, (source, target) in enumerate(((rows_in, rows), (cols_in, cols), (live_in, live), (dual_in, dual))):
        small.append(pltpu.make_async_copy(source, target, sems.at[n]))
        small[-1].start()
    chunks = []
    for n in range(groups):
        chunks.append(pltpu.make_async_copy(tiles_in.at[pl.ds(n * GROUP, GROUP)], tiles[n], tile_sems.at[n]))
        chunks[-1].start()
    for copy in small:
        copy.wait()
    req_blocks = dual.shape[0]
    test_blocks = pull_out.shape[0] - STAT_ROWS
    alive = lax.broadcasted_iota(jnp.int32, (1, slots), 1) < live[...]
    at_row = lax.broadcasted_iota(jnp.int32, (req_blocks, slots), 0) == rows[...]
    at_col = lax.broadcasted_iota(jnp.int32, (test_blocks, slots), 0) == cols[...]
    one_row = jnp.where(at_row, 1.0, 0.0)
    one_col = jnp.where(at_col, 1.0, 0.0)
    place_rows[...] = jnp.where(alive, one_row, 0.0)
    place_cols[...] = jnp.where(alive, one_col, 0.0)
    pick = one_row.T.astype(BF16)
    pick_rows[...] = pick
    pick_cols[...] = jnp.concatenate([one_col, jnp.zeros((slots - test_blocks, slots), F32)], axis=0).T.astype(BF16)
    picked = gather_rows(pick, dual[...])
    contrib = []
    for group in range(groups):
        chunks[group].wait()
        contrib.append(pull_group(picked, tiles, group))
    pull_out[:test_blocks, :] = scatter_sum(place_cols[...], jnp.concatenate(contrib, axis=0))
    pull_out[test_blocks:, :] = jnp.zeros((STAT_ROWS, LANES), F32)


def update_dual(iteration, inverse_tests, summed, params, dual, sum_dual, scal, demand):
    req_blocks = dual.shape[0]
    load = summed[:req_blocks, :]
    stats = summed[req_blocks:, :]
    spent = jnp.sum(stats[0:1, :], axis=1, keepdims=True) * inverse_tests
    bdual = scal[0:1, :]
    bdual_new = jnp.maximum(bdual + step_dual * (spent - params[0:1, :]), 0.0)
    old = dual[...]
    new = jnp.maximum(old + step_dual * (demand[...] - load), 0.0)
    dual_sq = jnp.sum((new - old) ** 2, axis=0, keepdims=True)
    total = new if sum_dual is None else sum_dual[...] + new
    dual_next, total_next = average(params, iteration, total, new)
    bdual_next, bdual_total = average(params, iteration, scal[1:2, :] + bdual_new, bdual_new)
    scal_next = stat_rows(bdual_next, bdual_total, (bdual_new - bdual) ** 2, stats[1:2, :])
    return dual_next, total_next, scal_next, dual_sq


def dual_pull_kernel(iteration, inverse_tests, *refs):
    summed, params, pick_rows, place_cols, dual, scal, demand, *refs = refs
    groups = pick_rows.shape[0] // GROUP
    tiles, refs = refs[:groups], refs[groups:]
    sum_dual = refs.pop(0) if iteration > 0 else None
    pull_out, dual_out, sum_out, scal_out = refs
    dual_next, total_next, scal_next, dual_sq = update_dual(
        iteration, inverse_tests, summed, params, dual, sum_dual, scal, demand
    )
    dual_out[...] = dual_next
    sum_out[...] = total_next
    scal_out[...] = scal_next
    picked = gather_rows(pick_rows[...], dual_next)
    contrib = [pull_group(picked, tiles, group) for group in range(groups)]
    test_blocks = pull_out.shape[0] - STAT_ROWS
    pull_out[:test_blocks, :] = scatter_sum(place_cols[...], jnp.concatenate(contrib, axis=0))
    pull_out[test_blocks:, :] = stat_rows(dual_sq)


def dual_last_kernel(
    iteration, inverse_tests, summed, params, dual, scal, demand, sum_dual, dual_out, scal_out, sq_out
):
    dual_next, _, scal_next, dual_sq = update_dual(
        iteration, inverse_tests, summed, params, dual, sum_dual, scal, demand
    )
    dual_out[...] = dual_next
    scal_out[...] = scal_next
    sq_out[...] = stat_rows(dual_sq)


def primal_load_kernel(iteration, *refs):
    pull_own, pull_1, pull_2, pull_3, params, pick_cols, place_rows, primal, scal, costs, runtimes, *refs = refs
    slots = pick_cols.shape[0]
    groups = slots // GROUP
    tiles, refs = refs[:groups], refs[groups:]
    sum_primal = refs.pop(0) if iteration > 0 else None
    load_out, primal_out, sum_out, sq_out = refs
    test_blocks = primal.shape[0]
    parts = (pull_own, pull_1, pull_2, pull_3)
    pull = sum_four(parts, slice(0, test_blocks))
    sq_out[...] = sum_four(parts, slice(test_blocks, test_blocks + STAT_ROWS))
    old = primal[...]
    new = jnp.clip(old - step_primal * (costs[...] - pull + scal[0:1, :] * runtimes[...]), 0.0, 1.0)
    extrap = (2.0 * new - old).astype(BF16).astype(F32)
    total = new if sum_primal is None else sum_primal[...] + new
    primal_next, total_next = average(params, iteration, total, new)
    primal_out[...] = primal_next
    sum_out[...] = total_next
    padded = jnp.concatenate([extrap, jnp.zeros((slots - test_blocks, LANES), F32)], axis=0)
    picked = gather_rows(pick_cols[...], padded)
    contrib = [load_group(picked, tiles, group) for group in range(groups)]
    req_blocks = load_out.shape[0] - STAT_ROWS
    load_out[:req_blocks, :] = scatter_sum(place_rows[...], jnp.concatenate(contrib, axis=0))
    load_out[req_blocks:, :] = stat_rows(
        jnp.sum(runtimes[...] * extrap, axis=0, keepdims=True),
        jnp.sum((new - old) ** 2, axis=0, keepdims=True),
    )


def norms_kernel(sq_0, sq_1, last_0, last_1, last_2, last_3, scal_0, scal_1, scal_2, norms_out):
    row_ids = lax.broadcasted_iota(jnp.int32, norms_out.shape, 0)
    col_ids = lax.broadcasted_iota(jnp.int32, norms_out.shape, 1)
    last = sum_four((last_0, last_1, last_2, last_3), slice(0, 1))
    out = jnp.zeros(norms_out.shape, F32)
    for k, (sq, scal) in enumerate(((sq_0[0:1, :], scal_0), (sq_1[0:1, :], scal_1), (last, scal_2))):
        move_dual = jnp.sum(sq, axis=1, keepdims=True) + scal[2:3, 0:1]
        move_primal = jnp.sum(scal[3:4, :], axis=1, keepdims=True)
        out = jnp.where(row_ids == k, jnp.where(col_ids == 0, move_primal, move_dual), out)
    norms_out[...] = out


def call(body, outs, n_in, scratch=(), space=VMEM):
    return pl.pallas_call(
        body,
        out_shape=outs,
        in_specs=[space] * n_in,
        out_specs=jax.tree.map(lambda _: VMEM, outs),
        scratch_shapes=list(scratch),
        compiler_params=pltpu.CompilerParams(vmem_limit_bytes=50 * 1024 * 1024),
    )


def per_device(
    n_y, n_z,
    coverage_tiles, tile_rows, tile_cols, tile_counts, test_costs, runtimes, time_limit, demand,
    primal_start, dual_start, limit_dual_start, restarts,
):
    slots = coverage_tiles.shape[0]
    test_blocks = test_costs.shape[0] // LANES
    req_blocks = demand.shape[0] // LANES
    inverse_tests = 1.0 / (test_costs.shape[0] * lax.axis_size("tst"))
    costs = test_costs.reshape(test_blocks, LANES)
    runs = runtimes.reshape(test_blocks, LANES)
    want = demand.reshape(req_blocks, LANES)
    primal = primal_start.reshape(test_blocks, LANES)
    dual = dual_start.reshape(req_blocks, LANES)

    far_core = lax.axis_index("tst") % 2 == 1

    n_req = lax.axis_size("req")

    def on_mesh(x, move):
        pairs = []
        for y in range(n_y):
            for z in range(n_z):
                for c in range(2):
                    for r in range(n_req):
                        to_y, to_z, to_c, to_r = move(y, z, c, r)
                        source = ((y * n_z + z) * 2 + c) * n_req + r
                        pairs.append((source, ((to_y * n_z + to_z) * 2 + to_c) * n_req + to_r))
        return lax.ppermute(x, ("tst", "req"), pairs)

    def swap_core(x):
        return on_mesh(x, lambda y, z, c, r: (y, z, 1 - c, r))

    def chips(x, y_bits, z_bits):
        return on_mesh(x, lambda y, z, c, r: (y ^ y_bits, z ^ z_bits, c, r) if c == 1 else (y, z, c, r ^ 1))

    def on_req(x):
        return [lax.ppermute(x, "req", [(i, i ^ bit) for i in range(n_req)]) for bit in (1, 3, 2)]

    def total_tst(x):
        with jax.named_scope("sum_core"):
            x = x + swap_core(x)
        with jax.named_scope("sum_y"):
            a, b, c = [chips(x, bits, 0) for bits in (1, 3, 2)]
            x = (x + a) + (b + c)
        with jax.named_scope("sum_z_inner"):
            a, b, c = [chips(x, 0, bits) for bits in (1, 3, 2)]
            x = (x + a) + (b + c)
        with jax.named_scope("sum_z_outer"):
            x = x + chips(x, 0, n_z - 1)
        with jax.named_scope("back_core"):
            return jnp.where(far_core, x, swap_core(x))

    wide = lambda x: jnp.broadcast_to(x.astype(F32).reshape(-1, 1), (x.shape[0], LANES))
    params = jnp.concatenate([wide(time_limit), wide(restarts), jnp.zeros((STAT_ROWS - 1 - ITERS, LANES), F32)], axis=0)
    scal = jnp.concatenate([wide(limit_dual_start), jnp.zeros((STAT_ROWS - 1, LANES), F32)], axis=0)
    big_t = struct(test_blocks, LANES)
    big_r = struct(req_blocks, LANES)
    small = struct(STAT_ROWS, LANES)
    pull_shape = struct(test_blocks + STAT_ROWS, LANES)
    load_shape = struct(req_blocks + STAT_ROWS, LANES)
    sq_list, scal_list = [], []
    sum_primal = sum_dual = ()
    for iteration in range(ITERS):
        if iteration == 0:
            given = (
                coverage_tiles, dual, tile_rows.reshape(1, slots), tile_cols.reshape(1, slots), tile_counts.reshape(1, 1)
            )
            pull, pick_rows, place_rows, pick_cols, place_cols, *tiles = call(
                first_pull_kernel,
                (
                    pull_shape, struct(slots, req_blocks, dtype=BF16), struct(req_blocks, slots),
                    struct(slots, slots, dtype=BF16), struct(test_blocks, slots),
                    *[struct(GROUP, LANES, LANES, dtype=BF16)] * (slots // GROUP),
                ),
                len(given),
                [pltpu.VMEM(x.shape, x.dtype) for x in given[1:]]
                + [pltpu.SemaphoreType.DMA((len(given) - 1,)), pltpu.SemaphoreType.DMA((slots // GROUP,))],
                HBM,
            )(*given)
        else:
            given = (summed, params, pick_rows, place_cols, dual, scal, want, *tiles, *sum_dual)
            pull, dual, total, scal = call(
                functools.partial(dual_pull_kernel, iteration - 1, inverse_tests),
                (pull_shape, big_r, big_r, small), len(given),
            )(*given)
            sum_dual = (total,)
            scal_list.append(scal)
        with jax.named_scope("sum_req"):
            parts = [pull, *on_req(pull)]
        given = (*parts, params, pick_cols, place_rows, primal, scal, costs, runs, *tiles, *sum_primal)
        load, primal, total, sq = call(
            functools.partial(primal_load_kernel, iteration), (load_shape, big_t, big_t, small), len(given)
        )(*given)
        sum_primal = (total,)
        if iteration > 0:
            sq_list.append(sq)
        summed = total_tst(load)
    dual, scal, sq = call(
        functools.partial(dual_last_kernel, ITERS - 1, inverse_tests), (big_r, small, small), 6
    )(summed, params, dual, scal, want, *sum_dual)
    scal_list.append(scal)
    with jax.named_scope("sum_req"):
        last = [sq, *on_req(sq)]
    norms = call(norms_kernel, struct(ITERS, 2), 9)(*sq_list, *last, *scal_list)
    return primal.reshape(-1), dual.reshape(-1), scal[0, :1], norms


def solution(mesh):
    n_y = 4
    n_z = mesh.shape["tst"] // (2 * n_y)
    return jax.shard_map(
        functools.partial(per_device, n_y, n_z),
        mesh=mesh,
        in_specs=(
            P(("tst", "req"), None, None),
            P(("tst", "req")),
            P(("tst", "req")),
            P(("tst", "req")),
            P("tst"),
            P("tst"),
            P(),
            P("req"),
            P("tst"),
            P("req"),
            P(),
            P(),
        ),
        out_specs=(P("tst"), P("req"), P(), P()),
        check_vma=False,
    )
```

```python
import functools

import jax
import jax.numpy as jnp
from jax import lax
from jax.experimental import pallas as pl
from jax.experimental.pallas import tpu as pltpu
from jax.sharding import PartitionSpec as P

ITERS = 3
LANES = 128
STAT_ROWS = 8
GROUP = 16
KEPT = 6

step_primal = 0.6
step_dual = 0.6

VMEM = pl.BlockSpec(memory_space=pltpu.VMEM)
HBM = pl.BlockSpec(memory_space=pltpu.HBM)
F32 = jnp.float32
BF16 = jnp.bfloat16


def struct(*shape, dtype=F32):
    return jax.ShapeDtypeStruct(shape, dtype)


def stat_rows(*given):
    return jnp.concatenate([*given, jnp.zeros((STAT_ROWS - len(given), LANES), F32)], axis=0)


def sum_four(parts, rows):
    a, b, c, d = [part[rows, :] for part in parts]
    return (a + b) + (c + d)


def slot_count(params, iteration):
    seen = jnp.ones((1, LANES), F32)
    for earlier in range(iteration):
        seen = jnp.where(params[1 + earlier : 2 + earlier, :] == 1.0, 1.0, seen + 1.0)
    return seen


def average(params, iteration, total, new):
    restart_now = params[1 + iteration : 2 + iteration, :] == 1.0
    return (
        jnp.where(restart_now, total / slot_count(params, iteration), new),
        jnp.where(restart_now, 0.0, total),
    )


def spread(picked, group):
    rows = picked[group * GROUP : (group + 1) * GROUP, :]
    row_ids = lax.broadcasted_iota(jnp.int32, rows.shape, 0)
    return jnp.concatenate(
        [jnp.where(row_ids == offset, rows, 0.0) for offset in range(GROUP)], axis=1
    ).astype(BF16)


def gather_rows(pick, source):
    return jnp.dot(pick, source.astype(BF16), preferred_element_type=F32)


def scatter_sum(place, contrib):
    return jnp.dot(place, contrib, preferred_element_type=F32, precision=lax.Precision.HIGHEST)


def pull_group(picked, tiles, group):
    block = tiles[group][...].reshape(GROUP * LANES, LANES)
    return jnp.dot(spread(picked, group), block, preferred_element_type=F32)


def load_group(picked, tiles, group):
    block = jnp.concatenate([tiles[group][offset] for offset in range(GROUP)], axis=1)
    return lax.dot_general(
        spread(picked, group), block, (((1,), (1,)), ((), ())), preferred_element_type=F32
    )


def list_of(fetched):
    return [fetched.at[n] for n in range(fetched.shape[0])]


def fetch(tiles_in, fetched, sems):
    copies = []
    for n in range(fetched.shape[0]):
        part = tiles_in.at[pl.ds((KEPT + n) * GROUP, GROUP)]
        copies.append(pltpu.make_async_copy(part, fetched.at[n], sems.at[n]))
        copies[-1].start()
    return copies


def first_pull_kernel(
    tiles_in, packed, pull_out, pick_rows, place_rows, pick_cols, place_cols, params_out, scal_out, *refs
):
    slots = tiles_in.shape[0]
    groups = slots // GROUP
    kept, (fetched, tile_sems) = refs[:KEPT], refs[KEPT:]
    tiles = [*kept, *list_of(fetched)]
    chunks = []
    for n in range(groups):
        chunks.append(pltpu.make_async_copy(tiles_in.at[pl.ds(n * GROUP, GROUP)], tiles[n], tile_sems.at[n]))
        chunks[-1].start()
    req_blocks = packed.shape[0] - STAT_ROWS
    test_blocks = pull_out.shape[0] - STAT_ROWS
    rows, cols, live, limit, bdual, *flags = [packed[req_blocks + n : req_blocks + n + 1, :] for n in range(5 + ITERS)]
    params_out[...] = stat_rows(limit, *flags)
    scal_out[...] = stat_rows(bdual)
    alive = lax.broadcasted_iota(jnp.int32, (1, slots), 1) < live.astype(jnp.int32)
    at_row = lax.broadcasted_iota(jnp.int32, (req_blocks, slots), 0) == rows.astype(jnp.int32)
    at_col = lax.broadcasted_iota(jnp.int32, (test_blocks, slots), 0) == cols.astype(jnp.int32)
    one_row = jnp.where(at_row, 1.0, 0.0)
    one_col = jnp.where(at_col, 1.0, 0.0)
    place_rows[...] = jnp.where(alive, one_row, 0.0)
    place_cols[...] = jnp.where(alive, one_col, 0.0)
    pick = one_row.T.astype(BF16)
    pick_rows[...] = pick
    pick_cols[...] = jnp.concatenate([one_col, jnp.zeros((slots - test_blocks, slots), F32)], axis=0).T.astype(BF16)
    picked = gather_rows(pick, packed[:req_blocks, :])
    contrib = []
    for group in range(groups):
        chunks[group].wait()
        contrib.append(pull_group(picked, tiles, group))
    pull_out[:test_blocks, :] = scatter_sum(place_cols[...], jnp.concatenate(contrib, axis=0))
    pull_out[test_blocks:, :] = jnp.zeros((STAT_ROWS, LANES), F32)


def update_dual(iteration, inverse_tests, summed, params, dual, sum_dual, scal, demand):
    req_blocks = dual.shape[0]
    load = summed[:req_blocks, :]
    stats = summed[req_blocks:, :]
    spent = jnp.sum(stats[0:1, :], axis=1, keepdims=True) * inverse_tests
    bdual = scal[0:1, :]
    bdual_new = jnp.maximum(bdual + step_dual * (spent - params[0:1, :]), 0.0)
    old = dual[...]
    new = jnp.maximum(old + step_dual * (demand[...] - load), 0.0)
    dual_sq = jnp.sum((new - old) ** 2, axis=0, keepdims=True)
    total = new if sum_dual is None else sum_dual[...] + new
    dual_next, total_next = average(params, iteration, total, new)
    bdual_next, bdual_total = average(params, iteration, scal[1:2, :] + bdual_new, bdual_new)
    scal_next = stat_rows(bdual_next, bdual_total, (bdual_new - bdual) ** 2, stats[1:2, :])
    return dual_next, total_next, scal_next, dual_sq


def dual_pull_kernel(iteration, inverse_tests, *refs):
    summed, params, pick_rows, place_cols, dual, scal, demand, *refs = refs
    tiles_in, kept, refs = refs[0], refs[1 : 1 + KEPT], refs[1 + KEPT :]
    sum_dual = refs.pop(0) if iteration > 0 else None
    pull_out, dual_out, sum_out, scal_out, fetched, sems = refs
    copies = fetch(tiles_in, fetched, sems)
    dual_next, total_next, scal_next, dual_sq = update_dual(
        iteration, inverse_tests, summed, params, dual, sum_dual, scal, demand
    )
    dual_out[...] = dual_next
    sum_out[...] = total_next
    scal_out[...] = scal_next
    picked = gather_rows(pick_rows[...], dual_next)
    contrib = [pull_group(picked, kept, group) for group in range(KEPT)]
    for copy in copies:
        copy.wait()
    contrib += [pull_group(picked, [None] * KEPT + list_of(fetched), group) for group in range(KEPT, tiles_in.shape[0] // GROUP)]
    test_blocks = pull_out.shape[0] - STAT_ROWS
    pull_out[:test_blocks, :] = scatter_sum(place_cols[...], jnp.concatenate(contrib, axis=0))
    pull_out[test_blocks:, :] = stat_rows(dual_sq)


def dual_last_kernel(
    iteration, inverse_tests, summed, params, dual, scal, demand, sum_dual, dual_out, scal_out, sq_out
):
    dual_next, _, scal_next, dual_sq = update_dual(
        iteration, inverse_tests, summed, params, dual, sum_dual, scal, demand
    )
    dual_out[...] = dual_next
    scal_out[...] = scal_next
    sq_out[...] = stat_rows(dual_sq)


def primal_load_kernel(iteration, *refs):
    pull_own, pull_1, pull_2, pull_3, params, pick_cols, place_rows, primal, scal, costs, runtimes, *refs = refs
    slots = pick_cols.shape[0]
    tiles_in, kept, refs = refs[0], refs[1 : 1 + KEPT], refs[1 + KEPT :]
    sum_primal = refs.pop(0) if iteration > 0 else None
    load_out, primal_out, sum_out, sq_out, fetched, sems = refs
    copies = fetch(tiles_in, fetched, sems)
    test_blocks = primal.shape[0]
    parts = (pull_own, pull_1, pull_2, pull_3)
    pull = sum_four(parts, slice(0, test_blocks))
    sq_out[...] = sum_four(parts, slice(test_blocks, test_blocks + STAT_ROWS))
    old = primal[...]
    new = jnp.clip(old - step_primal * (costs[...] - pull + scal[0:1, :] * runtimes[...]), 0.0, 1.0)
    extrap = (2.0 * new - old).astype(BF16).astype(F32)
    total = new if sum_primal is None else sum_primal[...] + new
    primal_next, total_next = average(params, iteration, total, new)
    primal_out[...] = primal_next
    sum_out[...] = total_next
    padded = jnp.concatenate([extrap, jnp.zeros((slots - test_blocks, LANES), F32)], axis=0)
    picked = gather_rows(pick_cols[...], padded)
    contrib = [load_group(picked, kept, group) for group in range(KEPT)]
    for copy in copies:
        copy.wait()
    contrib += [load_group(picked, [None] * KEPT + list_of(fetched), group) for group in range(KEPT, slots // GROUP)]
    req_blocks = load_out.shape[0] - STAT_ROWS
    load_out[:req_blocks, :] = scatter_sum(place_rows[...], jnp.concatenate(contrib, axis=0))
    load_out[req_blocks:, :] = stat_rows(
        jnp.sum(runtimes[...] * extrap, axis=0, keepdims=True),
        jnp.sum((new - old) ** 2, axis=0, keepdims=True),
    )


def norms_kernel(sq_0, sq_1, last_0, last_1, last_2, last_3, scal_0, scal_1, scal_2, norms_out):
    row_ids = lax.broadcasted_iota(jnp.int32, norms_out.shape, 0)
    col_ids = lax.broadcasted_iota(jnp.int32, norms_out.shape, 1)
    last = sum_four((last_0, last_1, last_2, last_3), slice(0, 1))
    out = jnp.zeros(norms_out.shape, F32)
    for k, (sq, scal) in enumerate(((sq_0[0:1, :], scal_0), (sq_1[0:1, :], scal_1), (last, scal_2))):
        move_dual = jnp.sum(sq, axis=1, keepdims=True) + scal[2:3, 0:1]
        move_primal = jnp.sum(scal[3:4, :], axis=1, keepdims=True)
        out = jnp.where(col_ids == k, jnp.where(row_ids == 0, move_primal, move_dual), out)
    norms_out[...] = out


def call(body, outs, specs, scratch=()):
    return pl.pallas_call(
        body,
        out_shape=outs,
        in_specs=specs,
        out_specs=jax.tree.map(lambda _: VMEM, outs),
        scratch_shapes=list(scratch),
        compiler_params=pltpu.CompilerParams(vmem_limit_bytes=50 * 1024 * 1024),
    )


def per_device(
    n_y, n_z,
    coverage_tiles, tile_rows, tile_cols, tile_counts, test_costs, runtimes, time_limit, demand,
    primal_start, dual_start, limit_dual_start, restarts,
):
    slots = coverage_tiles.shape[0]
    test_blocks = test_costs.shape[0] // LANES
    req_blocks = demand.shape[0] // LANES
    inverse_tests = 1.0 / (test_costs.shape[0] * lax.axis_size("tst"))
    costs = test_costs.reshape(test_blocks, LANES)
    runs = runtimes.reshape(test_blocks, LANES)
    want = demand.reshape(req_blocks, LANES)
    primal = primal_start.reshape(test_blocks, LANES)
    dual = dual_start.reshape(req_blocks, LANES)

    far_core = lax.axis_index("tst") % 2 == 1

    n_req = lax.axis_size("req")

    def on_mesh(x, move):
        pairs = []
        for y in range(n_y):
            for z in range(n_z):
                for c in range(2):
                    for r in range(n_req):
                        to_y, to_z, to_c, to_r = move(y, z, c, r)
                        source = ((y * n_z + z) * 2 + c) * n_req + r
                        pairs.append((source, ((to_y * n_z + to_z) * 2 + to_c) * n_req + to_r))
        return lax.ppermute(x, ("tst", "req"), pairs)

    def swap_core(x):
        return on_mesh(x, lambda y, z, c, r: (y, z, 1 - c, r))

    def chips(x, y_bits, z_bits):
        return on_mesh(x, lambda y, z, c, r: (y ^ y_bits, z ^ z_bits, c, r) if c == 1 else (y, z, c, r ^ 1))

    def on_req(x):
        return [lax.ppermute(x, "req", [(i, i ^ bit) for i in range(n_req)]) for bit in (1, 3, 2)]

    def total_tst(x):
        with jax.named_scope("sum_core"):
            x = x + swap_core(x)
        with jax.named_scope("sum_y"):
            a, b, c = [chips(x, bits, 0) for bits in (1, 3, 2)]
            x = (x + a) + (b + c)
        with jax.named_scope("sum_z_inner"):
            a, b, c = [chips(x, 0, bits) for bits in (1, 3, 2)]
            x = (x + a) + (b + c)
        with jax.named_scope("sum_z_outer"):
            x = x + chips(x, 0, n_z - 1)
        return x

    def hand_on(x):
        with jax.named_scope("back_core"):
            return jnp.where(far_core, x, swap_core(x))

    wide = lambda x: jnp.broadcast_to(x.astype(F32).reshape(-1, 1), (x.shape[0], LANES))
    line = lambda x: x.astype(F32).reshape(1, slots)
    packed = jnp.concatenate(
        [dual, line(tile_rows), line(tile_cols), *map(wide, (tile_counts, time_limit, limit_dual_start, restarts))], axis=0
    )

    big_t = struct(test_blocks, LANES)
    big_r = struct(req_blocks, LANES)
    small = struct(STAT_ROWS, LANES)
    pull_shape = struct(test_blocks + STAT_ROWS, LANES)
    load_shape = struct(req_blocks + STAT_ROWS, LANES)
    rest = slots // GROUP - KEPT
    scratch = [pltpu.VMEM((rest, GROUP, LANES, LANES), BF16), pltpu.SemaphoreType.DMA((rest,))]

    def specs(given):
        return [HBM if x is coverage_tiles else VMEM for x in given]

    sq_list, scal_list = [], []
    sum_primal = sum_dual = ()
    for iteration in range(ITERS):
        if iteration == 0:
            given = (coverage_tiles, packed)
            pull, pick_rows, place_rows, pick_cols, place_cols, params, scal, *tiles = call(
                first_pull_kernel,
                (
                    pull_shape, struct(slots, req_blocks, dtype=BF16), struct(req_blocks, slots),
                    struct(slots, slots, dtype=BF16), struct(test_blocks, slots), small, small,
                    *[struct(GROUP, LANES, LANES, dtype=BF16)] * KEPT,
                ),
                specs(given),
                [scratch[0], pltpu.SemaphoreType.DMA((slots // GROUP,))],
            )(*given)
        else:
            given = (summed, params, pick_rows, place_cols, dual, scal, want, coverage_tiles, *tiles, *sum_dual)
            pull, dual, total, scal = call(
                functools.partial(dual_pull_kernel, iteration - 1, inverse_tests),
                (pull_shape, big_r, big_r, small), specs(given), scratch,
            )(*given)
            sum_dual = (total,)
            scal_list.append(scal)
        with jax.named_scope("sum_req"):
            parts = [pull, *on_req(pull)]
        given = (*parts, params, pick_cols, place_rows, primal, scal, costs, runs, coverage_tiles, *tiles, *sum_primal)
        load, primal, total, sq = call(
            functools.partial(primal_load_kernel, iteration), (load_shape, big_t, big_t, small), specs(given), scratch
        )(*given)
        sum_primal = (total,)
        if iteration > 0:
            sq_list.append(sq)
        summed = total_tst(load)
        if iteration < ITERS - 1:
            summed = hand_on(summed)
    dual, scal, sq = call(
        functools.partial(dual_last_kernel, ITERS - 1, inverse_tests), (big_r, small, small), [VMEM] * 6
    )(summed, params, dual, scal, want, *sum_dual)
    scal_list.append(scal)
    with jax.named_scope("sum_req_last"):
        moves = [lambda y, z, c, r, bit=bit: (y, z, c, r ^ bit) if c == 1 else (y ^ 1, z, c, r) for bit in (1, 3, 2)]
        last = [sq, *[on_mesh(sq, move) for move in moves]]
    norms = call(norms_kernel, struct(2, ITERS), [VMEM] * 9)(*sq_list, *last, *scal_list)
    state = hand_on(jnp.concatenate([dual, scal], axis=0))
    return primal.reshape(-1), state[:req_blocks].reshape(-1), state[req_blocks, :1], hand_on(norms).T


def solution(mesh):
    n_y = 4
    n_z = mesh.shape["tst"] // (2 * n_y)
    return jax.shard_map(
        functools.partial(per_device, n_y, n_z),
        mesh=mesh,
        in_specs=(
            P(("tst", "req"), None, None),
            P(("tst", "req")),
            P(("tst", "req")),
            P(("tst", "req")),
            P("tst"),
            P("tst"),
            P(),
            P("req"),
            P("tst"),
            P("req"),
            P(),
            P(),
        ),
        out_specs=(P("tst"), P("req"), P(), P()),
        check_vma=False,
    )
```

```python
import functools

import jax
import jax.numpy as jnp
from jax import lax
from jax.experimental import pallas as pl
from jax.experimental.pallas import tpu as pltpu
from jax.sharding import PartitionSpec as P

ITERS = 3
LANES = 128
STAT_ROWS = 8
GROUP = 16
KEPT = 6
PIECES = 4

step_primal = 0.6
step_dual = 0.6

VMEM = pl.BlockSpec(memory_space=pltpu.VMEM)
HBM = pl.BlockSpec(memory_space=pltpu.HBM)
F32 = jnp.float32
BF16 = jnp.bfloat16


def struct(*shape, dtype=F32):
    return jax.ShapeDtypeStruct(shape, dtype)


def stat_rows(*given):
    return jnp.concatenate([*given, jnp.zeros((STAT_ROWS - len(given), LANES), F32)], axis=0)


def sum_four(parts, rows):
    a, b, c, d = [part[rows, :] for part in parts]
    return (a + b) + (c + d)


def slot_count(params, iteration):
    seen = jnp.ones((1, LANES), F32)
    for earlier in range(iteration):
        seen = jnp.where(params[1 + earlier : 2 + earlier, :] == 1.0, 1.0, seen + 1.0)
    return seen


def average(params, iteration, total, new):
    restart_now = params[1 + iteration : 2 + iteration, :] == 1.0
    return (
        jnp.where(restart_now, total / slot_count(params, iteration), new),
        jnp.where(restart_now, 0.0, total),
    )


def spread(picked, group):
    rows = picked[group * GROUP : (group + 1) * GROUP, :]
    row_ids = lax.broadcasted_iota(jnp.int32, rows.shape, 0)
    return jnp.concatenate(
        [jnp.where(row_ids == offset, rows, 0.0) for offset in range(GROUP)], axis=1
    ).astype(BF16)


def gather_rows(pick, source):
    return jnp.dot(pick, source.astype(BF16), preferred_element_type=F32)


def scatter_sum(place, contrib):
    return jnp.dot(place, contrib, preferred_element_type=F32, precision=lax.Precision.HIGHEST)


def pull_group(picked, tiles, group):
    block = tiles[group][...].reshape(GROUP * LANES, LANES)
    return jnp.dot(spread(picked, group), block, preferred_element_type=F32)


def load_group(picked, tiles, group):
    block = jnp.concatenate([tiles[group][offset] for offset in range(GROUP)], axis=1)
    return lax.dot_general(
        spread(picked, group), block, (((1,), (1,)), ((), ())), preferred_element_type=F32
    )


def list_of(fetched):
    return [fetched.at[n] for n in range(fetched.shape[0])]


def fetch(tiles_in, fetched, sems):
    copies = []
    size = GROUP // PIECES
    for n in range(fetched.shape[0]):
        for piece in range(PIECES):
            part = tiles_in.at[pl.ds((KEPT + n) * GROUP + piece * size, size)]
            target = fetched.at[n, pl.ds(piece * size, size)]
            copies.append(pltpu.make_async_copy(part, target, sems.at[n * PIECES + piece]))
            copies[-1].start()
    return copies


def first_pull_kernel(
    tiles_in, dual_in, rows_in, cols_in, live_in, pull_out, pick_rows, place_rows, pick_cols, place_cols, *refs
):
    slots = tiles_in.shape[0]
    groups = slots // GROUP
    kept, (fetched, dual, rows, cols, live, sems, tile_sems) = refs[:KEPT], refs[KEPT:]
    tiles = [*kept, *list_of(fetched)]
    small = []
    for n, (source, target) in enumerate(((rows_in, rows), (cols_in, cols), (live_in, live), (dual_in, dual))):
        small.append(pltpu.make_async_copy(source, target, sems.at[n]))
        small[-1].start()
    chunks = []
    for n in range(groups):
        chunks.append(pltpu.make_async_copy(tiles_in.at[pl.ds(n * GROUP, GROUP)], tiles[n], tile_sems.at[n]))
        chunks[-1].start()
    for copy in small:
        copy.wait()
    req_blocks = dual.shape[0]
    test_blocks = pull_out.shape[0] - STAT_ROWS
    alive = lax.broadcasted_iota(jnp.int32, (1, slots), 1) < live[...]
    at_row = lax.broadcasted_iota(jnp.int32, (req_blocks, slots), 0) == rows[...]
    at_col = lax.broadcasted_iota(jnp.int32, (test_blocks, slots), 0) == cols[...]
    one_row = jnp.where(at_row, 1.0, 0.0)
    one_col = jnp.where(at_col, 1.0, 0.0)
    place_rows[...] = jnp.where(alive, one_row, 0.0)
    place_cols[...] = jnp.where(alive, one_col, 0.0)
    pick = one_row.T.astype(BF16)
    pick_rows[...] = pick
    pick_cols[...] = jnp.concatenate([one_col, jnp.zeros((slots - test_blocks, slots), F32)], axis=0).T.astype(BF16)
    picked = gather_rows(pick, dual[...])
    contrib = []
    for group in range(groups):
        chunks[group].wait()
        contrib.append(pull_group(picked, tiles, group))
    pull_out[:test_blocks, :] = scatter_sum(place_cols[...], jnp.concatenate(contrib, axis=0))
    pull_out[test_blocks:, :] = jnp.zeros((STAT_ROWS, LANES), F32)


def update_dual(iteration, inverse_tests, summed, params, dual, sum_dual, scal, demand):
    req_blocks = dual.shape[0]
    load = summed[:req_blocks, :]
    stats = summed[req_blocks:, :]
    spent = jnp.sum(stats[0:1, :], axis=1, keepdims=True) * inverse_tests
    bdual = scal[0:1, :]
    bdual_new = jnp.maximum(bdual + step_dual * (spent - params[0:1, :]), 0.0)
    old = dual[...]
    new = jnp.maximum(old + step_dual * (demand[...] - load), 0.0)
    dual_sq = jnp.sum((new - old) ** 2, axis=0, keepdims=True)
    total = new if sum_dual is None else sum_dual[...] + new
    dual_next, total_next = average(params, iteration, total, new)
    bdual_next, bdual_total = average(params, iteration, scal[1:2, :] + bdual_new, bdual_new)
    scal_next = stat_rows(bdual_next, bdual_total, (bdual_new - bdual) ** 2, stats[1:2, :])
    return dual_next, total_next, scal_next, dual_sq


def dual_pull_kernel(iteration, inverse_tests, *refs):
    summed, params, pick_rows, place_cols, dual, scal, demand, *refs = refs
    tiles_in, kept, refs = refs[0], refs[1 : 1 + KEPT], refs[1 + KEPT :]
    sum_dual = refs.pop(0) if iteration > 0 else None
    pull_out, dual_out, sum_out, scal_out, fetched, sems = refs
    copies = fetch(tiles_in, fetched, sems)
    dual_next, total_next, scal_next, dual_sq = update_dual(
        iteration, inverse_tests, summed, params, dual, sum_dual, scal, demand
    )
    dual_out[...] = dual_next
    sum_out[...] = total_next
    scal_out[...] = scal_next
    picked = gather_rows(pick_rows[...], dual_next)
    contrib = [pull_group(picked, kept, group) for group in range(KEPT)]
    for copy in copies:
        copy.wait()
    contrib += [pull_group(picked, [None] * KEPT + list_of(fetched), group) for group in range(KEPT, tiles_in.shape[0] // GROUP)]
    test_blocks = pull_out.shape[0] - STAT_ROWS
    pull_out[:test_blocks, :] = scatter_sum(place_cols[...], jnp.concatenate(contrib, axis=0))
    pull_out[test_blocks:, :] = stat_rows(dual_sq)


def dual_last_kernel(
    iteration, inverse_tests, summed, params, dual, scal, demand, sum_dual, dual_out, scal_out, sq_out
):
    dual_next, _, scal_next, dual_sq = update_dual(
        iteration, inverse_tests, summed, params, dual, sum_dual, scal, demand
    )
    dual_out[...] = dual_next
    scal_out[...] = scal_next
    sq_out[...] = stat_rows(dual_sq)


def primal_load_kernel(iteration, *refs):
    pull_own, pull_1, pull_2, pull_3, params, pick_cols, place_rows, primal, scal, costs, runtimes, *refs = refs
    slots = pick_cols.shape[0]
    tiles_in, kept, refs = refs[0], refs[1 : 1 + KEPT], refs[1 + KEPT :]
    sum_primal = refs.pop(0) if iteration > 0 else None
    load_out, primal_out, sum_out, sq_out, fetched, sems = refs
    copies = fetch(tiles_in, fetched, sems)
    test_blocks = primal.shape[0]
    parts = (pull_own, pull_1, pull_2, pull_3)
    pull = sum_four(parts, slice(0, test_blocks))
    sq_out[...] = sum_four(parts, slice(test_blocks, test_blocks + STAT_ROWS))
    old = primal[...]
    new = jnp.clip(old - step_primal * (costs[...] - pull + scal[0:1, :] * runtimes[...]), 0.0, 1.0)
    extrap = (2.0 * new - old).astype(BF16).astype(F32)
    total = new if sum_primal is None else sum_primal[...] + new
    primal_next, total_next = average(params, iteration, total, new)
    primal_out[...] = primal_next
    sum_out[...] = total_next
    padded = jnp.concatenate([extrap, jnp.zeros((slots - test_blocks, LANES), F32)], axis=0)
    picked = gather_rows(pick_cols[...], padded)
    contrib = [load_group(picked, kept, group) for group in range(KEPT)]
    for copy in copies:
        copy.wait()
    contrib += [load_group(picked, [None] * KEPT + list_of(fetched), group) for group in range(KEPT, slots // GROUP)]
    req_blocks = load_out.shape[0] - STAT_ROWS
    load_out[:req_blocks, :] = scatter_sum(place_rows[...], jnp.concatenate(contrib, axis=0))
    load_out[req_blocks:, :] = stat_rows(
        jnp.sum(runtimes[...] * extrap, axis=0, keepdims=True),
        jnp.sum((new - old) ** 2, axis=0, keepdims=True),
    )


def norms_kernel(sq_0, sq_1, last_0, last_1, last_2, last_3, scal_0, scal_1, scal_2, norms_out):
    row_ids = lax.broadcasted_iota(jnp.int32, norms_out.shape, 0)
    col_ids = lax.broadcasted_iota(jnp.int32, norms_out.shape, 1)
    last = sum_four((last_0, last_1, last_2, last_3), slice(0, 1))
    out = jnp.zeros(norms_out.shape, F32)
    for k, (sq, scal) in enumerate(((sq_0[0:1, :], scal_0), (sq_1[0:1, :], scal_1), (last, scal_2))):
        move_dual = jnp.sum(sq, axis=1, keepdims=True) + scal[2:3, 0:1]
        move_primal = jnp.sum(scal[3:4, :], axis=1, keepdims=True)
        out = jnp.where(col_ids == k, jnp.where(row_ids == 0, move_primal, move_dual), out)
    norms_out[...] = out


def results_kernel(params, state_own, state_other, norms_own, norms_other, dual_out, limit_out, norms_out):
    mine = params[1 + ITERS : 2 + ITERS, :] == 1.0
    req_blocks = dual_out.shape[0]
    dual_out[...] = jnp.where(mine, state_own[:req_blocks, :], state_other[:req_blocks, :])
    limit_out[...] = jnp.where(mine, state_own[req_blocks : req_blocks + 1, :], state_other[req_blocks : req_blocks + 1, :])[:, :1]
    norms_out[...] = jnp.where(mine[:, :ITERS], norms_own[...], norms_other[...])


def call(body, outs, specs, scratch=()):
    return pl.pallas_call(
        body,
        out_shape=outs,
        in_specs=specs,
        out_specs=jax.tree.map(lambda _: VMEM, outs),
        scratch_shapes=list(scratch),
        compiler_params=pltpu.CompilerParams(vmem_limit_bytes=50 * 1024 * 1024),
    )


def per_device(
    n_y, n_z,
    coverage_tiles, tile_rows, tile_cols, tile_counts, test_costs, runtimes, time_limit, demand,
    primal_start, dual_start, limit_dual_start, restarts,
):
    slots = coverage_tiles.shape[0]
    test_blocks = test_costs.shape[0] // LANES
    req_blocks = demand.shape[0] // LANES
    inverse_tests = 1.0 / (test_costs.shape[0] * lax.axis_size("tst"))
    costs = test_costs.reshape(test_blocks, LANES)
    runs = runtimes.reshape(test_blocks, LANES)
    want = demand.reshape(req_blocks, LANES)
    primal = primal_start.reshape(test_blocks, LANES)
    dual = dual_start.reshape(req_blocks, LANES)

    far_core = lax.axis_index("tst") % 2 == 1

    n_req = lax.axis_size("req")

    def on_mesh(x, move):
        pairs = []
        for y in range(n_y):
            for z in range(n_z):
                for c in range(2):
                    for r in range(n_req):
                        to_y, to_z, to_c, to_r = move(y, z, c, r)
                        source = ((y * n_z + z) * 2 + c) * n_req + r
                        pairs.append((source, ((to_y * n_z + to_z) * 2 + to_c) * n_req + to_r))
        return lax.ppermute(x, ("tst", "req"), pairs)

    def swap_core(x):
        return on_mesh(x, lambda y, z, c, r: (y, z, 1 - c, r))

    def chips(x, y_bits, z_bits):
        return on_mesh(x, lambda y, z, c, r: (y ^ y_bits, z ^ z_bits, c, r) if c == 1 else (y, z, c, r ^ 1))

    def on_req(x):
        return [lax.ppermute(x, "req", [(i, i ^ bit) for i in range(n_req)]) for bit in (1, 3, 2)]

    def total_tst(x):
        with jax.named_scope("sum_core"):
            x = x + swap_core(x)
        with jax.named_scope("sum_y"):
            a, b, c = [chips(x, bits, 0) for bits in (1, 3, 2)]
            x = (x + a) + (b + c)
        with jax.named_scope("sum_z_inner"):
            a, b, c = [chips(x, 0, bits) for bits in (1, 3, 2)]
            x = (x + a) + (b + c)
        with jax.named_scope("sum_z_outer"):
            x = x + chips(x, 0, n_z - 2)
        return x

    def hand_on(x):
        with jax.named_scope("back_core"):
            return jnp.where(far_core, x, swap_core(x))

    wide = lambda x: jnp.broadcast_to(x.astype(F32).reshape(-1, 1), (x.shape[0], LANES))
    params = jnp.concatenate(
        [wide(time_limit), wide(restarts), wide(far_core.reshape(1)), jnp.zeros((STAT_ROWS - 2 - ITERS, LANES), F32)], axis=0
    )
    scal = jnp.concatenate([wide(limit_dual_start), jnp.zeros((STAT_ROWS - 1, LANES), F32)], axis=0)
    big_t = struct(test_blocks, LANES)
    big_r = struct(req_blocks, LANES)
    small = struct(STAT_ROWS, LANES)
    pull_shape = struct(test_blocks + STAT_ROWS, LANES)
    load_shape = struct(req_blocks + STAT_ROWS, LANES)
    rest = slots // GROUP - KEPT
    scratch = [pltpu.VMEM((rest, GROUP, LANES, LANES), BF16), pltpu.SemaphoreType.DMA((rest * PIECES,))]

    def specs(given):
        return [HBM if x is coverage_tiles else VMEM for x in given]

    sq_list, scal_list = [], []
    sum_primal = sum_dual = ()
    for iteration in range(ITERS):
        if iteration == 0:
            given = (
                coverage_tiles, dual, tile_rows.reshape(1, slots), tile_cols.reshape(1, slots), tile_counts.reshape(1, 1)
            )
            pull, pick_rows, place_rows, pick_cols, place_cols, *tiles = call(
                first_pull_kernel,
                (
                    pull_shape, struct(slots, req_blocks, dtype=BF16), struct(req_blocks, slots),
                    struct(slots, slots, dtype=BF16), struct(test_blocks, slots),
                    *[struct(GROUP, LANES, LANES, dtype=BF16)] * KEPT,
                ),
                [HBM] * len(given),
                [scratch[0], *[pltpu.VMEM(x.shape, x.dtype) for x in given[1:]]]
                + [pltpu.SemaphoreType.DMA((n,)) for n in (len(given) - 1, slots // GROUP)],
            )(*given)
        else:
            given = (summed, params, pick_rows, place_cols, dual, scal, want, coverage_tiles, *tiles, *sum_dual)
            pull, dual, total, scal = call(
                functools.partial(dual_pull_kernel, iteration - 1, inverse_tests),
                (pull_shape, big_r, big_r, small), specs(given), scratch,
            )(*given)
            sum_dual = (total,)
            scal_list.append(scal)
        with jax.named_scope("sum_req"):
            parts = [pull, *on_req(pull)]
        given = (*parts, params, pick_cols, place_rows, primal, scal, costs, runs, coverage_tiles, *tiles, *sum_primal)
        load, primal, total, sq = call(
            functools.partial(primal_load_kernel, iteration), (load_shape, big_t, big_t, small), specs(given), scratch
        )(*given)
        sum_primal = (total,)
        if iteration > 0:
            sq_list.append(sq)
        summed = total_tst(load)
        if iteration < ITERS - 1:
            summed = hand_on(summed)
    dual, scal, sq = call(
        functools.partial(dual_last_kernel, ITERS - 1, inverse_tests), (big_r, small, small), [VMEM] * 6
    )(summed, params, dual, scal, want, *sum_dual)
    scal_list.append(scal)
    with jax.named_scope("sum_req_last"):
        moves = [lambda y, z, c, r, bit=bit: (y, z, c, r ^ bit) if c == 1 else (y ^ 1, z, c, r) for bit in (1, 3, 2)]
        last = [sq, *[on_mesh(sq, move) for move in moves]]
    norms = call(norms_kernel, struct(2, ITERS), [VMEM] * 9)(*sq_list, *last, *scal_list)
    state = jnp.concatenate([dual, scal], axis=0)
    with jax.named_scope("back_core"):
        other = swap_core(state), swap_core(norms)
    dual, limit, norms = call(results_kernel, (big_r, struct(1, 1), struct(2, ITERS)), [VMEM] * 5)(
        params, state, other[0], norms, other[1]
    )
    return primal.reshape(-1), dual.reshape(-1), limit.reshape(1), norms.T


def solution(mesh):
    n_y = 4
    n_z = mesh.shape["tst"] // (2 * n_y)
    return jax.shard_map(
        functools.partial(per_device, n_y, n_z),
        mesh=mesh,
        in_specs=(
            P(("tst", "req"), None, None),
            P(("tst", "req")),
            P(("tst", "req")),
            P(("tst", "req")),
            P("tst"),
            P("tst"),
            P(),
            P("req"),
            P("tst"),
            P("req"),
            P(),
            P(),
        ),
        out_specs=(P("tst"), P("req"), P(), P()),
        check_vma=False,
    )
```

```python
import functools

import jax
import jax.numpy as jnp
from jax import lax
from jax.experimental import pallas as pl
from jax.experimental.pallas import tpu as pltpu
from jax.sharding import PartitionSpec as P

ITERS = 3
LANES = 128
STAT_ROWS = 8
GROUP = 16
KEPT = 6

step_primal = 0.6
step_dual = 0.6

VMEM = pl.BlockSpec(memory_space=pltpu.VMEM)
HBM = pl.BlockSpec(memory_space=pltpu.HBM)
F32 = jnp.float32
BF16 = jnp.bfloat16


def struct(*shape, dtype=F32):
    return jax.ShapeDtypeStruct(shape, dtype)


def stat_rows(*given):
    return jnp.concatenate([*given, jnp.zeros((STAT_ROWS - len(given), LANES), F32)], axis=0)


def sum_four(parts, rows):
    a, b, c, d = [part[rows, :] for part in parts]
    return (a + b) + (c + d)


def slot_count(params, iteration):
    seen = jnp.ones((1, LANES), F32)
    for earlier in range(iteration):
        seen = jnp.where(params[1 + earlier : 2 + earlier, :] == 1.0, 1.0, seen + 1.0)
    return seen


def average(params, iteration, total, new):
    restart_now = params[1 + iteration : 2 + iteration, :] == 1.0
    return (
        jnp.where(restart_now, total / slot_count(params, iteration), new),
        jnp.where(restart_now, 0.0, total),
    )


def spread(picked, group):
    rows = picked[group * GROUP : (group + 1) * GROUP, :]
    row_ids = lax.broadcasted_iota(jnp.int32, rows.shape, 0)
    return jnp.concatenate(
        [jnp.where(row_ids == offset, rows, 0.0) for offset in range(GROUP)], axis=1
    ).astype(BF16)


def gather_rows(pick, source):
    return jnp.dot(pick, source.astype(BF16), preferred_element_type=F32)


def scatter_sum(place, contrib):
    return jnp.dot(place, contrib, preferred_element_type=F32, precision=lax.Precision.HIGHEST)


def pull_group(picked, tiles, group):
    block = tiles[group][...].reshape(GROUP * LANES, LANES)
    return jnp.dot(spread(picked, group), block, preferred_element_type=F32)


def load_group(picked, tiles, group):
    block = jnp.concatenate([tiles[group][offset] for offset in range(GROUP)], axis=1)
    return lax.dot_general(
        spread(picked, group), block, (((1,), (1,)), ((), ())), preferred_element_type=F32
    )


def list_of(fetched):
    return [fetched.at[n] for n in range(fetched.shape[0])]


def rest_kernel(tiles_in, after, *refs):
    kept, sems = refs[:-1], refs[-1]
    copies = []
    for n, target in enumerate(kept):
        part = tiles_in.at[pl.ds((KEPT + n) * GROUP, GROUP)]
        copies.append(pltpu.make_async_copy(part, target, sems.at[n]))
        copies[-1].start()
    for copy in copies:
        copy.wait()


def first_pull_kernel(
    tiles_in, dual_in, rows_in, cols_in, live_in, pull_out, pick_rows, place_rows, pick_cols, place_cols, *refs
):
    slots = tiles_in.shape[0]
    groups = slots // GROUP
    kept, (fetched, dual, rows, cols, live, sems, tile_sems) = refs[:KEPT], refs[KEPT:]
    tiles = [*kept, *list_of(fetched)]
    small = []
    for n, (source, target) in enumerate(((rows_in, rows), (cols_in, cols), (live_in, live), (dual_in, dual))):
        small.append(pltpu.make_async_copy(source, target, sems.at[n]))
        small[-1].start()
    chunks = []
    for n in range(groups):
        chunks.append(pltpu.make_async_copy(tiles_in.at[pl.ds(n * GROUP, GROUP)], tiles[n], tile_sems.at[n]))
        chunks[-1].start()
    for copy in small:
        copy.wait()
    req_blocks = dual.shape[0]
    test_blocks = pull_out.shape[0] - STAT_ROWS
    alive = lax.broadcasted_iota(jnp.int32, (1, slots), 1) < live[...]
    at_row = lax.broadcasted_iota(jnp.int32, (req_blocks, slots), 0) == rows[...]
    at_col = lax.broadcasted_iota(jnp.int32, (test_blocks, slots), 0) == cols[...]
    one_row = jnp.where(at_row, 1.0, 0.0)
    one_col = jnp.where(at_col, 1.0, 0.0)
    place_rows[...] = jnp.where(alive, one_row, 0.0)
    place_cols[...] = jnp.where(alive, one_col, 0.0)
    pick = one_row.T.astype(BF16)
    pick_rows[...] = pick
    pick_cols[...] = jnp.concatenate([one_col, jnp.zeros((slots - test_blocks, slots), F32)], axis=0).T.astype(BF16)
    picked = gather_rows(pick, dual[...])
    contrib = []
    for group in range(groups):
        chunks[group].wait()
        contrib.append(pull_group(picked, tiles, group))
    pull_out[:test_blocks, :] = scatter_sum(place_cols[...], jnp.concatenate(contrib, axis=0))
    pull_out[test_blocks:, :] = jnp.zeros((STAT_ROWS, LANES), F32)


def update_dual(iteration, inverse_tests, summed, params, dual, sum_dual, scal, demand):
    req_blocks = dual.shape[0]
    load = summed[:req_blocks, :]
    stats = summed[req_blocks:, :]
    spent = jnp.sum(stats[0:1, :], axis=1, keepdims=True) * inverse_tests
    bdual = scal[0:1, :]
    bdual_new = jnp.maximum(bdual + step_dual * (spent - params[0:1, :]), 0.0)
    old = dual[...]
    new = jnp.maximum(old + step_dual * (demand[...] - load), 0.0)
    dual_sq = jnp.sum((new - old) ** 2, axis=0, keepdims=True)
    total = new if sum_dual is None else sum_dual[...] + new
    dual_next, total_next = average(params, iteration, total, new)
    bdual_next, bdual_total = average(params, iteration, scal[1:2, :] + bdual_new, bdual_new)
    scal_next = stat_rows(bdual_next, bdual_total, (bdual_new - bdual) ** 2, stats[1:2, :])
    return dual_next, total_next, scal_next, dual_sq


def dual_pull_kernel(iteration, inverse_tests, *refs):
    summed, params, pick_rows, place_cols, dual, scal, demand, *refs = refs
    groups = pick_rows.shape[0] // GROUP
    tiles, refs = refs[:groups], refs[groups:]
    sum_dual = refs.pop(0) if iteration > 0 else None
    pull_out, dual_out, sum_out, scal_out = refs
    dual_next, total_next, scal_next, dual_sq = update_dual(
        iteration, inverse_tests, summed, params, dual, sum_dual, scal, demand
    )
    dual_out[...] = dual_next
    sum_out[...] = total_next
    scal_out[...] = scal_next
    picked = gather_rows(pick_rows[...], dual_next)
    contrib = [pull_group(picked, tiles, group) for group in range(groups)]
    test_blocks = pull_out.shape[0] - STAT_ROWS
    pull_out[:test_blocks, :] = scatter_sum(place_cols[...], jnp.concatenate(contrib, axis=0))
    pull_out[test_blocks:, :] = stat_rows(dual_sq)


def dual_last_kernel(
    iteration, inverse_tests, summed, params, dual, scal, demand, sum_dual, dual_out, scal_out, sq_out
):
    dual_next, _, scal_next, dual_sq = update_dual(
        iteration, inverse_tests, summed, params, dual, sum_dual, scal, demand
    )
    dual_out[...] = dual_next
    scal_out[...] = scal_next
    sq_out[...] = stat_rows(dual_sq)


def primal_load_kernel(iteration, *refs):
    pull_own, pull_1, pull_2, pull_3, params, pick_cols, place_rows, primal, scal, costs, runtimes, *refs = refs
    slots = pick_cols.shape[0]
    groups = slots // GROUP
    tiles, refs = refs[:groups], refs[groups:]
    sum_primal = refs.pop(0) if iteration > 0 else None
    load_out, primal_out, sum_out, sq_out = refs
    test_blocks = primal.shape[0]
    parts = (pull_own, pull_1, pull_2, pull_3)
    pull = sum_four(parts, slice(0, test_blocks))
    sq_out[...] = sum_four(parts, slice(test_blocks, test_blocks + STAT_ROWS))
    old = primal[...]
    new = jnp.clip(old - step_primal * (costs[...] - pull + scal[0:1, :] * runtimes[...]), 0.0, 1.0)
    extrap = (2.0 * new - old).astype(BF16).astype(F32)
    total = new if sum_primal is None else sum_primal[...] + new
    primal_next, total_next = average(params, iteration, total, new)
    primal_out[...] = primal_next
    sum_out[...] = total_next
    padded = jnp.concatenate([extrap, jnp.zeros((slots - test_blocks, LANES), F32)], axis=0)
    picked = gather_rows(pick_cols[...], padded)
    contrib = [load_group(picked, tiles, group) for group in range(groups)]
    req_blocks = load_out.shape[0] - STAT_ROWS
    load_out[:req_blocks, :] = scatter_sum(place_rows[...], jnp.concatenate(contrib, axis=0))
    load_out[req_blocks:, :] = stat_rows(
        jnp.sum(runtimes[...] * extrap, axis=0, keepdims=True),
        jnp.sum((new - old) ** 2, axis=0, keepdims=True),
    )


def norms_kernel(sq_0, sq_1, last_0, last_1, last_2, last_3, scal_0, scal_1, scal_2, norms_out):
    row_ids = lax.broadcasted_iota(jnp.int32, norms_out.shape, 0)
    col_ids = lax.broadcasted_iota(jnp.int32, norms_out.shape, 1)
    last = sum_four((last_0, last_1, last_2, last_3), slice(0, 1))
    out = jnp.zeros(norms_out.shape, F32)
    for k, (sq, scal) in enumerate(((sq_0[0:1, :], scal_0), (sq_1[0:1, :], scal_1), (last, scal_2))):
        move_dual = jnp.sum(sq, axis=1, keepdims=True) + scal[2:3, 0:1]
        move_primal = jnp.sum(scal[3:4, :], axis=1, keepdims=True)
        out = jnp.where(col_ids == k, jnp.where(row_ids == 0, move_primal, move_dual), out)
    norms_out[...] = out


def results_kernel(params, state_own, state_other, norms_own, norms_other, dual_out, limit_out, norms_out):
    mine = params[1 + ITERS : 2 + ITERS, :] == 1.0
    req_blocks = dual_out.shape[0]
    dual_out[...] = jnp.where(mine, state_own[:req_blocks, :], state_other[:req_blocks, :])
    limit_out[...] = jnp.where(mine, state_own[req_blocks : req_blocks + 1, :], state_other[req_blocks : req_blocks + 1, :])[:, :1]
    norms_out[...] = jnp.where(mine[:, :ITERS], norms_own[...], norms_other[...])


def call(body, outs, specs, scratch=()):
    return pl.pallas_call(
        body,
        out_shape=outs,
        in_specs=specs,
        out_specs=jax.tree.map(lambda _: VMEM, outs),
        scratch_shapes=list(scratch),
        compiler_params=pltpu.CompilerParams(vmem_limit_bytes=(50 if HBM in specs else 16) * 1024 * 1024),
    )


def per_device(
    n_y, n_z,
    coverage_tiles, tile_rows, tile_cols, tile_counts, test_costs, runtimes, time_limit, demand,
    primal_start, dual_start, limit_dual_start, restarts,
):
    slots = coverage_tiles.shape[0]
    test_blocks = test_costs.shape[0] // LANES
    req_blocks = demand.shape[0] // LANES
    inverse_tests = 1.0 / (test_costs.shape[0] * lax.axis_size("tst"))
    costs = test_costs.reshape(test_blocks, LANES)
    runs = runtimes.reshape(test_blocks, LANES)
    want = demand.reshape(req_blocks, LANES)
    primal = primal_start.reshape(test_blocks, LANES)
    dual = dual_start.reshape(req_blocks, LANES)

    far_core = lax.axis_index("tst") % 2 == 1

    n_req = lax.axis_size("req")

    def on_mesh(x, move):
        pairs = []
        for y in range(n_y):
            for z in range(n_z):
                for c in range(2):
                    for r in range(n_req):
                        to_y, to_z, to_c, to_r = move(y, z, c, r)
                        source = ((y * n_z + z) * 2 + c) * n_req + r
                        pairs.append((source, ((to_y * n_z + to_z) * 2 + to_c) * n_req + to_r))
        return lax.ppermute(x, ("tst", "req"), pairs)

    def swap_core(x):
        return on_mesh(x, lambda y, z, c, r: (y, z, 1 - c, r))

    def chips(x, y_bits, z_bits):
        return on_mesh(x, lambda y, z, c, r: (y ^ y_bits, z ^ z_bits, c, r) if c == 1 else (y, z, c, r ^ 1))

    def on_req(x):
        return [lax.ppermute(x, "req", [(i, i ^ bit) for i in range(n_req)]) for bit in (1, 3, 2)]

    def total_tst(x):
        with jax.named_scope("sum_core"):
            x = x + swap_core(x)
        with jax.named_scope("sum_y"):
            a, b, c = [chips(x, bits, 0) for bits in (1, 3, 2)]
            x = (x + a) + (b + c)
        with jax.named_scope("sum_z_inner"):
            a, b, c = [chips(x, 0, bits) for bits in (1, 3, 2)]
            x = (x + a) + (b + c)
        with jax.named_scope("sum_z_outer"):
            x = x + chips(x, 0, n_z - 2)
        return x

    def hand_on(x):
        with jax.named_scope("back_core"):
            return jnp.where(far_core, x, swap_core(x))

    wide = lambda x: jnp.broadcast_to(x.astype(F32).reshape(-1, 1), (x.shape[0], LANES))
    params = jnp.concatenate(
        [wide(time_limit), wide(restarts), wide(far_core.reshape(1)), jnp.zeros((STAT_ROWS - 2 - ITERS, LANES), F32)], axis=0
    )
    scal = jnp.concatenate([wide(limit_dual_start), jnp.zeros((STAT_ROWS - 1, LANES), F32)], axis=0)
    big_t = struct(test_blocks, LANES)
    big_r = struct(req_blocks, LANES)
    small = struct(STAT_ROWS, LANES)
    pull_shape = struct(test_blocks + STAT_ROWS, LANES)
    load_shape = struct(req_blocks + STAT_ROWS, LANES)
    group_shape = struct(GROUP, LANES, LANES, dtype=BF16)
    rest = slots // GROUP - KEPT
    sq_list, scal_list = [], []
    sum_primal = sum_dual = ()
    for iteration in range(ITERS):
        if iteration == 0:
            given = (
                coverage_tiles, dual, tile_rows.reshape(1, slots), tile_cols.reshape(1, slots), tile_counts.reshape(1, 1)
            )
            pull, pick_rows, place_rows, pick_cols, place_cols, *tiles = call(
                first_pull_kernel,
                (
                    pull_shape, struct(slots, req_blocks, dtype=BF16), struct(req_blocks, slots),
                    struct(slots, slots, dtype=BF16), struct(test_blocks, slots),
                    *[group_shape] * KEPT,
                ),
                [HBM] * len(given),
                [pltpu.VMEM((rest, *group_shape.shape), BF16), *[pltpu.VMEM(x.shape, x.dtype) for x in given[1:]]]
                + [pltpu.SemaphoreType.DMA((n,)) for n in (len(given) - 1, slots // GROUP)],
            )(*given)
            tiles += call(
                rest_kernel, [group_shape] * rest, [HBM, VMEM], [pltpu.SemaphoreType.DMA((rest,))]
            )(coverage_tiles, pick_cols)
        else:
            given = (summed, params, pick_rows, place_cols, dual, scal, want, *tiles, *sum_dual)
            pull, dual, total, scal = call(
                functools.partial(dual_pull_kernel, iteration - 1, inverse_tests),
                (pull_shape, big_r, big_r, small), [VMEM] * len(given),
            )(*given)
            sum_dual = (total,)
            scal_list.append(scal)
        with jax.named_scope("sum_req"):
            parts = [pull, *on_req(pull)]
        given = (*parts, params, pick_cols, place_rows, primal, scal, costs, runs, *tiles, *sum_primal)
        load, primal, total, sq = call(
            functools.partial(primal_load_kernel, iteration), (load_shape, big_t, big_t, small), [VMEM] * len(given)
        )(*given)
        sum_primal = (total,)
        if iteration > 0:
            sq_list.append(sq)
        summed = total_tst(load)
        if iteration < ITERS - 1:
            summed = hand_on(summed)
    dual, scal, sq = call(
        functools.partial(dual_last_kernel, ITERS - 1, inverse_tests), (big_r, small, small), [VMEM] * 6
    )(summed, params, dual, scal, want, *sum_dual)
    scal_list.append(scal)
    with jax.named_scope("sum_req_last"):
        moves = [lambda y, z, c, r, bit=bit: (y, z, c, r ^ bit) if c == 1 else (y ^ 1, z, c, r) for bit in (1, 3, 2)]
        last = [sq, *[on_mesh(sq, move) for move in moves]]
    norms = call(norms_kernel, struct(2, ITERS), [VMEM] * 9)(*sq_list, *last, *scal_list)
    state = jnp.concatenate([dual, scal], axis=0)
    with jax.named_scope("back_core"):
        other = swap_core(state), swap_core(norms)
    dual, limit, norms = call(results_kernel, (big_r, struct(1, 1), struct(2, ITERS)), [VMEM] * 5)(
        params, state, other[0], norms, other[1]
    )
    return primal.reshape(-1), dual.reshape(-1), limit.reshape(1), norms.T


def solution(mesh):
    n_y = 4
    n_z = mesh.shape["tst"] // (2 * n_y)
    return jax.shard_map(
        functools.partial(per_device, n_y, n_z),
        mesh=mesh,
        in_specs=(
            P(("tst", "req"), None, None),
            P(("tst", "req")),
            P(("tst", "req")),
            P(("tst", "req")),
            P("tst"),
            P("tst"),
            P(),
            P("req"),
            P("tst"),
            P("req"),
            P(),
            P(),
        ),
        out_specs=(P("tst"), P("req"), P(), P()),
        check_vma=False,
    )
```

```python
import functools

import jax
import jax.numpy as jnp
from jax import lax
from jax.experimental import pallas as pl
from jax.experimental.pallas import tpu as pltpu
from jax.sharding import PartitionSpec as P

ITERS = 3
LANES = 128
STAT_ROWS = 8
GROUP = 16
KEPT = 6

step_primal = 0.6
step_dual = 0.6

VMEM = pl.BlockSpec(memory_space=pltpu.VMEM)
HBM = pl.BlockSpec(memory_space=pltpu.HBM)
F32 = jnp.float32
BF16 = jnp.bfloat16


def struct(*shape, dtype=F32):
    return jax.ShapeDtypeStruct(shape, dtype)


def stat_rows(*given):
    return jnp.concatenate([*given, jnp.zeros((STAT_ROWS - len(given), LANES), F32)], axis=0)


def sum_four(parts, rows):
    a, b, c, d = [part[rows, :] for part in parts]
    return (a + b) + (c + d)


def slot_count(params, iteration):
    seen = jnp.ones((1, LANES), F32)
    for earlier in range(iteration):
        seen = jnp.where(params[1 + earlier : 2 + earlier, :] == 1.0, 1.0, seen + 1.0)
    return seen


def average(params, iteration, total, new):
    restart_now = params[1 + iteration : 2 + iteration, :] == 1.0
    return (
        jnp.where(restart_now, total / slot_count(params, iteration), new),
        jnp.where(restart_now, 0.0, total),
    )


def spread(picked, group):
    rows = picked[group * GROUP : (group + 1) * GROUP, :]
    row_ids = lax.broadcasted_iota(jnp.int32, rows.shape, 0)
    return jnp.concatenate(
        [jnp.where(row_ids == offset, rows, 0.0) for offset in range(GROUP)], axis=1
    ).astype(BF16)


def gather_rows(pick, source):
    return jnp.dot(pick, source.astype(BF16), preferred_element_type=F32)


def scatter_sum(place, contrib):
    return jnp.dot(place, contrib, preferred_element_type=F32, precision=lax.Precision.HIGHEST)


def pull_group(picked, tiles, group):
    block = tiles[group][...].reshape(GROUP * LANES, LANES)
    return jnp.dot(spread(picked, group), block, preferred_element_type=F32)


def load_group(picked, tiles, group):
    block = jnp.concatenate([tiles[group][offset] for offset in range(GROUP)], axis=1)
    return lax.dot_general(
        spread(picked, group), block, (((1,), (1,)), ((), ())), preferred_element_type=F32
    )


def list_of(fetched):
    return [fetched.at[n] for n in range(fetched.shape[0])]


def rest_kernel(tiles_in, after, *refs):
    kept, sems = refs[:-1], refs[-1]
    copies = []
    for n, target in enumerate(kept):
        part = tiles_in.at[pl.ds((KEPT + n) * GROUP, GROUP)]
        copies.append(pltpu.make_async_copy(part, target, sems.at[n]))
        copies[-1].start()
    for copy in copies:
        copy.wait()


def first_pull_kernel(
    tiles_in, dual_in, rows_in, cols_in, live_in, pull_out, pick_rows, place_rows, pick_cols, place_cols, *refs
):
    slots = tiles_in.shape[0]
    groups = slots // GROUP
    kept, (fetched, dual, rows, cols, live, sems, tile_sems) = refs[:KEPT], refs[KEPT:]
    tiles = [*kept, *list_of(fetched)]
    small = []
    for n, (source, target) in enumerate(((rows_in, rows), (cols_in, cols), (live_in, live), (dual_in, dual))):
        small.append(pltpu.make_async_copy(source, target, sems.at[n]))
        small[-1].start()
    chunks = []
    for n in range(groups):
        chunks.append(pltpu.make_async_copy(tiles_in.at[pl.ds(n * GROUP, GROUP)], tiles[n], tile_sems.at[n]))
        chunks[-1].start()
    for copy in small:
        copy.wait()
    req_blocks = dual.shape[0]
    test_blocks = pull_out.shape[0] - STAT_ROWS
    alive = lax.broadcasted_iota(jnp.int32, (1, slots), 1) < live[...]
    at_row = lax.broadcasted_iota(jnp.int32, (req_blocks, slots), 0) == rows[...]
    at_col = lax.broadcasted_iota(jnp.int32, (test_blocks, slots), 0) == cols[...]
    one_row = jnp.where(at_row, 1.0, 0.0)
    one_col = jnp.where(at_col, 1.0, 0.0)
    place_rows[...] = jnp.where(alive, one_row, 0.0)
    place_cols[...] = jnp.where(alive, one_col, 0.0)
    pick = one_row.T.astype(BF16)
    pick_rows[...] = pick
    pick_cols[...] = jnp.concatenate([one_col, jnp.zeros((slots - test_blocks, slots), F32)], axis=0).T.astype(BF16)
    picked = gather_rows(pick, dual[...])
    contrib = []
    for group in range(groups):
        chunks[group].wait()
        contrib.append(pull_group(picked, tiles, group))
    pull_out[:test_blocks, :] = scatter_sum(place_cols[...], jnp.concatenate(contrib, axis=0))
    pull_out[test_blocks:, :] = jnp.zeros((STAT_ROWS, LANES), F32)


def update_dual(iteration, inverse_tests, summed, params, dual, sum_dual, scal, demand):
    req_blocks = dual.shape[0]
    load = summed[:req_blocks, :]
    stats = summed[req_blocks:, :]
    spent = jnp.sum(stats[0:1, :], axis=1, keepdims=True) * inverse_tests
    bdual = scal[0:1, :]
    bdual_new = jnp.maximum(bdual + step_dual * (spent - params[0:1, :]), 0.0)
    old = dual[...]
    new = jnp.maximum(old + step_dual * (demand[...] - load), 0.0)
    dual_sq = jnp.sum((new - old) ** 2, axis=0, keepdims=True)
    total = new if sum_dual is None else sum_dual[...] + new
    dual_next, total_next = average(params, iteration, total, new)
    bdual_next, bdual_total = average(params, iteration, scal[1:2, :] + bdual_new, bdual_new)
    scal_next = stat_rows(bdual_next, bdual_total, (bdual_new - bdual) ** 2, stats[1:2, :])
    return dual_next, total_next, scal_next, dual_sq


def dual_pull_kernel(iteration, inverse_tests, *refs):
    summed, params, pick_rows, place_cols, dual, scal, demand, *refs = refs
    groups = pick_rows.shape[0] // GROUP
    tiles, refs = refs[:groups], refs[groups:]
    sum_dual = refs.pop(0) if iteration > 0 else None
    pull_out, dual_out, sum_out, scal_out = refs
    dual_next, total_next, scal_next, dual_sq = update_dual(
        iteration, inverse_tests, summed, params, dual, sum_dual, scal, demand
    )
    dual_out[...] = dual_next
    sum_out[...] = total_next
    scal_out[...] = scal_next
    picked = gather_rows(pick_rows[...], dual_next)
    contrib = [pull_group(picked, tiles, group) for group in range(groups)]
    test_blocks = pull_out.shape[0] - STAT_ROWS
    pull_out[:test_blocks, :] = scatter_sum(place_cols[...], jnp.concatenate(contrib, axis=0))
    pull_out[test_blocks:, :] = stat_rows(dual_sq)


def dual_last_kernel(
    iteration, inverse_tests, summed, params, dual, scal, demand, sum_dual, dual_out, scal_out, sq_out
):
    dual_next, _, scal_next, dual_sq = update_dual(
        iteration, inverse_tests, summed, params, dual, sum_dual, scal, demand
    )
    dual_out[...] = dual_next
    scal_out[...] = scal_next
    sq_out[...] = stat_rows(dual_sq)


def primal_load_kernel(iteration, *refs):
    pull_own, pull_1, pull_2, pull_3, params, pick_cols, place_rows, primal, scal, costs, runtimes, *refs = refs
    slots = pick_cols.shape[0]
    groups = slots // GROUP
    tiles, refs = refs[:groups], refs[groups:]
    sum_primal = refs.pop(0) if iteration > 0 else None
    load_out, primal_out, *refs = refs
    sum_out = refs.pop(0) if iteration < ITERS - 1 else None
    sq_out = refs.pop(0) if iteration > 0 else None
    test_blocks = primal.shape[0]
    parts = (pull_own, pull_1, pull_2, pull_3)
    pull = sum_four(parts, slice(0, test_blocks))
    if sq_out is not None:
        sq_out[...] = sum_four(parts, slice(test_blocks, test_blocks + STAT_ROWS))
    old = primal[...]
    new = jnp.clip(old - step_primal * (costs[...] - pull + scal[0:1, :] * runtimes[...]), 0.0, 1.0)
    extrap = (2.0 * new - old).astype(BF16).astype(F32)
    total = new if sum_primal is None else sum_primal[...] + new
    primal_next, total_next = average(params, iteration, total, new)
    primal_out[...] = primal_next
    if sum_out is not None:
        sum_out[...] = total_next
    padded = jnp.concatenate([extrap, jnp.zeros((slots - test_blocks, LANES), F32)], axis=0)
    picked = gather_rows(pick_cols[...], padded)
    contrib = [load_group(picked, tiles, group) for group in range(groups)]
    req_blocks = load_out.shape[0] - STAT_ROWS
    load_out[:req_blocks, :] = scatter_sum(place_rows[...], jnp.concatenate(contrib, axis=0))
    load_out[req_blocks:, :] = stat_rows(
        jnp.sum(runtimes[...] * extrap, axis=0, keepdims=True),
        jnp.sum((new - old) ** 2, axis=0, keepdims=True),
    )


def norms_kernel(sq_0, sq_1, last_0, last_1, last_2, last_3, scal_0, scal_1, scal_2, norms_out):
    row_ids = lax.broadcasted_iota(jnp.int32, norms_out.shape, 0)
    col_ids = lax.broadcasted_iota(jnp.int32, norms_out.shape, 1)
    last = sum_four((last_0, last_1, last_2, last_3), slice(0, 1))
    out = jnp.zeros(norms_out.shape, F32)
    for k, (sq, scal) in enumerate(((sq_0[0:1, :], scal_0), (sq_1[0:1, :], scal_1), (last, scal_2))):
        move_dual = jnp.sum(sq, axis=1, keepdims=True) + scal[2:3, 0:1]
        move_primal = jnp.sum(scal[3:4, :], axis=1, keepdims=True)
        out = jnp.where(col_ids == k, jnp.where(row_ids == 0, move_primal, move_dual), out)
    norms_out[...] = out


def results_kernel(params, state_own, state_other, norms_own, norms_other, dual_out, limit_out, norms_out):
    mine = params[1 + ITERS : 2 + ITERS, :] == 1.0
    req_blocks = dual_out.shape[0]
    dual_out[...] = jnp.where(mine, state_own[:req_blocks, :], state_other[:req_blocks, :])
    limit_out[...] = jnp.where(mine, state_own[req_blocks : req_blocks + 1, :], state_other[req_blocks : req_blocks + 1, :])[:, :1]
    norms_out[...] = jnp.where(mine[:, :ITERS], norms_own[...], norms_other[...])


def call(body, outs, specs, scratch=()):
    return pl.pallas_call(
        body,
        out_shape=outs,
        in_specs=specs,
        out_specs=jax.tree.map(lambda _: VMEM, outs),
        scratch_shapes=list(scratch),
        compiler_params=pltpu.CompilerParams(vmem_limit_bytes=(50 if HBM in specs else 16) * 1024 * 1024),
    )


def per_device(
    n_y, n_z,
    coverage_tiles, tile_rows, tile_cols, tile_counts, test_costs, runtimes, time_limit, demand,
    primal_start, dual_start, limit_dual_start, restarts,
):
    slots = coverage_tiles.shape[0]
    test_blocks = test_costs.shape[0] // LANES
    req_blocks = demand.shape[0] // LANES
    inverse_tests = 1.0 / (test_costs.shape[0] * lax.axis_size("tst"))
    costs = test_costs.reshape(test_blocks, LANES)
    runs = runtimes.reshape(test_blocks, LANES)
    want = demand.reshape(req_blocks, LANES)
    primal = primal_start.reshape(test_blocks, LANES)
    dual = dual_start.reshape(req_blocks, LANES)

    far_core = lax.axis_index("tst") % 2 == 1

    n_req = lax.axis_size("req")

    def on_mesh(x, move):
        pairs = []
        for y in range(n_y):
            for z in range(n_z):
                for c in range(2):
                    for r in range(n_req):
                        to_y, to_z, to_c, to_r = move(y, z, c, r)
                        source = ((y * n_z + z) * 2 + c) * n_req + r
                        pairs.append((source, ((to_y * n_z + to_z) * 2 + to_c) * n_req + to_r))
        return lax.ppermute(x, ("tst", "req"), pairs)

    def swap_core(x):
        return on_mesh(x, lambda y, z, c, r: (y, z, 1 - c, r))

    def chips(x, y_bits, z_bits):
        return on_mesh(x, lambda y, z, c, r: (y ^ y_bits, z ^ z_bits, c, r) if c == 1 else (y, z, c, r ^ 1))

    def on_req(x):
        return [lax.ppermute(x, "req", [(i, i ^ bit) for i in range(n_req)]) for bit in (1, 3, 2)]

    def total_tst(x):
        with jax.named_scope("sum_core"):
            x = x + swap_core(x)
        with jax.named_scope("sum_y"):
            a, b, c = [chips(x, bits, 0) for bits in (1, 3, 2)]
            x = (x + a) + (b + c)
        with jax.named_scope("sum_z_inner"):
            a, b, c = [chips(x, 0, bits) for bits in (1, 3, 2)]
            x = (x + a) + (b + c)
        with jax.named_scope("sum_z_outer"):
            x = x + chips(x, 0, n_z - 2)
        return x

    def hand_on(x):
        with jax.named_scope("back_core"):
            return jnp.where(far_core, x, swap_core(x))

    wide = lambda x: jnp.broadcast_to(x.astype(F32).reshape(-1, 1), (x.shape[0], LANES))
    params = jnp.concatenate(
        [wide(time_limit), wide(restarts), wide(far_core.reshape(1)), jnp.zeros((STAT_ROWS - 2 - ITERS, LANES), F32)], axis=0
    )
    scal = jnp.concatenate([wide(limit_dual_start), jnp.zeros((STAT_ROWS - 1, LANES), F32)], axis=0)
    big_t = struct(test_blocks, LANES)
    big_r = struct(req_blocks, LANES)
    small = struct(STAT_ROWS, LANES)
    pull_shape = struct(test_blocks + STAT_ROWS, LANES)
    load_shape = struct(req_blocks + STAT_ROWS, LANES)
    group_shape = struct(GROUP, LANES, LANES, dtype=BF16)
    rest = slots // GROUP - KEPT
    sq_list, scal_list = [], []
    sum_primal = sum_dual = ()
    for iteration in range(ITERS):
        if iteration == 0:
            given = (
                coverage_tiles, dual, tile_rows.reshape(1, slots), tile_cols.reshape(1, slots), tile_counts.reshape(1, 1)
            )
            pull, pick_rows, place_rows, pick_cols, place_cols, *tiles = call(
                first_pull_kernel,
                (
                    pull_shape, struct(slots, req_blocks, dtype=BF16), struct(req_blocks, slots),
                    struct(slots, slots, dtype=BF16), struct(test_blocks, slots),
                    *[group_shape] * KEPT,
                ),
                [HBM] * len(given),
                [pltpu.VMEM((rest, *group_shape.shape), BF16), *[pltpu.VMEM(x.shape, x.dtype) for x in given[1:]]]
                + [pltpu.SemaphoreType.DMA((n,)) for n in (len(given) - 1, slots // GROUP)],
            )(*[pltpu.with_memory_space_constraint(x, pltpu.HBM) for x in given[:4]], given[4])
            tiles += call(
                rest_kernel, [group_shape] * rest, [HBM, VMEM], [pltpu.SemaphoreType.DMA((rest,))]
            )(coverage_tiles, pick_cols)
        else:
            given = (summed, params, pick_rows, place_cols, dual, scal, want, *tiles, *sum_dual)
            pull, dual, total, scal = call(
                functools.partial(dual_pull_kernel, iteration - 1, inverse_tests),
                (pull_shape, big_r, big_r, small), [VMEM] * len(given),
            )(*given)
            sum_dual = (total,)
            scal_list.append(scal)
        with jax.named_scope("sum_req"):
            parts = [pull, *on_req(pull)]
        given = (*parts, params, pick_cols, place_rows, primal, scal, costs, runs, *tiles, *sum_primal)
        outs = (load_shape, big_t) + (big_t,) * (iteration < ITERS - 1) + (small,) * (iteration > 0)
        load, primal, *more = call(functools.partial(primal_load_kernel, iteration), outs, [VMEM] * len(given))(*given)
        if iteration < ITERS - 1:
            sum_primal = (more.pop(0),)
        if iteration > 0:
            sq_list.append(more.pop(0))
        summed = total_tst(load)
        if iteration < ITERS - 1:
            summed = hand_on(summed)
    dual, scal, sq = call(
        functools.partial(dual_last_kernel, ITERS - 1, inverse_tests), (big_r, small, small), [VMEM] * 6
    )(summed, params, dual, scal, want, *sum_dual)
    scal_list.append(scal)
    with jax.named_scope("sum_req_last"):
        moves = [lambda y, z, c, r, bit=bit: (y, z, c, r ^ bit) if c == 1 else (y ^ 1, z, c, r) for bit in (1, 3, 2)]
        last = [sq, *[on_mesh(sq, move) for move in moves]]
    norms = call(norms_kernel, struct(2, ITERS), [VMEM] * 9)(*sq_list, *last, *scal_list)
    state = jnp.concatenate([dual, scal], axis=0)
    with jax.named_scope("back_core"):
        other = swap_core(state), swap_core(norms)
    dual, limit, norms = call(results_kernel, (big_r, struct(1, 1), struct(2, ITERS)), [VMEM] * 5)(
        params, state, other[0], norms, other[1]
    )
    return primal.reshape(-1), dual.reshape(-1), limit.reshape(1), norms.T


def solution(mesh):
    n_y = 4
    n_z = mesh.shape["tst"] // (2 * n_y)
    return jax.shard_map(
        functools.partial(per_device, n_y, n_z),
        mesh=mesh,
        in_specs=(
            P(("tst", "req"), None, None),
            P(("tst", "req")),
            P(("tst", "req")),
            P(("tst", "req")),
            P("tst"),
            P("tst"),
            P(),
            P("req"),
            P("tst"),
            P("req"),
            P(),
            P(),
        ),
        out_specs=(P("tst"), P("req"), P(), P()),
        check_vma=False,
    )
```

```python
import functools

import jax
import jax.numpy as jnp
from jax import lax
from jax.experimental import pallas as pl
from jax.experimental.pallas import tpu as pltpu
from jax.sharding import PartitionSpec as P

ITERS = 3
LANES = 128
STAT_ROWS = 8
GROUP = 16
KEPT = 6

step_primal = 0.6
step_dual = 0.6

VMEM = pl.BlockSpec(memory_space=pltpu.VMEM)
HBM = pl.BlockSpec(memory_space=pltpu.HBM)
F32 = jnp.float32
BF16 = jnp.bfloat16


def struct(*shape, dtype=F32):
    return jax.ShapeDtypeStruct(shape, dtype)


def stat_rows(*given):
    return jnp.concatenate([*given, jnp.zeros((STAT_ROWS - len(given), LANES), F32)], axis=0)


def sum_four(parts, rows):
    a, b, c, d = [part[rows, :] for part in parts]
    return (a + b) + (c + d)


def slot_count(params, iteration):
    seen = jnp.ones((1, LANES), F32)
    for earlier in range(iteration):
        seen = jnp.where(params[1 + earlier : 2 + earlier, :] == 1.0, 1.0, seen + 1.0)
    return seen


def average(params, iteration, total, new):
    restart_now = params[1 + iteration : 2 + iteration, :] == 1.0
    return (
        jnp.where(restart_now, total / slot_count(params, iteration), new),
        jnp.where(restart_now, 0.0, total),
    )


def spread(picked, group):
    rows = picked[group * GROUP : (group + 1) * GROUP, :]
    row_ids = lax.broadcasted_iota(jnp.int32, rows.shape, 0)
    return jnp.concatenate(
        [jnp.where(row_ids == offset, rows, 0.0) for offset in range(GROUP)], axis=1
    ).astype(BF16)


def gather_rows(pick, source):
    return jnp.dot(pick, source.astype(BF16), preferred_element_type=F32)


def scatter_sum(place, contrib):
    return jnp.dot(place, contrib, preferred_element_type=F32, precision=lax.Precision.HIGHEST)


def pull_group(picked, tiles, group):
    block = tiles[group][...].reshape(GROUP * LANES, LANES)
    return jnp.dot(spread(picked, group), block, preferred_element_type=F32)


def load_group(picked, tiles, group):
    block = jnp.concatenate([tiles[group][offset] for offset in range(GROUP)], axis=1)
    return lax.dot_general(
        spread(picked, group), block, (((1,), (1,)), ((), ())), preferred_element_type=F32
    )


def list_of(fetched):
    return [fetched.at[n] for n in range(fetched.shape[0])]


def rest_kernel(tiles_in, after, *refs):
    kept, sems = refs[:-1], refs[-1]
    copies = []
    for n, target in enumerate(kept):
        part = tiles_in.at[pl.ds((KEPT + n) * GROUP, GROUP)]
        copies.append(pltpu.make_async_copy(part, target, sems.at[n]))
        copies[-1].start()
    for copy in copies:
        copy.wait()


def first_pull_kernel(
    tiles_in, dual_in, rows_in, cols_in, live_in, pull_out, pick_rows, place_rows, pick_cols, place_cols, *refs
):
    slots = tiles_in.shape[0]
    groups = slots // GROUP
    kept, (fetched, dual, rows, cols, live, sems, tile_sems) = refs[:KEPT], refs[KEPT:]
    tiles = [*kept, *list_of(fetched)]
    small = []
    for n, (source, target) in enumerate(((rows_in, rows), (cols_in, cols), (live_in, live), (dual_in, dual))):
        small.append(pltpu.make_async_copy(source, target, sems.at[n]))
        small[-1].start()
    chunks = []
    for n in range(groups):
        chunks.append(pltpu.make_async_copy(tiles_in.at[pl.ds(n * GROUP, GROUP)], tiles[n], tile_sems.at[n]))
        chunks[-1].start()
    for copy in small:
        copy.wait()
    req_blocks = dual.shape[0]
    test_blocks = pull_out.shape[0] - STAT_ROWS
    alive = lax.broadcasted_iota(jnp.int32, (1, slots), 1) < live[...]
    at_row = lax.broadcasted_iota(jnp.int32, (req_blocks, slots), 0) == rows[...]
    at_col = lax.broadcasted_iota(jnp.int32, (test_blocks, slots), 0) == cols[...]
    one_row = jnp.where(at_row, 1.0, 0.0)
    one_col = jnp.where(at_col, 1.0, 0.0)
    place_rows[...] = jnp.where(alive, one_row, 0.0)
    place_cols[...] = jnp.where(alive, one_col, 0.0)
    pick = one_row.T.astype(BF16)
    pick_rows[...] = pick
    pick_cols[...] = jnp.concatenate([one_col, jnp.zeros((slots - test_blocks, slots), F32)], axis=0).T.astype(BF16)
    picked = gather_rows(pick, dual[...])
    contrib = []
    for group in range(groups):
        chunks[group].wait()
        contrib.append(pull_group(picked, tiles, group))
    pull_out[:test_blocks, :] = scatter_sum(place_cols[...], jnp.concatenate(contrib, axis=0))
    pull_out[test_blocks:, :] = jnp.zeros((STAT_ROWS, LANES), F32)


def update_dual(iteration, inverse_tests, summed, params, dual, sum_dual, scal, demand):
    req_blocks = dual.shape[0]
    load = summed[:req_blocks, :]
    stats = summed[req_blocks:, :]
    spent = jnp.sum(stats[0:1, :], axis=1, keepdims=True) * inverse_tests
    bdual = scal[0:1, :]
    bdual_new = jnp.maximum(bdual + step_dual * (spent - params[0:1, :]), 0.0)
    old = dual[...]
    new = jnp.maximum(old + step_dual * (demand[...] - load), 0.0)
    dual_sq = jnp.sum((new - old) ** 2, axis=0, keepdims=True)
    total = new if sum_dual is None else sum_dual[...] + new
    dual_next, total_next = average(params, iteration, total, new)
    bdual_next, bdual_total = average(params, iteration, scal[1:2, :] + bdual_new, bdual_new)
    scal_next = stat_rows(bdual_next, bdual_total, (bdual_new - bdual) ** 2, stats[1:2, :])
    return dual_next, total_next, scal_next, dual_sq


def dual_pull_kernel(iteration, inverse_tests, *refs):
    summed, params, pick_rows, place_cols, dual, scal, demand, *refs = refs
    groups = pick_rows.shape[0] // GROUP
    tiles, refs = refs[:groups], refs[groups:]
    sum_dual = refs.pop(0) if iteration > 0 else None
    pull_out, dual_out, sum_out, scal_out = refs
    dual_next, total_next, scal_next, dual_sq = update_dual(
        iteration, inverse_tests, summed, params, dual, sum_dual, scal, demand
    )
    dual_out[...] = dual_next
    sum_out[...] = total_next
    scal_out[...] = scal_next
    picked = gather_rows(pick_rows[...], dual_next)
    contrib = [pull_group(picked, tiles, group) for group in range(groups)]
    test_blocks = pull_out.shape[0] - STAT_ROWS
    pull_out[:test_blocks, :] = scatter_sum(place_cols[...], jnp.concatenate(contrib, axis=0))
    pull_out[test_blocks:, :] = stat_rows(dual_sq)


def dual_last_kernel(
    iteration, inverse_tests, summed, params, dual, scal, demand, sum_dual, dual_out, scal_out, sq_out
):
    dual_next, _, scal_next, dual_sq = update_dual(
        iteration, inverse_tests, summed, params, dual, sum_dual, scal, demand
    )
    dual_out[...] = dual_next
    scal_out[...] = scal_next
    sq_out[...] = stat_rows(dual_sq)


def primal_load_kernel(iteration, *refs):
    pull_own, pull_1, pull_2, pull_3, params, pick_cols, place_rows, primal, scal, costs, runtimes, *refs = refs
    slots = pick_cols.shape[0]
    groups = slots // GROUP
    tiles, refs = refs[:groups], refs[groups:]
    sum_primal = refs.pop(0) if iteration > 0 else None
    load_out, primal_out, *refs = refs
    sum_out = refs.pop(0) if iteration < ITERS - 1 else None
    sq_out = refs.pop(0) if iteration > 0 else None
    test_blocks = primal.shape[0]
    parts = (pull_own, pull_1, pull_2, pull_3)
    pull = sum_four(parts, slice(0, test_blocks))
    if sq_out is not None:
        sq_out[...] = sum_four(parts, slice(test_blocks, test_blocks + STAT_ROWS))
    old = primal[...]
    new = jnp.clip(old - step_primal * (costs[...] - pull + scal[0:1, :] * runtimes[...]), 0.0, 1.0)
    extrap = (2.0 * new - old).astype(BF16).astype(F32)
    total = new if sum_primal is None else sum_primal[...] + new
    primal_next, total_next = average(params, iteration, total, new)
    primal_out[...] = primal_next
    if sum_out is not None:
        sum_out[...] = total_next
    padded = jnp.concatenate([extrap, jnp.zeros((slots - test_blocks, LANES), F32)], axis=0)
    picked = gather_rows(pick_cols[...], padded)
    contrib = [load_group(picked, tiles, group) for group in range(groups)]
    req_blocks = load_out.shape[0] - STAT_ROWS
    load_out[:req_blocks, :] = scatter_sum(place_rows[...], jnp.concatenate(contrib, axis=0))
    load_out[req_blocks:, :] = stat_rows(
        jnp.sum(runtimes[...] * extrap, axis=0, keepdims=True),
        jnp.sum((new - old) ** 2, axis=0, keepdims=True),
    )


def norms_kernel(sq_0, sq_1, last_0, last_1, last_2, last_3, scal_0, scal_1, scal_2, norms_out):
    row_ids = lax.broadcasted_iota(jnp.int32, norms_out.shape, 0)
    col_ids = lax.broadcasted_iota(jnp.int32, norms_out.shape, 1)
    last = sum_four((last_0, last_1, last_2, last_3), slice(0, 1))
    out = jnp.zeros(norms_out.shape, F32)
    for k, (sq, scal) in enumerate(((sq_0[0:1, :], scal_0), (sq_1[0:1, :], scal_1), (last, scal_2))):
        move_dual = jnp.sum(sq, axis=1, keepdims=True) + scal[2:3, 0:1]
        move_primal = jnp.sum(scal[3:4, :], axis=1, keepdims=True)
        out = jnp.where(col_ids == k, jnp.where(row_ids == 0, move_primal, move_dual), out)
    norms_out[...] = out


def results_kernel(params, state_own, state_other, norms_own, norms_other, primal, dual_out, limit_out, norms_out, primal_out):
    primal_out[...] = primal[...]
    mine = params[1 + ITERS : 2 + ITERS, :] == 1.0
    req_blocks = dual_out.shape[0]
    dual_out[...] = jnp.where(mine, state_own[:req_blocks, :], state_other[:req_blocks, :])
    limit_out[...] = jnp.where(mine, state_own[req_blocks : req_blocks + 1, :], state_other[req_blocks : req_blocks + 1, :])[:, :1]
    norms_out[...] = jnp.where(mine[:, :ITERS], norms_own[...], norms_other[...])


def call(body, outs, specs, scratch=()):
    return pl.pallas_call(
        body,
        out_shape=outs,
        in_specs=specs,
        out_specs=jax.tree.map(lambda _: VMEM, outs),
        scratch_shapes=list(scratch),
        compiler_params=pltpu.CompilerParams(vmem_limit_bytes=(50 if HBM in specs else 16) * 1024 * 1024),
    )


def per_device(
    n_y, n_z,
    coverage_tiles, tile_rows, tile_cols, tile_counts, test_costs, runtimes, time_limit, demand,
    primal_start, dual_start, limit_dual_start, restarts,
):
    slots = coverage_tiles.shape[0]
    test_blocks = test_costs.shape[0] // LANES
    req_blocks = demand.shape[0] // LANES
    inverse_tests = 1.0 / (test_costs.shape[0] * lax.axis_size("tst"))
    costs = test_costs.reshape(test_blocks, LANES)
    runs = runtimes.reshape(test_blocks, LANES)
    want = demand.reshape(req_blocks, LANES)
    primal = primal_start.reshape(test_blocks, LANES)
    dual = dual_start.reshape(req_blocks, LANES)

    far_core = lax.axis_index("tst") % 2 == 1

    n_req = lax.axis_size("req")

    def on_mesh(x, move):
        pairs = []
        for y in range(n_y):
            for z in range(n_z):
                for c in range(2):
                    for r in range(n_req):
                        to_y, to_z, to_c, to_r = move(y, z, c, r)
                        source = ((y * n_z + z) * 2 + c) * n_req + r
                        pairs.append((source, ((to_y * n_z + to_z) * 2 + to_c) * n_req + to_r))
        return lax.ppermute(x, ("tst", "req"), pairs)

    def swap_core(x):
        return on_mesh(x, lambda y, z, c, r: (y, z, 1 - c, r))

    def chips(x, y_bits, z_bits):
        return on_mesh(x, lambda y, z, c, r: (y ^ y_bits, z ^ z_bits, c, r) if c == 1 else (y, z, c, r ^ 1))

    def on_req(x):
        return [lax.ppermute(x, "req", [(i, i ^ bit) for i in range(n_req)]) for bit in (1, 3, 2)]

    def total_tst(x):
        with jax.named_scope("sum_core"):
            x = x + swap_core(x)
        with jax.named_scope("sum_z_outer"):
            x = x + chips(x, 0, n_z - 2)
        with jax.named_scope("sum_z_inner"):
            a, b, c = [chips(x, 0, bits) for bits in (1, 3, 2)]
            x = (x + a) + (b + c)
        with jax.named_scope("sum_y"):
            a, b, c = [chips(x, bits, 0) for bits in (1, 3, 2)]
            x = (x + a) + (b + c)
        return x

    def hand_on(x):
        with jax.named_scope("back_core"):
            return jnp.where(far_core, x, swap_core(x))

    wide = lambda x: jnp.broadcast_to(x.astype(F32).reshape(-1, 1), (x.shape[0], LANES))
    params = jnp.concatenate(
        [wide(time_limit), wide(restarts), wide(far_core.reshape(1)), jnp.zeros((STAT_ROWS - 2 - ITERS, LANES), F32)], axis=0
    )
    scal = jnp.concatenate([wide(limit_dual_start), jnp.zeros((STAT_ROWS - 1, LANES), F32)], axis=0)
    big_t = struct(test_blocks, LANES)
    big_r = struct(req_blocks, LANES)
    small = struct(STAT_ROWS, LANES)
    pull_shape = struct(test_blocks + STAT_ROWS, LANES)
    load_shape = struct(req_blocks + STAT_ROWS, LANES)
    group_shape = struct(GROUP, LANES, LANES, dtype=BF16)
    rest = slots // GROUP - KEPT
    sq_list, scal_list = [], []
    sum_primal = sum_dual = ()
    for iteration in range(ITERS):
        if iteration == 0:
            given = (
                coverage_tiles, dual, tile_rows.reshape(1, slots), tile_cols.reshape(1, slots), tile_counts.reshape(1, 1)
            )
            pull, pick_rows, place_rows, pick_cols, place_cols, *tiles = call(
                first_pull_kernel,
                (
                    pull_shape, struct(slots, req_blocks, dtype=BF16), struct(req_blocks, slots),
                    struct(slots, slots, dtype=BF16), struct(test_blocks, slots),
                    *[group_shape] * KEPT,
                ),
                [HBM] * len(given),
                [pltpu.VMEM((rest, *group_shape.shape), BF16), *[pltpu.VMEM(x.shape, x.dtype) for x in given[1:]]]
                + [pltpu.SemaphoreType.DMA((n,)) for n in (len(given) - 1, slots // GROUP)],
            )(*[pltpu.with_memory_space_constraint(x, pltpu.HBM) for x in given[:4]], given[4])
            tiles += call(
                rest_kernel, [group_shape] * rest, [HBM, VMEM], [pltpu.SemaphoreType.DMA((rest,))]
            )(coverage_tiles, pick_cols)
        else:
            given = (summed, params, pick_rows, place_cols, dual, scal, want, *tiles, *sum_dual)
            pull, dual, total, scal = call(
                functools.partial(dual_pull_kernel, iteration - 1, inverse_tests),
                (pull_shape, big_r, big_r, small), [VMEM] * len(given),
            )(*given)
            sum_dual = (total,)
            scal_list.append(scal)
        with jax.named_scope("sum_req"):
            parts = [pull, *on_req(pull)]
        given = (*parts, params, pick_cols, place_rows, primal, scal, costs, runs, *tiles, *sum_primal)
        outs = (load_shape, big_t) + (big_t,) * (iteration < ITERS - 1) + (small,) * (iteration > 0)
        load, primal, *more = call(functools.partial(primal_load_kernel, iteration), outs, [VMEM] * len(given))(*given)
        if iteration < ITERS - 1:
            sum_primal = (more.pop(0),)
        if iteration > 0:
            sq_list.append(more.pop(0))
        summed = total_tst(load)
        if iteration < ITERS - 1:
            summed = hand_on(summed)
    dual, scal, sq = call(
        functools.partial(dual_last_kernel, ITERS - 1, inverse_tests), (big_r, small, small), [VMEM] * 6
    )(summed, params, dual, scal, want, *sum_dual)
    scal_list.append(scal)
    with jax.named_scope("sum_req_last"):
        moves = [lambda y, z, c, r, bit=bit: (y, z, c, r ^ bit) if c == 1 else (y ^ 1, z, c, r) for bit in (1, 3, 2)]
        last = [sq, *[on_mesh(sq, move) for move in moves]]
    norms = call(norms_kernel, struct(2, ITERS), [VMEM] * 9)(*sq_list, *last, *scal_list)
    state = jnp.concatenate([dual, scal], axis=0)
    with jax.named_scope("back_core"):
        other = swap_core(state), swap_core(norms)
    dual, limit, norms, primal = call(results_kernel, (big_r, struct(1, 1), struct(2, ITERS), big_t), [VMEM] * 6)(
        params, state, other[0], norms, other[1], primal
    )
    return primal.reshape(-1), dual.reshape(-1), limit.reshape(1), norms.T


def solution(mesh):
    n_y = 4
    n_z = mesh.shape["tst"] // (2 * n_y)
    return jax.shard_map(
        functools.partial(per_device, n_y, n_z),
        mesh=mesh,
        in_specs=(
            P(("tst", "req"), None, None),
            P(("tst", "req")),
            P(("tst", "req")),
            P(("tst", "req")),
            P("tst"),
            P("tst"),
            P(),
            P("req"),
            P("tst"),
            P("req"),
            P(),
            P(),
        ),
        out_specs=(P("tst"), P("req"), P(), P()),
        check_vma=False,
    )
```

```python
import functools

import jax
import jax.numpy as jnp
from jax import lax
from jax.experimental import pallas as pl
from jax.experimental.pallas import tpu as pltpu
from jax.sharding import PartitionSpec as P

ITERS = 3
LANES = 128
STAT_ROWS = 8
GROUP = 16
KEPT = 6

step_primal = 0.6
step_dual = 0.6

VMEM = pl.BlockSpec(memory_space=pltpu.VMEM)
HBM = pl.BlockSpec(memory_space=pltpu.HBM)
F32 = jnp.float32
BF16 = jnp.bfloat16


def struct(*shape, dtype=F32):
    return jax.ShapeDtypeStruct(shape, dtype)


def stat_rows(*given):
    return jnp.concatenate([*given, jnp.zeros((STAT_ROWS - len(given), LANES), F32)], axis=0)


def sum_four(parts, rows):
    a, b, c, d = [part[rows, :] for part in parts]
    return (a + b) + (c + d)


def slot_count(params, iteration):
    seen = jnp.ones((1, LANES), F32)
    for earlier in range(iteration):
        seen = jnp.where(params[1 + earlier : 2 + earlier, :] == 1.0, 1.0, seen + 1.0)
    return seen


def average(params, iteration, total, new):
    restart_now = params[1 + iteration : 2 + iteration, :] == 1.0
    return (
        jnp.where(restart_now, total / slot_count(params, iteration), new),
        jnp.where(restart_now, 0.0, total),
    )


def spread(picked, group):
    rows = picked[group * GROUP : (group + 1) * GROUP, :]
    row_ids = lax.broadcasted_iota(jnp.int32, rows.shape, 0)
    return jnp.concatenate(
        [jnp.where(row_ids == offset, rows, 0.0) for offset in range(GROUP)], axis=1
    ).astype(BF16)


def gather_rows(pick, source):
    return jnp.dot(pick, source.astype(BF16), preferred_element_type=F32)


def scatter_sum(place, contrib):
    return jnp.dot(place, contrib, preferred_element_type=F32, precision=lax.Precision.HIGHEST)


def pull_group(picked, tiles, group):
    block = tiles[group][...].reshape(GROUP * LANES, LANES)
    return jnp.dot(spread(picked, group), block, preferred_element_type=F32)


def load_group(picked, tiles, group):
    block = jnp.concatenate([tiles[group][offset] for offset in range(GROUP)], axis=1)
    return lax.dot_general(
        spread(picked, group), block, (((1,), (1,)), ((), ())), preferred_element_type=F32
    )


def list_of(fetched):
    return [fetched.at[n] for n in range(fetched.shape[0])]


def rest_kernel(tiles_in, pick_rows, place_cols, place_rows, pick_cols, *refs):
    kept, sems = refs[:-1], refs[-1]
    copies = []
    for n, target in enumerate(kept):
        part = tiles_in.at[pl.ds((KEPT + n) * GROUP, GROUP)]
        copies.append(pltpu.make_async_copy(part, target, sems.at[n]))
        copies[-1].start()
    place_rows[...] = pick_rows[...].astype(F32).T
    slots, test_blocks = pick_cols.shape[0], place_cols.shape[0]
    padded = jnp.concatenate([place_cols[...], jnp.zeros((slots - test_blocks, slots), F32)], axis=0)
    pick_cols[...] = padded.T.astype(BF16)
    for copy in copies:
        copy.wait()


def first_pull_kernel(
    tiles_in, dual_in, rows_in, cols_in, live_in, pull_out, pick_rows, place_cols, *refs
):
    slots = tiles_in.shape[0]
    groups = slots // GROUP
    kept, (fetched, dual, rows, cols, live, sems, tile_sems) = refs[:KEPT], refs[KEPT:]
    tiles = [*kept, *list_of(fetched)]
    small = []
    for n, (source, target) in enumerate(((rows_in, rows), (cols_in, cols), (live_in, live), (dual_in, dual))):
        small.append(pltpu.make_async_copy(source, target, sems.at[n]))
        small[-1].start()
    chunks = []
    for n in range(groups):
        chunks.append(pltpu.make_async_copy(tiles_in.at[pl.ds(n * GROUP, GROUP)], tiles[n], tile_sems.at[n]))
        chunks[-1].start()
    for copy in small:
        copy.wait()
    req_blocks = dual.shape[0]
    test_blocks = pull_out.shape[0] - STAT_ROWS
    alive = lax.broadcasted_iota(jnp.int32, (1, slots), 1) < live[...]
    at_row = lax.broadcasted_iota(jnp.int32, (req_blocks, slots), 0) == rows[...]
    at_col = lax.broadcasted_iota(jnp.int32, (test_blocks, slots), 0) == cols[...]
    one_row = jnp.where(at_row, 1.0, 0.0)
    place_cols[...] = jnp.where(at_col & alive, 1.0, 0.0)
    pick = one_row.T.astype(BF16)
    pick_rows[...] = pick
    picked = gather_rows(pick, dual[...])
    contrib = []
    for group in range(groups):
        chunks[group].wait()
        contrib.append(pull_group(picked, tiles, group))
    pull_out[:test_blocks, :] = scatter_sum(place_cols[...], jnp.concatenate(contrib, axis=0))
    pull_out[test_blocks:, :] = jnp.zeros((STAT_ROWS, LANES), F32)


def update_dual(iteration, inverse_tests, summed, params, dual, sum_dual, scal, demand):
    req_blocks = dual.shape[0]
    load = summed[:req_blocks, :]
    stats = summed[req_blocks:, :]
    spent = jnp.sum(stats[0:1, :], axis=1, keepdims=True) * inverse_tests
    bdual = scal[0:1, :]
    bdual_new = jnp.maximum(bdual + step_dual * (spent - params[0:1, :]), 0.0)
    old = dual[...]
    new = jnp.maximum(old + step_dual * (demand[...] - load), 0.0)
    dual_sq = jnp.sum((new - old) ** 2, axis=0, keepdims=True)
    total = new if sum_dual is None else sum_dual[...] + new
    dual_next, total_next = average(params, iteration, total, new)
    bdual_next, bdual_total = average(params, iteration, scal[1:2, :] + bdual_new, bdual_new)
    scal_next = stat_rows(bdual_next, bdual_total, (bdual_new - bdual) ** 2, stats[1:2, :])
    return dual_next, total_next, scal_next, dual_sq


def dual_pull_kernel(iteration, inverse_tests, *refs):
    summed, params, pick_rows, place_cols, dual, scal, demand, *refs = refs
    groups = pick_rows.shape[0] // GROUP
    tiles, refs = refs[:groups], refs[groups:]
    sum_dual = refs.pop(0) if iteration > 0 else None
    pull_out, dual_out, sum_out, scal_out = refs
    dual_next, total_next, scal_next, dual_sq = update_dual(
        iteration, inverse_tests, summed, params, dual, sum_dual, scal, demand
    )
    dual_out[...] = dual_next
    sum_out[...] = total_next
    scal_out[...] = scal_next
    picked = gather_rows(pick_rows[...], dual_next)
    contrib = [pull_group(picked, tiles, group) for group in range(groups)]
    test_blocks = pull_out.shape[0] - STAT_ROWS
    pull_out[:test_blocks, :] = scatter_sum(place_cols[...], jnp.concatenate(contrib, axis=0))
    pull_out[test_blocks:, :] = stat_rows(dual_sq)


def dual_last_kernel(
    iteration, inverse_tests, summed, params, dual, scal, demand, sum_dual, dual_out, scal_out, sq_out
):
    dual_next, _, scal_next, dual_sq = update_dual(
        iteration, inverse_tests, summed, params, dual, sum_dual, scal, demand
    )
    dual_out[...] = dual_next
    scal_out[...] = scal_next
    sq_out[...] = stat_rows(dual_sq)


def primal_load_kernel(iteration, *refs):
    pull_own, pull_1, pull_2, pull_3, params, pick_cols, place_rows, primal, scal, costs, runtimes, *refs = refs
    slots = pick_cols.shape[0]
    groups = slots // GROUP
    tiles, refs = refs[:groups], refs[groups:]
    sum_primal = refs.pop(0) if iteration > 0 else None
    load_out, primal_out, *refs = refs
    sum_out = refs.pop(0) if iteration < ITERS - 1 else None
    sq_out = refs.pop(0) if iteration > 0 else None
    test_blocks = primal.shape[0]
    parts = (pull_own, pull_1, pull_2, pull_3)
    pull = sum_four(parts, slice(0, test_blocks))
    if sq_out is not None:
        sq_out[...] = sum_four(parts, slice(test_blocks, test_blocks + STAT_ROWS))
    old = primal[...]
    new = jnp.clip(old - step_primal * (costs[...] - pull + scal[0:1, :] * runtimes[...]), 0.0, 1.0)
    extrap = (2.0 * new - old).astype(BF16).astype(F32)
    total = new if sum_primal is None else sum_primal[...] + new
    primal_next, total_next = average(params, iteration, total, new)
    primal_out[...] = primal_next
    if sum_out is not None:
        sum_out[...] = total_next
    padded = jnp.concatenate([extrap, jnp.zeros((slots - test_blocks, LANES), F32)], axis=0)
    picked = gather_rows(pick_cols[...], padded)
    contrib = [load_group(picked, tiles, group) for group in range(groups)]
    req_blocks = load_out.shape[0] - STAT_ROWS
    load_out[:req_blocks, :] = scatter_sum(place_rows[...], jnp.concatenate(contrib, axis=0))
    load_out[req_blocks:, :] = stat_rows(
        jnp.sum(runtimes[...] * extrap, axis=0, keepdims=True),
        jnp.sum((new - old) ** 2, axis=0, keepdims=True),
    )


def norms_kernel(sq_0, sq_1, last_0, last_1, last_2, last_3, scal_0, scal_1, scal_2, norms_out):
    row_ids = lax.broadcasted_iota(jnp.int32, norms_out.shape, 0)
    col_ids = lax.broadcasted_iota(jnp.int32, norms_out.shape, 1)
    last = sum_four((last_0, last_1, last_2, last_3), slice(0, 1))
    out = jnp.zeros(norms_out.shape, F32)
    for k, (sq, scal) in enumerate(((sq_0[0:1, :], scal_0), (sq_1[0:1, :], scal_1), (last, scal_2))):
        move_dual = jnp.sum(sq, axis=1, keepdims=True) + scal[2:3, 0:1]
        move_primal = jnp.sum(scal[3:4, :], axis=1, keepdims=True)
        out = jnp.where(col_ids == k, jnp.where(row_ids == 0, move_primal, move_dual), out)
    norms_out[...] = out


def results_kernel(params, state_own, state_other, norms_own, norms_other, primal, dual_out, limit_out, norms_out, primal_out):
    primal_out[...] = primal[...]
    mine = params[1 + ITERS : 2 + ITERS, :] == 1.0
    req_blocks = dual_out.shape[0]
    dual_out[...] = jnp.where(mine, state_own[:req_blocks, :], state_other[:req_blocks, :])
    limit_out[...] = jnp.where(mine, state_own[req_blocks : req_blocks + 1, :], state_other[req_blocks : req_blocks + 1, :])[:, :1]
    norms_out[...] = jnp.where(mine[:, :ITERS], norms_own[...], norms_other[...])


def call(body, outs, specs, scratch=()):
    return pl.pallas_call(
        body,
        out_shape=outs,
        in_specs=specs,
        out_specs=jax.tree.map(lambda _: VMEM, outs),
        scratch_shapes=list(scratch),
        compiler_params=pltpu.CompilerParams(vmem_limit_bytes=(50 if HBM in specs else 16) * 1024 * 1024),
    )


def per_device(
    n_y, n_z,
    coverage_tiles, tile_rows, tile_cols, tile_counts, test_costs, runtimes, time_limit, demand,
    primal_start, dual_start, limit_dual_start, restarts,
):
    slots = coverage_tiles.shape[0]
    test_blocks = test_costs.shape[0] // LANES
    req_blocks = demand.shape[0] // LANES
    inverse_tests = 1.0 / (test_costs.shape[0] * lax.axis_size("tst"))
    costs = test_costs.reshape(test_blocks, LANES)
    runs = runtimes.reshape(test_blocks, LANES)
    want = demand.reshape(req_blocks, LANES)
    primal = primal_start.reshape(test_blocks, LANES)
    dual = dual_start.reshape(req_blocks, LANES)

    far_core = lax.axis_index("tst") % 2 == 1

    n_req = lax.axis_size("req")

    def on_mesh(x, move):
        pairs = []
        for y in range(n_y):
            for z in range(n_z):
                for c in range(2):
                    for r in range(n_req):
                        to_y, to_z, to_c, to_r = move(y, z, c, r)
                        source = ((y * n_z + z) * 2 + c) * n_req + r
                        pairs.append((source, ((to_y * n_z + to_z) * 2 + to_c) * n_req + to_r))
        return lax.ppermute(x, ("tst", "req"), pairs)

    def swap_core(x):
        return on_mesh(x, lambda y, z, c, r: (y, z, 1 - c, r))

    def chips(x, y_bits, z_bits):
        return on_mesh(x, lambda y, z, c, r: (y ^ y_bits, z ^ z_bits, c, r) if c == 1 else (y, z, c, r ^ 1))

    def on_req(x):
        return [lax.ppermute(x, "req", [(i, i ^ bit) for i in range(n_req)]) for bit in (1, 3, 2)]

    def total_tst(x):
        with jax.named_scope("sum_core"):
            x = x + swap_core(x)
        with jax.named_scope("sum_z_outer"):
            x = x + chips(x, 0, n_z - 2)
        with jax.named_scope("sum_z_inner"):
            a, b, c = [chips(x, 0, bits) for bits in (1, 3, 2)]
            x = (x + a) + (b + c)
        with jax.named_scope("sum_y"):
            a, b, c = [chips(x, bits, 0) for bits in (1, 3, 2)]
            x = (x + a) + (b + c)
        return x

    def hand_on(x):
        with jax.named_scope("back_core"):
            return jnp.where(far_core, x, swap_core(x))

    wide = lambda x: jnp.broadcast_to(x.astype(F32).reshape(-1, 1), (x.shape[0], LANES))
    params = jnp.concatenate(
        [wide(time_limit), wide(restarts), wide(far_core.reshape(1)), jnp.zeros((STAT_ROWS - 2 - ITERS, LANES), F32)], axis=0
    )
    scal = jnp.concatenate([wide(limit_dual_start), jnp.zeros((STAT_ROWS - 1, LANES), F32)], axis=0)
    big_t = struct(test_blocks, LANES)
    big_r = struct(req_blocks, LANES)
    small = struct(STAT_ROWS, LANES)
    pull_shape = struct(test_blocks + STAT_ROWS, LANES)
    load_shape = struct(req_blocks + STAT_ROWS, LANES)
    group_shape = struct(GROUP, LANES, LANES, dtype=BF16)
    rest = slots // GROUP - KEPT
    sq_list, scal_list = [], []
    sum_primal = sum_dual = ()
    for iteration in range(ITERS):
        if iteration == 0:
            given = (
                coverage_tiles, dual, tile_rows.reshape(1, slots), tile_cols.reshape(1, slots), tile_counts.reshape(1, 1)
            )
            pull, pick_rows, place_cols, *tiles = call(
                first_pull_kernel,
                (
                    pull_shape, struct(slots, req_blocks, dtype=BF16), struct(test_blocks, slots),
                    *[group_shape] * KEPT,
                ),
                [HBM] * len(given),
                [pltpu.VMEM((rest, *group_shape.shape), BF16), *[pltpu.VMEM(x.shape, x.dtype) for x in given[1:]]]
                + [pltpu.SemaphoreType.DMA((n,)) for n in (len(given) - 1, slots // GROUP)],
            )(*[pltpu.with_memory_space_constraint(x, pltpu.HBM) for x in given[:4]], given[4])
            place_rows, pick_cols, *more = call(
                rest_kernel,
                [struct(req_blocks, slots), struct(slots, slots, dtype=BF16)] + [group_shape] * rest,
                [HBM, VMEM, VMEM],
                [pltpu.SemaphoreType.DMA((rest,))],
            )(coverage_tiles, pick_rows, place_cols)
            tiles += more
        else:
            given = (summed, params, pick_rows, place_cols, dual, scal, want, *tiles, *sum_dual)
            pull, dual, total, scal = call(
                functools.partial(dual_pull_kernel, iteration - 1, inverse_tests),
                (pull_shape, big_r, big_r, small), [VMEM] * len(given),
            )(*given)
            sum_dual = (total,)
            scal_list.append(scal)
        with jax.named_scope("sum_req"):
            parts = [pull, *on_req(pull)]
        given = (*parts, params, pick_cols, place_rows, primal, scal, costs, runs, *tiles, *sum_primal)
        outs = (load_shape, big_t) + (big_t,) * (iteration < ITERS - 1) + (small,) * (iteration > 0)
        load, primal, *more = call(functools.partial(primal_load_kernel, iteration), outs, [VMEM] * len(given))(*given)
        if iteration < ITERS - 1:
            sum_primal = (more.pop(0),)
        if iteration > 0:
            sq_list.append(more.pop(0))
        summed = total_tst(load)
        if iteration < ITERS - 1:
            summed = hand_on(summed)
    dual, scal, sq = call(
        functools.partial(dual_last_kernel, ITERS - 1, inverse_tests), (big_r, small, small), [VMEM] * 6
    )(summed, params, dual, scal, want, *sum_dual)
    scal_list.append(scal)
    with jax.named_scope("sum_req_last"):
        moves = [lambda y, z, c, r, bit=bit: (y, z, c, r ^ bit) if c == 1 else (y ^ 1, z, c, r) for bit in (1, 3, 2)]
        last = [sq, *[on_mesh(sq, move) for move in moves]]
    norms = call(norms_kernel, struct(2, ITERS), [VMEM] * 9)(*sq_list, *last, *scal_list)
    state = jnp.concatenate([dual, scal], axis=0)
    with jax.named_scope("back_core"):
        other = swap_core(state), swap_core(norms)
    dual, limit, norms, primal = call(results_kernel, (big_r, struct(1, 1), struct(2, ITERS), big_t), [VMEM] * 6)(
        params, state, other[0], norms, other[1], primal
    )
    return primal.reshape(-1), dual.reshape(-1), limit.reshape(1), norms.T


def solution(mesh):
    n_y = 4
    n_z = mesh.shape["tst"] // (2 * n_y)
    return jax.shard_map(
        functools.partial(per_device, n_y, n_z),
        mesh=mesh,
        in_specs=(
            P(("tst", "req"), None, None),
            P(("tst", "req")),
            P(("tst", "req")),
            P(("tst", "req")),
            P("tst"),
            P("tst"),
            P(),
            P("req"),
            P("tst"),
            P("req"),
            P(),
            P(),
        ),
        out_specs=(P("tst"), P("req"), P(), P()),
        check_vma=False,
    )
```

```python
import functools

import jax
import jax.numpy as jnp
from jax import lax
from jax.experimental import pallas as pl
from jax.experimental.pallas import tpu as pltpu
from jax.sharding import PartitionSpec as P

ITERS = 3
LANES = 128
STAT_ROWS = 8
GROUP = 16
KEPT = 6
PIECES = 4

step_primal = 0.6
step_dual = 0.6

VMEM = pl.BlockSpec(memory_space=pltpu.VMEM)
HBM = pl.BlockSpec(memory_space=pltpu.HBM)
F32 = jnp.float32
BF16 = jnp.bfloat16


def struct(*shape, dtype=F32):
    return jax.ShapeDtypeStruct(shape, dtype)


def stat_rows(*given):
    return jnp.concatenate([*given, jnp.zeros((STAT_ROWS - len(given), LANES), F32)], axis=0)


def sum_four(parts, rows):
    a, b, c, d = [part[rows, :] for part in parts]
    return (a + b) + (c + d)


def slot_count(params, iteration):
    seen = jnp.ones((1, LANES), F32)
    for earlier in range(iteration):
        seen = jnp.where(params[1 + earlier : 2 + earlier, :] == 1.0, 1.0, seen + 1.0)
    return seen


def average(params, iteration, total, new):
    restart_now = params[1 + iteration : 2 + iteration, :] == 1.0
    return (
        jnp.where(restart_now, total / slot_count(params, iteration), new),
        jnp.where(restart_now, 0.0, total),
    )


def spread(picked, group):
    rows = picked[group * GROUP : (group + 1) * GROUP, :]
    row_ids = lax.broadcasted_iota(jnp.int32, rows.shape, 0)
    return jnp.concatenate(
        [jnp.where(row_ids == offset, rows, 0.0) for offset in range(GROUP)], axis=1
    ).astype(BF16)


def gather_rows(pick, source):
    return jnp.dot(pick, source.astype(BF16), preferred_element_type=F32)


def scatter_sum(place, contrib):
    return jnp.dot(place, contrib, preferred_element_type=F32, precision=lax.Precision.HIGHEST)


def pull_group(picked, tiles, group):
    block = tiles[group][...].reshape(GROUP * LANES, LANES)
    return jnp.dot(spread(picked, group), block, preferred_element_type=F32)


def load_group(picked, tiles, group):
    block = jnp.concatenate([tiles[group][offset] for offset in range(GROUP)], axis=1)
    return lax.dot_general(
        spread(picked, group), block, (((1,), (1,)), ((), ())), preferred_element_type=F32
    )


def list_of(fetched):
    return [fetched.at[n] for n in range(fetched.shape[0])]


def rest_kernel(tiles_in, pick_rows, place_cols, place_rows, pick_cols, *refs):
    kept, sems = refs[:-1], refs[-1]
    copies = []
    for n, target in enumerate(kept):
        part = tiles_in.at[pl.ds((KEPT + n) * GROUP, GROUP)]
        copies.append(pltpu.make_async_copy(part, target, sems.at[n]))
        copies[-1].start()
    place_rows[...] = pick_rows[...].astype(F32).T
    slots, test_blocks = pick_cols.shape[0], place_cols.shape[0]
    padded = jnp.concatenate([place_cols[...], jnp.zeros((slots - test_blocks, slots), F32)], axis=0)
    pick_cols[...] = padded.T.astype(BF16)
    for copy in copies:
        copy.wait()


def first_pull_kernel(
    tiles_in, dual_in, rows_in, cols_in, live_in, pull_out, pick_rows, place_cols, *refs
):
    slots = tiles_in.shape[0]
    groups = slots // GROUP
    kept, (fetched, dual, rows, cols, live, sems, tile_sems) = refs[:KEPT], refs[KEPT:]
    tiles = [*kept, *list_of(fetched)]
    small = []
    for n, (source, target) in enumerate(((rows_in, rows), (cols_in, cols), (live_in, live), (dual_in, dual))):
        small.append(pltpu.make_async_copy(source, target, sems.at[n]))
        small[-1].start()
    chunks = []
    size = GROUP // PIECES
    for n in range(groups * PIECES):
        target = tiles[n // PIECES].at[pl.ds(n % PIECES * size, size)]
        chunks.append(pltpu.make_async_copy(tiles_in.at[pl.ds(n * size, size)], target, tile_sems.at[n]))
        chunks[-1].start()
    for copy in small:
        copy.wait()
    req_blocks = dual.shape[0]
    test_blocks = pull_out.shape[0]
    alive = lax.broadcasted_iota(jnp.int32, (1, slots), 1) < live[...]
    at_row = lax.broadcasted_iota(jnp.int32, (req_blocks, slots), 0) == rows[...]
    at_col = lax.broadcasted_iota(jnp.int32, (test_blocks, slots), 0) == cols[...]
    one_row = jnp.where(at_row, 1.0, 0.0)
    place_cols[...] = jnp.where(at_col & alive, 1.0, 0.0)
    pick = one_row.T.astype(BF16)
    pick_rows[...] = pick
    picked = gather_rows(pick, dual[...])
    contrib = []
    for group in range(groups):
        for copy in chunks[group * PIECES : (group + 1) * PIECES]:
            copy.wait()
        contrib.append(pull_group(picked, tiles, group))
    pull_out[...] = scatter_sum(place_cols[...], jnp.concatenate(contrib, axis=0))


def update_dual(iteration, inverse_tests, summed, params, dual, sum_dual, scal, demand):
    req_blocks = dual.shape[0]
    load = summed[:req_blocks, :]
    stats = summed[req_blocks:, :]
    spent = jnp.sum(stats[0:1, :], axis=1, keepdims=True) * inverse_tests
    bdual = scal[0:1, :]
    bdual_new = jnp.maximum(bdual + step_dual * (spent - params[0:1, :]), 0.0)
    old = dual[...]
    new = jnp.maximum(old + step_dual * (demand[...] - load), 0.0)
    dual_sq = jnp.sum((new - old) ** 2, axis=0, keepdims=True)
    total = new if sum_dual is None else sum_dual[...] + new
    dual_next, total_next = average(params, iteration, total, new)
    bdual_next, bdual_total = average(params, iteration, scal[1:2, :] + bdual_new, bdual_new)
    scal_next = stat_rows(bdual_next, bdual_total, (bdual_new - bdual) ** 2, stats[1:2, :])
    return dual_next, total_next, scal_next, dual_sq


def dual_pull_kernel(iteration, inverse_tests, *refs):
    summed, params, pick_rows, place_cols, dual, scal, demand, *refs = refs
    groups = pick_rows.shape[0] // GROUP
    tiles, refs = refs[:groups], refs[groups:]
    sum_dual = refs.pop(0) if iteration > 0 else None
    pull_out, dual_out, sum_out, scal_out = refs
    dual_next, total_next, scal_next, dual_sq = update_dual(
        iteration, inverse_tests, summed, params, dual, sum_dual, scal, demand
    )
    dual_out[...] = dual_next
    sum_out[...] = total_next
    scal_out[...] = scal_next
    picked = gather_rows(pick_rows[...], dual_next)
    contrib = [pull_group(picked, tiles, group) for group in range(groups)]
    test_blocks = pull_out.shape[0] - STAT_ROWS
    pull_out[:test_blocks, :] = scatter_sum(place_cols[...], jnp.concatenate(contrib, axis=0))
    pull_out[test_blocks:, :] = stat_rows(dual_sq)


def dual_last_kernel(
    iteration, inverse_tests, summed, params, dual, scal, demand, sum_dual, dual_out, scal_out, sq_out
):
    dual_next, _, scal_next, dual_sq = update_dual(
        iteration, inverse_tests, summed, params, dual, sum_dual, scal, demand
    )
    dual_out[...] = dual_next
    scal_out[...] = scal_next
    sq_out[...] = stat_rows(dual_sq)


def primal_load_kernel(iteration, *refs):
    pull_own, pull_1, pull_2, pull_3, params, pick_cols, place_rows, primal, scal, costs, runtimes, *refs = refs
    slots = pick_cols.shape[0]
    groups = slots // GROUP
    tiles, refs = refs[:groups], refs[groups:]
    sum_primal = refs.pop(0) if iteration > 0 else None
    load_out, primal_out, *refs = refs
    sum_out = refs.pop(0) if iteration < ITERS - 1 else None
    sq_out = refs.pop(0) if iteration > 0 else None
    test_blocks = primal.shape[0]
    parts = (pull_own, pull_1, pull_2, pull_3)
    pull = sum_four(parts, slice(0, test_blocks))
    if sq_out is not None:
        sq_out[...] = sum_four(parts, slice(test_blocks, test_blocks + STAT_ROWS))
    old = primal[...]
    new = jnp.clip(old - step_primal * (costs[...] - pull + scal[0:1, :] * runtimes[...]), 0.0, 1.0)
    extrap = (2.0 * new - old).astype(BF16).astype(F32)
    total = new if sum_primal is None else sum_primal[...] + new
    primal_next, total_next = average(params, iteration, total, new)
    primal_out[...] = primal_next
    if sum_out is not None:
        sum_out[...] = total_next
    padded = jnp.concatenate([extrap, jnp.zeros((slots - test_blocks, LANES), F32)], axis=0)
    picked = gather_rows(pick_cols[...], padded)
    contrib = [load_group(picked, tiles, group) for group in range(groups)]
    req_blocks = load_out.shape[0] - STAT_ROWS
    load_out[:req_blocks, :] = scatter_sum(place_rows[...], jnp.concatenate(contrib, axis=0))
    load_out[req_blocks:, :] = stat_rows(
        jnp.sum(runtimes[...] * extrap, axis=0, keepdims=True),
        jnp.sum((new - old) ** 2, axis=0, keepdims=True),
    )


def norms_kernel(sq_0, sq_1, last_0, last_1, last_2, last_3, scal_0, scal_1, scal_2, norms_out):
    row_ids = lax.broadcasted_iota(jnp.int32, norms_out.shape, 0)
    col_ids = lax.broadcasted_iota(jnp.int32, norms_out.shape, 1)
    last = sum_four((last_0, last_1, last_2, last_3), slice(0, 1))
    out = jnp.zeros(norms_out.shape, F32)
    for k, (sq, scal) in enumerate(((sq_0[0:1, :], scal_0), (sq_1[0:1, :], scal_1), (last, scal_2))):
        move_dual = jnp.sum(sq, axis=1, keepdims=True) + scal[2:3, 0:1]
        move_primal = jnp.sum(scal[3:4, :], axis=1, keepdims=True)
        out = jnp.where(col_ids == k, jnp.where(row_ids == 0, move_primal, move_dual), out)
    norms_out[...] = out


def results_kernel(params, state_own, state_other, norms_own, norms_other, primal, dual_out, limit_out, norms_out, primal_out):
    primal_out[...] = primal[...]
    mine = params[1 + ITERS : 2 + ITERS, :] == 1.0
    req_blocks = dual_out.shape[0]
    dual_out[...] = jnp.where(mine, state_own[:req_blocks, :], state_other[:req_blocks, :])
    limit_out[...] = jnp.where(mine, state_own[req_blocks : req_blocks + 1, :], state_other[req_blocks : req_blocks + 1, :])[:, :1]
    norms_out[...] = jnp.where(mine[:, :ITERS], norms_own[...], norms_other[...])


def call(body, outs, specs, scratch=()):
    return pl.pallas_call(
        body,
        out_shape=outs,
        in_specs=specs,
        out_specs=jax.tree.map(lambda _: VMEM, outs),
        scratch_shapes=list(scratch),
        compiler_params=pltpu.CompilerParams(vmem_limit_bytes=(50 if HBM in specs else 16) * 1024 * 1024),
    )


def per_device(
    n_y, n_z,
    coverage_tiles, tile_rows, tile_cols, tile_counts, test_costs, runtimes, time_limit, demand,
    primal_start, dual_start, limit_dual_start, restarts,
):
    slots = coverage_tiles.shape[0]
    test_blocks = test_costs.shape[0] // LANES
    req_blocks = demand.shape[0] // LANES
    inverse_tests = 1.0 / (test_costs.shape[0] * lax.axis_size("tst"))
    costs = test_costs.reshape(test_blocks, LANES)
    runs = runtimes.reshape(test_blocks, LANES)
    want = demand.reshape(req_blocks, LANES)
    primal = primal_start.reshape(test_blocks, LANES)
    dual = dual_start.reshape(req_blocks, LANES)

    far_core = lax.axis_index("tst") % 2 == 1

    n_req = lax.axis_size("req")

    def on_mesh(x, move):
        pairs = []
        for y in range(n_y):
            for z in range(n_z):
                for c in range(2):
                    for r in range(n_req):
                        to_y, to_z, to_c, to_r = move(y, z, c, r)
                        source = ((y * n_z + z) * 2 + c) * n_req + r
                        pairs.append((source, ((to_y * n_z + to_z) * 2 + to_c) * n_req + to_r))
        return lax.ppermute(x, ("tst", "req"), pairs)

    def swap_core(x):
        return on_mesh(x, lambda y, z, c, r: (y, z, 1 - c, r))

    def chips(x, y_bits, z_bits):
        return on_mesh(x, lambda y, z, c, r: (y ^ y_bits, z ^ z_bits, c, r) if c == 1 else (y, z, c, r ^ 1))

    def on_req(x):
        return [lax.ppermute(x, "req", [(i, i ^ bit) for i in range(n_req)]) for bit in (1, 3, 2)]

    def total_tst(x):
        with jax.named_scope("sum_core"):
            x = x + swap_core(x)
        with jax.named_scope("sum_z_outer"):
            x = x + chips(x, 0, n_z - 2)
        with jax.named_scope("sum_z_inner"):
            a, b, c = [chips(x, 0, bits) for bits in (1, 3, 2)]
            x = (x + a) + (b + c)
        with jax.named_scope("sum_y"):
            a, b, c = [chips(x, bits, 0) for bits in (1, 3, 2)]
            x = (x + a) + (b + c)
        return x

    def hand_on(x):
        with jax.named_scope("back_core"):
            return jnp.where(far_core, x, swap_core(x))

    wide = lambda x: jnp.broadcast_to(x.astype(F32).reshape(-1, 1), (x.shape[0], LANES))
    params = jnp.concatenate(
        [wide(time_limit), wide(restarts), wide(far_core.reshape(1)), jnp.zeros((STAT_ROWS - 2 - ITERS, LANES), F32)], axis=0
    )
    scal = jnp.concatenate([wide(limit_dual_start), jnp.zeros((STAT_ROWS - 1, LANES), F32)], axis=0)
    big_t = struct(test_blocks, LANES)
    big_r = struct(req_blocks, LANES)
    small = struct(STAT_ROWS, LANES)
    pull_shape = struct(test_blocks + STAT_ROWS, LANES)
    load_shape = struct(req_blocks + STAT_ROWS, LANES)
    group_shape = struct(GROUP, LANES, LANES, dtype=BF16)
    rest = slots // GROUP - KEPT
    sq_list, scal_list = [], []
    sum_primal = sum_dual = ()
    for iteration in range(ITERS):
        if iteration == 0:
            given = (
                coverage_tiles, dual, tile_rows.reshape(1, slots), tile_cols.reshape(1, slots), tile_counts.reshape(1, 1)
            )
            pull, pick_rows, place_cols, *tiles = call(
                first_pull_kernel,
                (
                    big_t, struct(slots, req_blocks, dtype=BF16), struct(test_blocks, slots),
                    *[group_shape] * KEPT,
                ),
                [HBM] * len(given),
                [pltpu.VMEM((rest, *group_shape.shape), BF16), *[pltpu.VMEM(x.shape, x.dtype) for x in given[1:]]]
                + [pltpu.SemaphoreType.DMA((n,)) for n in (len(given) - 1, slots // GROUP * PIECES)],
            )(*[pltpu.with_memory_space_constraint(x, pltpu.HBM) for x in given[:4]], given[4])
            place_rows, pick_cols, *more = call(
                rest_kernel,
                [struct(req_blocks, slots), struct(slots, slots, dtype=BF16)] + [group_shape] * rest,
                [HBM, VMEM, VMEM],
                [pltpu.SemaphoreType.DMA((rest,))],
            )(coverage_tiles, pick_rows, place_cols)
            tiles += more
        else:
            given = (summed, params, pick_rows, place_cols, dual, scal, want, *tiles, *sum_dual)
            pull, dual, total, scal = call(
                functools.partial(dual_pull_kernel, iteration - 1, inverse_tests),
                (pull_shape, big_r, big_r, small), [VMEM] * len(given),
            )(*given)
            sum_dual = (total,)
            scal_list.append(scal)
        with jax.named_scope("sum_req"):
            parts = [pull, *on_req(pull)]
        given = (*parts, params, pick_cols, place_rows, primal, scal, costs, runs, *tiles, *sum_primal)
        outs = (load_shape, big_t) + (big_t,) * (iteration < ITERS - 1) + (small,) * (iteration > 0)
        load, primal, *more = call(functools.partial(primal_load_kernel, iteration), outs, [VMEM] * len(given))(*given)
        if iteration < ITERS - 1:
            sum_primal = (more.pop(0),)
        if iteration > 0:
            sq_list.append(more.pop(0))
        summed = total_tst(load)
        if iteration < ITERS - 1:
            summed = hand_on(summed)
    dual, scal, sq = call(
        functools.partial(dual_last_kernel, ITERS - 1, inverse_tests), (big_r, small, small), [VMEM] * 6
    )(summed, params, dual, scal, want, *sum_dual)
    scal_list.append(scal)
    with jax.named_scope("sum_req_last"):
        moves = [lambda y, z, c, r, bit=bit: (y, z, c, r ^ bit) if c == 1 else (y ^ 1, z, c, r) for bit in (1, 3, 2)]
        last = [sq, *[on_mesh(sq, move) for move in moves]]
    norms = call(norms_kernel, struct(2, ITERS), [VMEM] * 9)(*sq_list, *last, *scal_list)
    state = jnp.concatenate([dual, scal], axis=0)
    with jax.named_scope("back_core"):
        other = swap_core(state), swap_core(norms)
    dual, limit, norms, primal = call(results_kernel, (big_r, struct(1, 1), struct(2, ITERS), big_t), [VMEM] * 6)(
        params, state, other[0], norms, other[1], primal
    )
    return primal.reshape(-1), dual.reshape(-1), limit.reshape(1), norms.T


def solution(mesh):
    n_y = 4
    n_z = mesh.shape["tst"] // (2 * n_y)
    return jax.shard_map(
        functools.partial(per_device, n_y, n_z),
        mesh=mesh,
        in_specs=(
            P(("tst", "req"), None, None),
            P(("tst", "req")),
            P(("tst", "req")),
            P(("tst", "req")),
            P("tst"),
            P("tst"),
            P(),
            P("req"),
            P("tst"),
            P("req"),
            P(),
            P(),
        ),
        out_specs=(P("tst"), P("req"), P(), P()),
        check_vma=False,
    )
```

```python
import functools

import jax
import jax.numpy as jnp
from jax import lax
from jax.experimental import pallas as pl
from jax.experimental.pallas import tpu as pltpu
from jax.sharding import PartitionSpec as P

ITERS = 3
LANES = 128
STAT_ROWS = 8
GROUP = 16
KEPT = 6

step_primal = 0.6
step_dual = 0.6

VMEM = pl.BlockSpec(memory_space=pltpu.VMEM)
HBM = pl.BlockSpec(memory_space=pltpu.HBM)
F32 = jnp.float32
BF16 = jnp.bfloat16


def struct(*shape, dtype=F32):
    return jax.ShapeDtypeStruct(shape, dtype)


def stat_rows(*given):
    return jnp.concatenate([*given, jnp.zeros((STAT_ROWS - len(given), LANES), F32)], axis=0)


def sum_four(parts, rows):
    a, b, c, d = [part[rows, :] for part in parts]
    return (a + b) + (c + d)


def slot_count(params, iteration):
    seen = jnp.ones((1, LANES), F32)
    for earlier in range(iteration):
        seen = jnp.where(params[1 + earlier : 2 + earlier, :] == 1.0, 1.0, seen + 1.0)
    return seen


def average(params, iteration, total, new):
    restart_now = params[1 + iteration : 2 + iteration, :] == 1.0
    return (
        jnp.where(restart_now, total / slot_count(params, iteration), new),
        jnp.where(restart_now, 0.0, total),
    )


def spread(picked, group):
    rows = picked[group * GROUP : (group + 1) * GROUP, :]
    row_ids = lax.broadcasted_iota(jnp.int32, rows.shape, 0)
    return jnp.concatenate(
        [jnp.where(row_ids == offset, rows, 0.0) for offset in range(GROUP)], axis=1
    ).astype(BF16)


def gather_rows(pick, source):
    return jnp.dot(pick, source.astype(BF16), preferred_element_type=F32)


def scatter_sum(place, contrib):
    return jnp.dot(place, contrib, preferred_element_type=F32, precision=lax.Precision.HIGHEST)


def pull_group(picked, tiles, group):
    block = tiles[group][...].reshape(GROUP * LANES, LANES)
    return jnp.dot(spread(picked, group), block, preferred_element_type=F32)


def load_group(picked, tiles, group):
    block = jnp.concatenate([tiles[group][offset] for offset in range(GROUP)], axis=1)
    return lax.dot_general(
        spread(picked, group), block, (((1,), (1,)), ((), ())), preferred_element_type=F32
    )


def list_of(fetched):
    return [fetched.at[n] for n in range(fetched.shape[0])]


def rest_kernel(tiles_in, pick_rows, place_cols, place_rows, pick_cols, *refs):
    kept, sems = refs[:-1], refs[-1]
    copies = []
    for n, target in enumerate(kept):
        part = tiles_in.at[pl.ds((KEPT + n) * GROUP, GROUP)]
        copies.append(pltpu.make_async_copy(part, target, sems.at[n]))
        copies[-1].start()
    place_rows[...] = pick_rows[...].astype(F32).T
    slots, test_blocks = pick_cols.shape[0], place_cols.shape[0]
    padded = jnp.concatenate([place_cols[...], jnp.zeros((slots - test_blocks, slots), F32)], axis=0)
    pick_cols[...] = padded.T.astype(BF16)
    for copy in copies:
        copy.wait()


def first_pull_kernel(
    tiles_in, dual_in, rows_in, cols_in, live_in, pull_out, pick_rows, place_cols, *refs
):
    slots = tiles_in.shape[0]
    groups = slots // GROUP
    kept, (fetched, dual, rows, cols, live, sems, tile_sems) = refs[:KEPT], refs[KEPT:]
    tiles = [*kept, *list_of(fetched)]
    small = []
    for n, (source, target) in enumerate(((rows_in, rows), (cols_in, cols), (live_in, live), (dual_in, dual))):
        small.append(pltpu.make_async_copy(source, target, sems.at[n]))
        small[-1].start()
    chunks = []
    for n in range(groups):
        chunks.append(pltpu.make_async_copy(tiles_in.at[pl.ds(n * GROUP, GROUP)], tiles[n], tile_sems.at[n]))
        chunks[-1].start()
    for copy in small:
        copy.wait()
    req_blocks = dual.shape[0]
    test_blocks = pull_out.shape[0] - STAT_ROWS
    alive = lax.broadcasted_iota(jnp.int32, (1, slots), 1) < live[...]
    at_row = lax.broadcasted_iota(jnp.int32, (req_blocks, slots), 0) == rows[...]
    at_col = lax.broadcasted_iota(jnp.int32, (test_blocks, slots), 0) == cols[...]
    one_row = jnp.where(at_row, 1.0, 0.0)
    place_cols[...] = jnp.where(at_col & alive, 1.0, 0.0)
    pick = one_row.T.astype(BF16)
    pick_rows[...] = pick
    picked = gather_rows(pick, dual[...])
    contrib = []
    for group in range(groups):
        chunks[group].wait()
        contrib.append(pull_group(picked, tiles, group))
    pull_out[:test_blocks, :] = scatter_sum(place_cols[...], jnp.concatenate(contrib, axis=0))
    pull_out[test_blocks:, :] = jnp.zeros((STAT_ROWS, LANES), F32)


def update_dual(iteration, inverse_tests, summed, params, dual, sum_dual, scal, demand):
    req_blocks = dual.shape[0]
    load = summed[:req_blocks, :]
    stats = summed[req_blocks:, :]
    spent = jnp.sum(stats[0:1, :], axis=1, keepdims=True) * inverse_tests
    bdual = scal[0:1, :]
    bdual_new = jnp.maximum(bdual + step_dual * (spent - params[0:1, :]), 0.0)
    old = dual[...]
    new = jnp.maximum(old + step_dual * (demand[...] - load), 0.0)
    dual_sq = jnp.sum((new - old) ** 2, axis=0, keepdims=True)
    total = new if sum_dual is None else sum_dual[...] + new
    dual_next, total_next = average(params, iteration, total, new)
    bdual_next, bdual_total = average(params, iteration, scal[1:2, :] + bdual_new, bdual_new)
    scal_next = stat_rows(bdual_next, bdual_total, (bdual_new - bdual) ** 2, stats[1:2, :])
    return dual_next, total_next, scal_next, dual_sq


def dual_pull_kernel(iteration, inverse_tests, *refs):
    summed, params, pick_rows, place_cols, dual, scal, demand, *refs = refs
    groups = pick_rows.shape[0] // GROUP
    tiles, refs = refs[:groups], refs[groups:]
    sum_dual = refs.pop(0) if iteration > 0 else None
    pull_out, dual_out, sum_out, scal_out = refs
    dual_next, total_next, scal_next, dual_sq = update_dual(
        iteration, inverse_tests, summed, params, dual, sum_dual, scal, demand
    )
    dual_out[...] = dual_next
    sum_out[...] = total_next
    scal_out[...] = scal_next
    picked = gather_rows(pick_rows[...], dual_next)
    contrib = [pull_group(picked, tiles, group) for group in range(groups)]
    test_blocks = pull_out.shape[0] - STAT_ROWS
    pull_out[:test_blocks, :] = scatter_sum(place_cols[...], jnp.concatenate(contrib, axis=0))
    pull_out[test_blocks:, :] = stat_rows(dual_sq)


def dual_last_kernel(
    iteration, inverse_tests, summed, params, dual, scal, demand, sum_dual, dual_out, scal_out, sq_out
):
    dual_next, _, scal_next, dual_sq = update_dual(
        iteration, inverse_tests, summed, params, dual, sum_dual, scal, demand
    )
    dual_out[...] = dual_next
    scal_out[...] = scal_next
    sq_out[...] = stat_rows(dual_sq)


def primal_load_kernel(iteration, *refs):
    pull_own, pull_1, pull_2, pull_3, params, pick_cols, place_rows, primal, scal, costs, runtimes, *refs = refs
    slots = pick_cols.shape[0]
    groups = slots // GROUP
    tiles, refs = refs[:groups], refs[groups:]
    sum_primal = refs.pop(0) if iteration > 0 else None
    load_out, primal_out, *refs = refs
    sum_out = refs.pop(0) if iteration < ITERS - 1 else None
    sq_out = refs.pop(0) if iteration > 0 else None
    test_blocks = primal.shape[0]
    parts = (pull_own, pull_1, pull_2, pull_3)
    pull = sum_four(parts, slice(0, test_blocks))
    if sq_out is not None:
        sq_out[...] = sum_four(parts, slice(test_blocks, test_blocks + STAT_ROWS))
    old = primal[...]
    new = jnp.clip(old - step_primal * (costs[...] - pull + scal[0:1, :] * runtimes[...]), 0.0, 1.0)
    extrap = (2.0 * new - old).astype(BF16).astype(F32)
    total = new if sum_primal is None else sum_primal[...] + new
    primal_next, total_next = average(params, iteration, total, new)
    primal_out[...] = primal_next
    if sum_out is not None:
        sum_out[...] = total_next
    padded = jnp.concatenate([extrap, jnp.zeros((slots - test_blocks, LANES), F32)], axis=0)
    picked = gather_rows(pick_cols[...], padded)
    contrib = [load_group(picked, tiles, group) for group in range(groups)]
    req_blocks = load_out.shape[0] - STAT_ROWS
    load_out[:req_blocks, :] = scatter_sum(place_rows[...], jnp.concatenate(contrib, axis=0))
    load_out[req_blocks:, :] = stat_rows(
        jnp.sum(runtimes[...] * extrap, axis=0, keepdims=True),
        jnp.sum((new - old) ** 2, axis=0, keepdims=True),
    )


def norms_kernel(sq_0, sq_1, last_0, last_1, last_2, last_3, scal_0, scal_1, scal_2, norms_out):
    row_ids = lax.broadcasted_iota(jnp.int32, norms_out.shape, 0)
    col_ids = lax.broadcasted_iota(jnp.int32, norms_out.shape, 1)
    last = sum_four((last_0, last_1, last_2, last_3), slice(0, 1))
    out = jnp.zeros(norms_out.shape, F32)
    for k, (sq, scal) in enumerate(((sq_0[0:1, :], scal_0), (sq_1[0:1, :], scal_1), (last, scal_2))):
        move_dual = jnp.sum(sq, axis=1, keepdims=True) + scal[2:3, 0:1]
        move_primal = jnp.sum(scal[3:4, :], axis=1, keepdims=True)
        out = jnp.where(col_ids == k, jnp.where(row_ids == 0, move_primal, move_dual), out)
    norms_out[...] = out


def results_kernel(params, state_own, state_other, norms_own, norms_other, primal, dual_out, limit_out, norms_out, primal_out):
    primal_out[...] = primal[...]
    mine = params[1 + ITERS : 2 + ITERS, :] == 1.0
    req_blocks = dual_out.shape[0]
    dual_out[...] = jnp.where(mine, state_own[:req_blocks, :], state_other[:req_blocks, :])
    limit_out[...] = jnp.where(mine, state_own[req_blocks : req_blocks + 1, :], state_other[req_blocks : req_blocks + 1, :])[:, :1]
    norms_out[...] = jnp.where(mine[:, :ITERS], norms_own[...], norms_other[...])


def call(body, outs, specs, scratch=()):
    return pl.pallas_call(
        body,
        out_shape=outs,
        in_specs=specs,
        out_specs=jax.tree.map(lambda _: VMEM, outs),
        scratch_shapes=list(scratch),
        compiler_params=pltpu.CompilerParams(vmem_limit_bytes=(50 if HBM in specs else 16) * 1024 * 1024),
    )


def per_device(
    n_y, n_z,
    coverage_tiles, tile_rows, tile_cols, tile_counts, test_costs, runtimes, time_limit, demand,
    primal_start, dual_start, limit_dual_start, restarts,
):
    slots = coverage_tiles.shape[0]
    test_blocks = test_costs.shape[0] // LANES
    req_blocks = demand.shape[0] // LANES
    inverse_tests = 1.0 / (test_costs.shape[0] * lax.axis_size("tst"))
    costs = test_costs.reshape(test_blocks, LANES)
    runs = runtimes.reshape(test_blocks, LANES)
    want = demand.reshape(req_blocks, LANES)
    primal = primal_start.reshape(test_blocks, LANES)
    dual = dual_start.reshape(req_blocks, LANES)

    far_core = lax.axis_index("tst") % 2 == 1

    n_req = lax.axis_size("req")

    def on_mesh(x, move):
        pairs = []
        for y in range(n_y):
            for z in range(n_z):
                for c in range(2):
                    for r in range(n_req):
                        to_y, to_z, to_c, to_r = move(y, z, c, r)
                        source = ((y * n_z + z) * 2 + c) * n_req + r
                        pairs.append((source, ((to_y * n_z + to_z) * 2 + to_c) * n_req + to_r))
        return lax.ppermute(x, ("tst", "req"), pairs)

    def swap_core(x):
        return on_mesh(x, lambda y, z, c, r: (y, z, 1 - c, r))

    def chips(x, y_bits, z_bits):
        return on_mesh(x, lambda y, z, c, r: (y ^ y_bits, z ^ z_bits, c, r) if c == 1 else (y ^ (z_bits > 0), z ^ (y_bits > 0), c, r))

    def on_req(x):
        return [lax.ppermute(x, "req", [(i, i ^ bit) for i in range(n_req)]) for bit in (1, 3, 2)]

    def total_tst(x):
        with jax.named_scope("sum_core"):
            x = x + swap_core(x)
        with jax.named_scope("sum_z_outer"):
            x = x + chips(x, 0, n_z - 2)
        with jax.named_scope("sum_z_inner"):
            a, b, c = [chips(x, 0, bits) for bits in (1, 3, 2)]
            x = (x + a) + (b + c)
        with jax.named_scope("sum_y"):
            a, b, c = [chips(x, bits, 0) for bits in (1, 3, 2)]
            x = (x + a) + (b + c)
        return x

    def hand_on(x):
        with jax.named_scope("back_core"):
            return jnp.where(far_core, x, swap_core(x))

    wide = lambda x: jnp.broadcast_to(x.astype(F32).reshape(-1, 1), (x.shape[0], LANES))
    params = jnp.concatenate(
        [wide(time_limit), wide(restarts), wide(far_core.reshape(1)), jnp.zeros((STAT_ROWS - 2 - ITERS, LANES), F32)], axis=0
    )
    scal = jnp.concatenate([wide(limit_dual_start), jnp.zeros((STAT_ROWS - 1, LANES), F32)], axis=0)
    big_t = struct(test_blocks, LANES)
    big_r = struct(req_blocks, LANES)
    small = struct(STAT_ROWS, LANES)
    pull_shape = struct(test_blocks + STAT_ROWS, LANES)
    load_shape = struct(req_blocks + STAT_ROWS, LANES)
    group_shape = struct(GROUP, LANES, LANES, dtype=BF16)
    rest = slots // GROUP - KEPT
    sq_list, scal_list = [], []
    sum_primal = sum_dual = ()
    for iteration in range(ITERS):
        if iteration == 0:
            given = (
                coverage_tiles, dual, tile_rows.reshape(1, slots), tile_cols.reshape(1, slots), tile_counts.reshape(1, 1)
            )
            pull, pick_rows, place_cols, *tiles = call(
                first_pull_kernel,
                (
                    pull_shape, struct(slots, req_blocks, dtype=BF16), struct(test_blocks, slots),
                    *[group_shape] * KEPT,
                ),
                [HBM] * len(given),
                [pltpu.VMEM((rest, *group_shape.shape), BF16), *[pltpu.VMEM(x.shape, x.dtype) for x in given[1:]]]
                + [pltpu.SemaphoreType.DMA((n,)) for n in (len(given) - 1, slots // GROUP)],
            )(*[pltpu.with_memory_space_constraint(x, pltpu.HBM) for x in given[:4]], given[4])
            place_rows, pick_cols, *more = call(
                rest_kernel,
                [struct(req_blocks, slots), struct(slots, slots, dtype=BF16)] + [group_shape] * rest,
                [HBM, VMEM, VMEM],
                [pltpu.SemaphoreType.DMA((rest,))],
            )(coverage_tiles, pick_rows, place_cols)
            tiles += more
        else:
            given = (summed, params, pick_rows, place_cols, dual, scal, want, *tiles, *sum_dual)
            pull, dual, total, scal = call(
                functools.partial(dual_pull_kernel, iteration - 1, inverse_tests),
                (pull_shape, big_r, big_r, small), [VMEM] * len(given),
            )(*given)
            sum_dual = (total,)
            scal_list.append(scal)
        with jax.named_scope("sum_req"):
            parts = [pull, *on_req(pull)]
        given = (*parts, params, pick_cols, place_rows, primal, scal, costs, runs, *tiles, *sum_primal)
        outs = (load_shape, big_t) + (big_t,) * (iteration < ITERS - 1) + (small,) * (iteration > 0)
        load, primal, *more = call(functools.partial(primal_load_kernel, iteration), outs, [VMEM] * len(given))(*given)
        if iteration < ITERS - 1:
            sum_primal = (more.pop(0),)
        if iteration > 0:
            sq_list.append(more.pop(0))
        summed = total_tst(load)
        if iteration < ITERS - 1:
            summed = hand_on(summed)
    dual, scal, sq = call(
        functools.partial(dual_last_kernel, ITERS - 1, inverse_tests), (big_r, small, small), [VMEM] * 6
    )(summed, params, dual, scal, want, *sum_dual)
    scal_list.append(scal)
    with jax.named_scope("sum_req_last"):
        moves = [lambda y, z, c, r, bit=bit: (y, z, c, r ^ bit) if c == 1 else (y ^ 1, z, c, r) for bit in (1, 3, 2)]
        last = [sq, *[on_mesh(sq, move) for move in moves]]
    norms = call(norms_kernel, struct(2, ITERS), [VMEM] * 9)(*sq_list, *last, *scal_list)
    state = jnp.concatenate([dual, scal], axis=0)
    with jax.named_scope("back_core"):
        other = swap_core(state), swap_core(norms)
    dual, limit, norms, primal = call(results_kernel, (big_r, struct(1, 1), struct(2, ITERS), big_t), [VMEM] * 6)(
        params, state, other[0], norms, other[1], primal
    )
    return primal.reshape(-1), dual.reshape(-1), limit.reshape(1), norms.T


def solution(mesh):
    n_y = 4
    n_z = mesh.shape["tst"] // (2 * n_y)
    return jax.shard_map(
        functools.partial(per_device, n_y, n_z),
        mesh=mesh,
        in_specs=(
            P(("tst", "req"), None, None),
            P(("tst", "req")),
            P(("tst", "req")),
            P(("tst", "req")),
            P("tst"),
            P("tst"),
            P(),
            P("req"),
            P("tst"),
            P("req"),
            P(),
            P(),
        ),
        out_specs=(P("tst"), P("req"), P(), P()),
        check_vma=False,
    )
```
